128 devices in a mesh: dp: 16 (over z, y), tensor: 8 (over x, core).
Axes of the slice: x: 4, y: 4, z: 4, core: 2. Of those that a mesh axis runs over, the one named last changes fastest.
Arguments:
- tokens: bfloat16 [8192, 2560], P('dp'), may hold values from -6 to 6
- cotangent: bfloat16 [8192, 2560], P('dp'), may hold values from -6 to 6
- segments: int32 [8192], replicated, may hold values from 0 to 2, as said below
- gains: float32 [2, 2560], replicated, may hold values from 0.5 to 1.5
- channel_params: float32 [5, 2560], P(None, 'tensor'), as said below
- branch_in: bfloat16 [2, 2560, 2560], P(None, None, 'tensor'), may hold values from -0.125 to 0.125
- gate_blocks: bfloat16 [2, 256, 2560], P(None, None, 'tensor'), may hold values from -0.375 to 0.375
- out_proj: bfloat16 [2560, 2560], P('tensor'), may hold values from -0.3125 to 0.3125
- ffn_in: bfloat16 [2, 2560, 7680], P(None, None, 'tensor'), may hold values from -0.125 to 0.125
- ffn_down: bfloat16 [7680, 2560], P('tensor'), may hold values from -0.09375 to 0.09375
- gains_first: float32 [2, 2560], replicated, may hold values from -64 to 64
- gains_second: float32 [2, 2560], replicated, may hold values from 434.176 to 1720.32
- channel_first: float32 [5, 2560], P(None, 'tensor'), may hold values from -32 to 32
- channel_second: float32 [5, 2560], P(None, 'tensor'), may hold values from 106.496 to 434.176
- branch_first: float32 [2, 2560, 2560], P(None, 'dp', 'tensor'), may hold values from -64 to 64
- branch_second: float32 [2, 2560, 2560], P(None, 'dp', 'tensor'), may hold values from 434.176 to 1720.32
- gate_first: float32 [2, 256, 2560], P(None, 'dp', 'tensor'), may hold values from -12 to 12
- gate_second: float32 [2, 256, 2560], P(None, 'dp', 'tensor'), may hold values from 17.2032 to 68.8128
- out_first: float32 [2560, 2560], P('tensor', 'dp'), may hold values from -24 to 24
- out_second: float32 [2560, 2560], P('tensor', 'dp'), may hold values from 69.632 to 278.528
- ffn_in_first: float32 [2, 2560, 7680], P(None, 'dp', 'tensor'), may hold values from -32 to 32
- ffn_in_second: float32 [2, 2560, 7680], P(None, 'dp', 'tensor'), may hold values from 106.496 to 434.176
- down_first: float32 [7680, 2560], P('tensor', 'dp'), may hold values from -40 to 40
- down_second: float32 [7680, 2560], P('tensor', 'dp'), may hold values from 180.224 to 729.088
Outputs:
- block_out: bfloat16 [8192, 2560], P(('dp', 'tensor'))
- tokens_grad: bfloat16 [8192, 2560], P(('dp', 'tensor'))
- gains_first_new: float32 [2, 2560], replicated
- gains_second_new: float32 [2, 2560], replicated
- gains_new: float32 [2, 2560], replicated
- channel_first_new: float32 [5, 2560], P(None, 'tensor')
- channel_second_new: float32 [5, 2560], P(None, 'tensor')
- channel_new: float32 [5, 2560], P(None, 'tensor')
- branch_first_new: float32 [2, 2560, 2560], P(None, 'dp', 'tensor')
- branch_second_new: float32 [2, 2560, 2560], P(None, 'dp', 'tensor')
- branch_new: float32 [2, 2560, 2560], P(None, 'dp', 'tensor')
- gate_first_new: float32 [2, 256, 2560], P(None, 'dp', 'tensor')
- gate_second_new: float32 [2, 256, 2560], P(None, 'dp', 'tensor')
- gate_new: float32 [2, 256, 2560], P(None, 'dp', 'tensor')
- out_first_new: float32 [2560, 2560], P('tensor', 'dp')
- out_second_new: float32 [2560, 2560], P('tensor', 'dp')
- out_new: float32 [2560, 2560], P('tensor', 'dp')
- ffn_in_first_new: float32 [2, 2560, 7680], P(None, 'dp', 'tensor')
- ffn_in_second_new: float32 [2, 2560, 7680], P(None, 'dp', 'tensor')
- ffn_in_new: float32 [2, 2560, 7680], P(None, 'dp', 'tensor')
- down_first_new: float32 [7680, 2560], P('tensor', 'dp')
- down_second_new: float32 [7680, 2560], P('tensor', 'dp')
- down_new: float32 [7680, 2560], P('tensor', 'dp')
The draws below stay inside these ranges and needn't reach their ends.
Inputs may be any that keep to these rules, and one draw needn't show every extreme that they name: `segments`: document numbers never fall along the sequence, start at 0 and end at 2. The first document ends within the first 512 tokens, the last begins within the last 512 tokens, and the middle one covers everything between. `channel_params`: rows 0 to 3 are convolution taps, row 4 is a negative decay parameter.
All inputs are finite; a program needn't handle non-finite values.
Results may differ from the reference program's by a relative error of at most 0.019.
Values may be sent and summed in bfloat16 or wider, within the bound.
A program may use at most 384 MiB of HBM per device.

```python
import math
import jax
import jax.numpy as jnp
from jax import lax

D = 2560
L = 2560
HEADS = 10
BLOCK = 256
F = 7680
TOK_DEV = 512
STEP = 10
TOKENS = 8192
N_DP = 16


def draw_segments(key, part):
    key = jax.random.fold_in(key, 5)
    first_key, last_key = jax.random.split(key)
    first = jax.random.randint(first_key, (), 1, TOK_DEV)
    last = TOKENS - jax.random.randint(last_key, (), 1, TOK_DEV)
    position = jnp.arange(TOKENS)
    return (position >= first).astype(jnp.int32) + (position >= last).astype(jnp.int32)


def draw_channel_params(key, part):
    key = jax.random.fold_in(key, 11)
    tap_key, pick_key, level_key = jax.random.split(key, 3)
    taps = 0.5 * jnp.clip(jax.random.normal(tap_key, (4, L), jnp.float32), -3.0, 3.0)
    slow_share = 0.5
    slow = jax.random.uniform(pick_key, (L,), jnp.float32) < slow_share
    level = jax.random.uniform(level_key, (L,), jnp.float32)
    slow_rate = jnp.exp(jnp.log(0.1 / TOKENS) + level * jnp.log(5.0))
    fast_rate = jnp.exp(jnp.log(0.5 / TOKENS) + level * (jnp.log(0.03) - jnp.log(0.5 / TOKENS)))
    rate = jnp.where(slow, slow_rate, fast_rate)
    decay_param = jnp.log(jnp.expm1(rate))
    return jnp.concatenate([taps, decay_param[None]], 0)


def shard_levels(own_key, shape, cuts, low, top_value):
    level, own = 1.0, jax.random.fold_in(own_key, 6)
    for axis_at, shards_of in cuts:
        heights = jnp.exp(jax.random.uniform(jax.random.fold_in(own, axis_at), (shards_of,), jnp.float32, low / len(cuts), top_value / len(cuts)))
        level = level * jnp.repeat(heights, shape[axis_at] // shards_of).reshape([-1 if axis == axis_at else 1 for axis in range(len(shape))])
    return level


def centred(key, extent, width, limit, cuts=(), kind=jnp.bfloat16):
    values = width * jax.random.normal(key, extent, jnp.float32)
    if cuts:
        values = values * shard_levels(key, extent, cuts, -0.22, 0.18)
    return jnp.clip(values, -limit, limit).astype(kind)


def setup_inputs(seed: int = 0) -> dict:
    seeds = jax.random.split(jax.random.key(seed), 25)
    tokens = centred(seeds[0], (TOKENS, D), 1.0, 6.0, ((0, 16),))
    cotangent = centred(seeds[1], (TOKENS, D), 1.0, 6.0, ((0, 16),))
    segments = draw_segments(jax.random.fold_in(seeds[24], 71), 0)
    gains = jnp.clip(1.0 + 0.1 * jax.random.normal(seeds[3], (2, D), jnp.float32), 0.5, 1.5)
    channel_params = draw_channel_params(jax.random.fold_in(seeds[24], 71), 0)
    branch_in = centred(seeds[5], (2, D, L), D ** -0.5, 0.125, ((2, 8),))
    gate_blocks = centred(seeds[6], (2, BLOCK, L), BLOCK ** -0.5, 0.375, ((2, 8),))
    out_proj = centred(seeds[7], (L, D), (L // 8) ** -0.5, 0.3125, ((0, 8),))
    ffn_in = centred(seeds[8], (2, D, F), D ** -0.5, 0.125, ((2, 8),))
    ffn_down = centred(seeds[9], (F, D), (F // 2) ** -0.5, 0.09375, ((0, 8),))
    gains_first = centred(seeds[10], (2, D), (0.11 * TOKENS ** 0.5), 64.0, (), jnp.float32)
    gains_second = jnp.clip(jnp.exp(jax.random.uniform(seeds[11], (2, D), jnp.float32, math.log(434.176), math.log(1720.32))), 434.176, 1720.32)
    channel_first = centred(seeds[12], (5, L), (0.055 * TOKENS ** 0.5), 32.0, ((1, 8),), jnp.float32)
    channel_second = jnp.clip(jnp.exp(math.log(434.176) - 1.40534252 * jax.random.uniform(seeds[13], (5, L), jnp.float32) ** shard_levels(seeds[13], (5, L), ((1, 8),), -0.2, 0.2)), 106.496, 434.176)
    branch_first = centred(seeds[14], (2, D, L), (0.11 * TOKENS ** 0.5), 64.0, ((1, 16), (2, 8)), jnp.float32)
    branch_second = jnp.clip(jnp.exp(math.log(1720.32) - 1.3768156 * jax.random.uniform(seeds[15], (2, D, L), jnp.float32) ** shard_levels(seeds[15], (2, D, L), ((1, 16), (2, 8)), -0.2, 0.2)), 434.176, 1720.32)
    gate_first = centred(seeds[16], (2, BLOCK, L), (0.022 * TOKENS ** 0.5), 12.0, ((1, 16), (2, 8)), jnp.float32)
    gate_second = jnp.clip(jnp.exp(math.log(68.8128) - 1.3862944 * jax.random.uniform(seeds[17], (2, BLOCK, L), jnp.float32) ** shard_levels(seeds[17], (2, BLOCK, L), ((1, 16), (2, 8)), -0.2, 0.2)), 17.2032, 68.8128)
    out_first = centred(seeds[18], (L, D), (0.044 * TOKENS ** 0.5), 24.0, ((0, 8), (1, 16)), jnp.float32)
    out_second = jnp.clip(jnp.exp(math.log(278.528) - 1.3862944 * jax.random.uniform(seeds[19], (L, D), jnp.float32) ** shard_levels(seeds[19], (L, D), ((0, 8), (1, 16)), -0.2, 0.2)), 69.632, 278.528)
    ffn_in_first = centred(seeds[20], (2, D, F), (0.055 * TOKENS ** 0.5), 32.0, ((1, 16), (2, 8)), jnp.float32)
    ffn_in_second = jnp.clip(jnp.exp(math.log(434.176) - 1.40534252 * jax.random.uniform(seeds[21], (2, D, F), jnp.float32) ** shard_levels(seeds[21], (2, D, F), ((1, 16), (2, 8)), -0.2, 0.2)), 106.496, 434.176)
    down_first = centred(seeds[22], (F, D), (0.072 * TOKENS ** 0.5), 40.0, ((0, 8), (1, 16)), jnp.float32)
    down_second = jnp.clip(jnp.exp(math.log(729.088) - 1.397594 * jax.random.uniform(seeds[23], (F, D), jnp.float32) ** shard_levels(seeds[23], (F, D), ((0, 8), (1, 16)), -0.2, 0.2)), 180.224, 729.088)
    return {"tokens": tokens, "cotangent": cotangent, "segments": segments, "gains": gains, "channel_params": channel_params, "branch_in": branch_in, "gate_blocks": gate_blocks, "out_proj": out_proj, "ffn_in": ffn_in, "ffn_down": ffn_down, "gains_first": gains_first, "gains_second": gains_second, "channel_first": channel_first, "channel_second": channel_second, "branch_first": branch_first, "branch_second": branch_second, "gate_first": gate_first, "gate_second": gate_second, "out_first": out_first, "out_second": out_second, "ffn_in_first": ffn_in_first, "ffn_in_second": ffn_in_second, "down_first": down_first, "down_second": down_second}


@jax.custom_vjp
def low(v):
    return lax.optimization_barrier(v.astype(jnp.bfloat16)).astype(jnp.float32)

@jax.custom_vjp
def low_back(v):
    return v

def low_keep(v):
    return (low(v), None)

def low_pass(kept, grad):
    return (grad,)

def back_keep(v):
    return (v, None)

def back_low(kept, grad):
    return (low(grad),)
low.defvjp(low_keep, low_pass)
low_back.defvjp(back_keep, back_low)
NORM_EPS = 1e-06
ADAM_EPS = 1e-08
BETA_ONE = 0.9
BETA_TWO = 0.95

def rms_norm(values, gain):
    return values * lax.rsqrt(lax.optimization_barrier(jnp.mean(values * values, axis=-1, keepdims=True)) + NORM_EPS) * gain

def gelu_tanh(values):
    return jax.nn.gelu(values, approximate=True)

def matmul(left, right):
    return jnp.dot(left, right, precision=lax.Precision.HIGHEST, preferred_element_type=jnp.float32)

def gate_product(conv_round, weight):
    blocks = conv_round.reshape(TOKENS, HEADS, BLOCK)
    matrices = weight.reshape(BLOCK, HEADS, BLOCK).transpose(1, 0, 2)
    return jnp.einsum('thi,hic->thc', blocks, matrices, precision=lax.Precision.HIGHEST).reshape(TOKENS, L)

def block_scan(start_state, block):

    def one_token(state, pair):
        state = pair[0] * state + pair[1]
        return (state, state)
    return lax.scan(one_token, start_state, block)

def forward(x_float, gains, channel_params, branch_in, gate_blocks, out_proj, ffn_in, ffn_down, segments):
    normed_one = low(rms_norm(x_float, gains[0]))
    branch_x = low(low_back(matmul(normed_one, branch_in[0])))
    branch_y = low_back(matmul(normed_one, branch_in[1]))
    conv = channel_params[0] * branch_x
    for offset in range(1, 4):
        shifted = jnp.concatenate([jnp.zeros((offset, L), jnp.float32), branch_x[:-offset]], 0)
        same = jnp.concatenate([segments[:offset] != segments[:offset], segments[offset:] == segments[:-offset]])
        conv = conv + channel_params[offset] * jnp.where(same[:, None], shifted, 0.0)
    conv_round = low(conv)
    pre_a = low_back(gate_product(conv_round, gate_blocks[0]))
    pre_x = low_back(gate_product(conv_round, gate_blocks[1]))
    reset = jnp.concatenate([segments[:1] == segments[:1], segments[1:] != segments[:-1]])[:, None]
    log_a = -8.0 * jax.nn.sigmoid(pre_a) * jax.nn.softplus(channel_params[4])
    carry = jnp.where(reset, 0.0, jnp.exp(log_a))
    scale = jnp.where(reset, 1.0, jnp.sqrt(-jnp.expm1(2.0 * log_a)))
    update = conv_round * jax.nn.sigmoid(pre_x) * scale
    carry_blocks = carry.reshape(N_DP, TOK_DEV, L)
    update_blocks = update.reshape(N_DP, TOK_DEV, L)
    _, states = lax.scan(jax.checkpoint(block_scan), jnp.zeros((L,), jnp.float32), (carry_blocks, update_blocks))
    states = states.reshape(TOKENS, L)
    mixed = low(states * gelu_tanh(branch_y))
    residual = x_float + low_back(matmul(mixed, out_proj))
    normed_two = low(rms_norm(residual, gains[1]))
    gate_pre = low_back(matmul(normed_two, ffn_in[0]))
    up_pre = low_back(matmul(normed_two, ffn_in[1]))
    hidden = low(gelu_tanh(gate_pre) * up_pre)
    return residual + matmul(hidden, ffn_down)

def adam_step(weight, grad, first, second, rate, decay):
    first_new = BETA_ONE * first + (1.0 - BETA_ONE) * grad
    second_new = BETA_TWO * second + (1.0 - BETA_TWO) * grad * grad
    first_hat = first_new / (1.0 - BETA_ONE ** STEP)
    second_hat = second_new / (1.0 - BETA_TWO ** STEP)
    weight_new = weight - rate * (first_hat / (jnp.sqrt(second_hat) + ADAM_EPS) + decay * weight)
    return (first_new, second_new, weight_new)

def reference(tokens, cotangent, segments, gains, channel_params, branch_in, gate_blocks, out_proj, ffn_in, ffn_down, gains_first, gains_second, channel_first, channel_second, branch_first, branch_second, gate_first, gate_second, out_first, out_second, ffn_in_first, ffn_in_second, down_first, down_second):
    params = (gains, channel_params, branch_in.astype(jnp.float32), gate_blocks.astype(jnp.float32), out_proj.astype(jnp.float32), ffn_in.astype(jnp.float32), ffn_down.astype(jnp.float32))
    x_float = tokens.astype(jnp.float32)

    def whole_block(x_in, gain_in, chan_in, branch_w, gate_w, out_w, ffn_w, down_w):
        return forward(x_in, gain_in, chan_in, branch_w, gate_w, out_w, ffn_w, down_w, segments)
    block_value, pullback = jax.vjp(whole_block, x_float, *params)
    grads = pullback(cotangent.astype(jnp.float32))
    channel_rate = jnp.array([1.0, 1.0, 1.0, 1.0, 3.0], jnp.float32)[:, None]
    gains_out = adam_step(params[0], grads[1], gains_first, gains_second, 1.0, 0.0)
    channel_out = adam_step(params[1], grads[2], channel_first, channel_second, channel_rate, 0.0)
    branch_out = adam_step(params[2], grads[3], branch_first, branch_second, 3.0 * D ** (-0.5), 0.1)
    gate_out = adam_step(params[3], grads[4], gate_first, gate_second, 3.0 * BLOCK ** (-0.5), 0.1)
    proj_out = adam_step(params[4], grads[5], out_first, out_second, 3.0 * (L // 8) ** (-0.5), 0.1)
    ffn_out = adam_step(params[5], grads[6], ffn_in_first, ffn_in_second, 3.0 * D ** (-0.5), 0.1)
    down_out = adam_step(params[6], grads[7], down_first, down_second, 3.0 * (F // 2) ** (-0.5), 0.1)
    return (block_value.astype(jnp.bfloat16), grads[0].astype(jnp.bfloat16), gains_out[0], gains_out[1], gains_out[2], channel_out[0], channel_out[1], channel_out[2], branch_out[0], branch_out[1], branch_out[2], gate_out[0], gate_out[1], gate_out[2], proj_out[0], proj_out[1], proj_out[2], ffn_out[0], ffn_out[1], ffn_out[2], down_out[0], down_out[1], down_out[2])
```

```python
import functools

import jax
import jax.numpy as jnp
from jax import lax
from jax.experimental import pallas as pl
from jax.experimental.pallas import tpu as pltpu
from jax.sharding import PartitionSpec as P

D = 2560
L = 2560
BLOCK = 256
F = 7680
STEP = 10
N_DP = 16
N_T = 8
ROWS = 512
OWN = ROWS // N_T
WIDTH = L // N_T
CHUNKS = 8
SPAN = ROWS // CHUNKS
GROUPS = 3
MESH = pl.DeviceIdType.MESH

NORM_EPS = 1e-06
ADAM_EPS = 1e-08
BETA_ONE = 0.9
BETA_TWO = 0.95


def params(cid):
    return pltpu.CompilerParams(
        collective_id=cid, has_side_effects=True, vmem_limit_bytes=56 * 2**20
    )


def vmem(count):
    return [pl.BlockSpec(memory_space=pltpu.VMEM)] * count


def greet(peers):
    barrier = pltpu.get_barrier_semaphore()
    for peer in peers:
        pl.semaphore_signal(barrier, inc=1, device_id=peer, device_id_type=MESH)
    pl.semaphore_wait(barrier, len(peers))


def remote(source, target, send_sem, recv_sem, peer):
    return pltpu.make_async_remote_copy(
        src_ref=source,
        dst_ref=target,
        send_sem=send_sem,
        recv_sem=recv_sem,
        device_id=peer,
        device_id_type=MESH,
    )


def place():
    index = lax.axis_index("tensor")
    return index // 2, lax.rem(index, 2)


def at_x(x, core, by):
    return {"tensor": lax.rem(x + by, 4) * 2 + core}


def tensor_peers():
    x, core = place()
    return [{"tensor": x * 2 + 1 - core}] + [at_x(x, core, by) for by in (1, 2, 3)]


def reduce_rows(partial, pair, held, landed, pair_send, pair_recv, x_send, x_recv):
    x, core = place()
    other = {"tensor": x * 2 + 1 - core}

    def row(by, which):
        return pl.multiple_of((lax.rem(x + by, 4) * 2 + which) * OWN, OWN)

    pair_copies, x_copies = {}, {}
    for by in (2, 1, 3, 0):
        copy = remote(
            partial.at[pl.ds(row(by, 1 - core), OWN)],
            pair.at[by],
            pair_send.at[by],
            pair_recv.at[by],
            other,
        )
        copy.start()
        pair_copies[by] = copy
    for by in (2, 1, 3):
        pair_copies[by].wait_recv()
        mine = partial[pl.ds(row(by, core), OWN), :].astype(jnp.float32)
        held[by - 1] = (mine + pair[by].astype(jnp.float32)).astype(jnp.bfloat16)
        copy = remote(
            held.at[by - 1],
            landed.at[by - 1],
            x_send.at[by - 1],
            x_recv.at[by - 1],
            at_x(x, core, by),
        )
        copy.start()
        x_copies[by] = copy
    pair_copies[0].wait_recv()
    total = partial[pl.ds(row(0, core), OWN), :].astype(jnp.float32) + pair[0].astype(jnp.float32)
    for by in (1, 3, 2):
        x_copies[by].wait_recv()
        total = total + landed[by - 1].astype(jnp.float32)
    for by in (2, 1, 3, 0):
        pair_copies[by].wait_send()
    for by in (2, 1, 3):
        x_copies[by].wait_send()
    return total


def reduce_scratch():
    return [
        pltpu.VMEM((4, OWN, D), jnp.bfloat16),
        pltpu.VMEM((3, OWN, D), jnp.bfloat16),
        pltpu.VMEM((3, OWN, D), jnp.bfloat16),
        pltpu.SemaphoreType.DMA((4,)),
        pltpu.SemaphoreType.DMA((4,)),
        pltpu.SemaphoreType.DMA((3,)),
        pltpu.SemaphoreType.DMA((3,)),
    ]


def gather_rows(block, whole, x_send, x_recv, pair_send, pair_recv):
    x, core = place()
    other = {"tensor": x * 2 + 1 - core}

    def row(by, which):
        return pl.multiple_of((lax.rem(x + by, 4) * 2 + which) * OWN, OWN)

    whole[pl.ds(row(0, core), OWN), :] = block
    mine = whole.at[pl.ds(row(0, core), OWN)]
    sends = []
    for by in (2, 1, 3):
        copy = remote(mine, mine, x_send.at[by - 1], x_recv.at[by - 1], at_x(x, core, by))
        copy.start()
        sends.append(copy)
    first = remote(mine, mine, pair_send.at[0], pair_recv.at[0], other)
    first.start()
    pairs = [first]
    for by in (1, 3, 2):
        sender = lax.rem(4 - by, 4)
        block_ref = whole.at[pl.ds(row(sender, core), OWN)]
        arrived = remote(block_ref, block_ref, x_send.at[by - 1], x_recv.at[by - 1], other)
        arrived.wait_recv()
        copy = remote(block_ref, block_ref, pair_send.at[by], pair_recv.at[by], other)
        copy.start()
        pairs.append(copy)
    for copy in sends:
        copy.wait_send()
    for copy in pairs:
        copy.wait()


def gather_scratch():
    return [
        pltpu.SemaphoreType.DMA((3,)),
        pltpu.SemaphoreType.DMA((3,)),
        pltpu.SemaphoreType.DMA((4,)),
        pltpu.SemaphoreType.DMA((4,)),
    ]


def dp_peers():
    me = lax.axis_index("dp")
    return [{"dp": lax.rem(me + by, N_DP)} for by in range(1, N_DP)]


def share_dp(slots, send, recv):
    me = lax.axis_index("dp")
    copies = []
    for by in range(1, N_DP):
        copy = remote(
            slots.at[me], slots.at[me], send.at[by], recv.at[by], {"dp": lax.rem(me + by, N_DP)}
        )
        copy.start()
        copies.append(copy)
    for copy in copies:
        copy.wait()


def lanes_in(target, rows, values):
    for group in range(GROUPS):
        part = values[:, group * 128 : min((group + 1) * 128, WIDTH)]
        target[group, rows, 0 : part.shape[1]] = part
        if part.shape[1] < 128:
            target[group, rows, part.shape[1] : 128] = jnp.zeros(
                (values.shape[0], 128 - part.shape[1]), values.dtype
            )


def chunk_scan(carry, update, values, prods, reverse):
    def step(i, held):
        j = SPAN - 1 - i if reverse else i
        at = pl.ds(j, CHUNKS, stride=SPAN)
        factor_at = pl.ds(j + 1, CHUNKS, stride=SPAN) if reverse else at
        after = []
        for group in range(GROUPS):
            prod, value = held[group]
            now = carry[group, factor_at, :]
            value = now * value + update[group, at, :]
            prod = now * prod
            values[group, at, :] = value
            prods[group, at, :] = prod
            after.append((prod, value))
        return tuple(after)

    start = (jnp.ones((CHUNKS, 128), jnp.float32), jnp.zeros((CHUNKS, 128), jnp.float32))
    return lax.fori_loop(0, SPAN, step, (start,) * GROUPS, unroll=4)


def chunk_ends(ends, order):
    found = []
    for prod, value in ends:
        p, v = jnp.ones((1, 128), jnp.float32), jnp.zeros((1, 128), jnp.float32)
        rows = []
        for chunk in order:
            rows.append((p, v))
            here = prod[chunk : chunk + 1], value[chunk : chunk + 1]
            p, v = p * here[0], here[0] * v + here[1]
        found.append((rows, (p, v)))
    return found


def scan_forward_kernel(carry, update, state, incoming, factors, terms, values, prods, slots, send, recv):
    greet(dp_peers())
    me = lax.axis_index("dp")
    lanes_in(factors, pl.ds(0, ROWS), carry[...])
    lanes_in(terms, pl.ds(0, ROWS), update[...])
    ends = chunk_scan(factors, terms, values, prods, False)
    found = chunk_ends(ends, range(CHUNKS))
    for group, (_, (p, v)) in enumerate(found):
        slots[me, 0:1, pl.ds(group * 128, 128)] = p
        slots[me, 1:2, pl.ds(group * 128, 128)] = v
    share_dp(slots, send, recv)
    before = jnp.zeros((1, GROUPS * 128), jnp.float32)
    for index in range(N_DP - 1):
        longer = slots[index, 0:1, :] * before + slots[index, 1:2, :]
        before = jnp.where(index < me, longer, before)
    for group, (starts, _) in enumerate(found):
        width = min(128, WIDTH - group * 128)
        lanes = pl.ds(group * 128, width)
        for chunk in range(CHUNKS):
            rows = pl.ds(chunk * SPAN, SPAN)
            p, v = starts[chunk]
            entry = p * before[:, group * 128 : (group + 1) * 128] + v
            total = values[group, rows, :] + prods[group, rows, :] * entry
            state[rows, lanes] = total[:, :width]
    incoming[...] = before[:, :WIDTH]


def scan_scratch():
    return [
        pltpu.VMEM((GROUPS, ROWS + 8, 128), jnp.float32),
        pltpu.VMEM((GROUPS, ROWS, 128), jnp.float32),
        pltpu.VMEM((GROUPS, ROWS, 128), jnp.float32),
        pltpu.VMEM((GROUPS, ROWS, 128), jnp.float32),
        pltpu.VMEM((N_DP, 8, GROUPS * 128), jnp.float32),
        pltpu.SemaphoreType.DMA((N_DP,)),
        pltpu.SemaphoreType.DMA((N_DP,)),
    ]


def scan_forward(carry, update):
    return pl.pallas_call(
        scan_forward_kernel,
        out_shape=(
            jax.ShapeDtypeStruct((ROWS, WIDTH), jnp.float32),
            jax.ShapeDtypeStruct((1, WIDTH), jnp.float32),
        ),
        in_specs=vmem(2),
        out_specs=tuple(vmem(2)),
        scratch_shapes=scan_scratch(),
        compiler_params=params(1),
    )(carry, update)


def scan_backward_kernel(carry, local, total, factors, terms, values, prods, slots, send, recv):
    greet(dp_peers())
    me = lax.axis_index("dp")
    lanes_in(factors, pl.ds(0, ROWS), carry[...])
    for group in range(GROUPS):
        factors[group, ROWS : ROWS + 8, :] = jnp.ones((8, 128), jnp.float32)
    lanes_in(terms, pl.ds(0, ROWS), local[...])
    ends = chunk_scan(factors, terms, values, prods, True)
    found = chunk_ends(ends, range(CHUNKS - 1, -1, -1))
    for group, (_, (p, v)) in enumerate(found):
        first = factors[group, 0:1, :]
        slots[me, 0:1, pl.ds(group * 128, 128)] = first * p
        slots[me, 1:2, pl.ds(group * 128, 128)] = first * v
    share_dp(slots, send, recv)
    later = jnp.zeros((1, GROUPS * 128), jnp.float32)
    for index in range(N_DP - 1, 0, -1):
        longer = slots[index, 0:1, :] * later + slots[index, 1:2, :]
        later = jnp.where(index > me, longer, later)
    for group, (starts, _) in enumerate(found):
        width = min(128, WIDTH - group * 128)
        lanes = pl.ds(group * 128, width)
        for chunk in range(CHUNKS):
            rows = pl.ds(chunk * SPAN, SPAN)
            p, v = starts[CHUNKS - 1 - chunk]
            entry = p * later[:, group * 128 : (group + 1) * 128] + v
            sums = values[group, rows, :] + prods[group, rows, :] * entry
            total[rows, lanes] = sums[:, :width]


def scan_backward(carry, local):
    return pl.pallas_call(
        scan_backward_kernel,
        out_shape=jax.ShapeDtypeStruct((ROWS, WIDTH), jnp.float32),
        in_specs=vmem(2),
        out_specs=pl.BlockSpec(memory_space=pltpu.VMEM),
        scratch_shapes=scan_scratch(),
        compiler_params=params(2),
    )(carry, local)


def mixer_norm_kernel(partial, own, gain, residual, normed, *scratch):
    greet(tensor_peers())
    total = own[...].astype(jnp.float32) + reduce_rows(partial, *scratch[:7])
    residual[...] = total
    block = rms_norm(total, gain[...]).astype(jnp.bfloat16)
    gather_rows(block, normed, *scratch[7:])


def mixer_norm(partial, own, gain):
    return pl.pallas_call(
        mixer_norm_kernel,
        out_shape=(
            jax.ShapeDtypeStruct((OWN, D), jnp.float32),
            jax.ShapeDtypeStruct((ROWS, D), jnp.bfloat16),
        ),
        in_specs=vmem(3),
        out_specs=tuple(vmem(2)),
        scratch_shapes=reduce_scratch() + gather_scratch(),
        compiler_params=params(3),
    )(partial, own, gain)


def norm_back(value, gain, grad):
    scale = lax.rsqrt(jnp.mean(value * value, axis=-1, keepdims=True) + NORM_EPS)
    unit = value * scale
    scaled = grad * gain
    back = scale * (scaled - unit * jnp.mean(scaled * unit, axis=-1, keepdims=True))
    return back, jnp.sum(grad * unit, axis=0, keepdims=True)


def ffn_norm_kernel(partial, down_partial, residual, gain, dy, out, grad, grad_gain, rounded, *scratch):
    greet(tensor_peers())
    norm_grad = reduce_rows(partial, *scratch[:7])
    back, gain_part = norm_back(residual[...], gain[...], norm_grad)
    back = back + dy[...].astype(jnp.float32)
    grad[...] = back
    grad_gain[...] = gain_part
    gather_rows(back.astype(jnp.bfloat16), rounded, *scratch[7:11])
    out[...] = (residual[...] + reduce_rows(down_partial, *scratch[11:])).astype(jnp.bfloat16)


def ffn_norm(partial, down_partial, residual, gain, dy):
    return pl.pallas_call(
        ffn_norm_kernel,
        out_shape=(
            jax.ShapeDtypeStruct((OWN, D), jnp.bfloat16),
            jax.ShapeDtypeStruct((OWN, D), jnp.float32),
            jax.ShapeDtypeStruct((1, D), jnp.float32),
            jax.ShapeDtypeStruct((ROWS, D), jnp.bfloat16),
        ),
        in_specs=vmem(5),
        out_specs=tuple(vmem(4)),
        scratch_shapes=reduce_scratch() + gather_scratch() + reduce_scratch(),
        compiler_params=params(4),
    )(partial, down_partial, residual, gain, dy)


def last_norm_kernel(
    partial, own, gain, grad, gain_two_part, channel_part, tokens_grad, gain_sum, channel_sum,
    gain_t, gain_dp, chan_dp, t_send, t_recv, g_send, g_recv, c_send, c_recv, *scratch
):
    greet(
        [{"tensor": lax.rem(lax.axis_index("tensor") + by, N_T)} for by in range(1, N_T)] + dp_peers()
    )
    me, index = lax.axis_index("dp"), lax.axis_index("tensor")
    chan_dp[me] = channel_part[...]
    channel_copies = []
    for by in range(1, N_DP):
        copy = remote(
            chan_dp.at[me], chan_dp.at[me], c_send.at[by], c_recv.at[by], {"dp": lax.rem(me + by, N_DP)}
        )
        copy.start()
        channel_copies.append(copy)
    norm_grad = reduce_rows(partial, *scratch)
    back, gain_part = norm_back(own[...].astype(jnp.float32), gain[...], norm_grad)
    tokens_grad[...] = (grad[...] + back).astype(jnp.bfloat16)
    gain_t[index, 0:1, :] = gain_part
    gain_t[index, 1:2, :] = gain_two_part[...]
    copies = []
    for by in range(1, N_T):
        copy = remote(
            gain_t.at[index],
            gain_t.at[index],
            t_send.at[by],
            t_recv.at[by],
            {"tensor": lax.rem(index + by, N_T)},
        )
        copy.start()
        copies.append(copy)
    for copy in copies:
        copy.wait()
    total = gain_t[0]
    for by in range(1, N_T):
        total = total + gain_t[by]
    gain_dp[me] = total
    share_dp(gain_dp, g_send, g_recv)
    for copy in channel_copies:
        copy.wait()
    total, channels = gain_dp[0], chan_dp[0]
    for by in range(1, N_DP):
        total = total + gain_dp[by]
        channels = channels + chan_dp[by]
    gain_sum[...] = total
    channel_sum[...] = channels


def last_norm(partial, own, gain, grad, gain_two_part, channel_part):
    return pl.pallas_call(
        last_norm_kernel,
        out_shape=(
            jax.ShapeDtypeStruct((OWN, D), jnp.bfloat16),
            jax.ShapeDtypeStruct((2, D), jnp.float32),
            jax.ShapeDtypeStruct((5, WIDTH), jnp.float32),
        ),
        in_specs=vmem(6),
        out_specs=tuple(vmem(3)),
        scratch_shapes=[
            pltpu.VMEM((N_T, 2, D), jnp.float32),
            pltpu.VMEM((N_DP, 2, D), jnp.float32),
            pltpu.VMEM((N_DP, 5, WIDTH), jnp.float32),
            pltpu.SemaphoreType.DMA((N_T,)),
            pltpu.SemaphoreType.DMA((N_T,)),
            pltpu.SemaphoreType.DMA((N_DP,)),
            pltpu.SemaphoreType.DMA((N_DP,)),
            pltpu.SemaphoreType.DMA((N_DP,)),
            pltpu.SemaphoreType.DMA((N_DP,)),
        ]
        + reduce_scratch(),
        compiler_params=params(5),
    )(partial, own, gain, grad, gain_two_part, channel_part)


def from_behind(array, axis, by):
    length = lax.axis_size(axis)
    pairs = [(i, i + by) for i in range(length) if 0 <= i + by < length]
    return lax.ppermute(array, axis, pairs)


def rms_norm(values, gain):
    return values * lax.rsqrt(jnp.mean(values * values, axis=-1, keepdims=True) + NORM_EPS) * gain


def gelu_tanh(values):
    return jax.nn.gelu(values, approximate=True)


def matmul(left, right):
    return jnp.dot(left, right, preferred_element_type=jnp.float32)


def times_transposed(left, right):
    return lax.dot_general(
        left, right, (((1,), (1,)), ((), ())), preferred_element_type=jnp.float32
    )


def transposed_times(left, right):
    return lax.dot_general(
        left, right, (((0,), (0,)), ((), ())), preferred_element_type=jnp.float32
    )


def conv_mix(extended, taps, same_doc):
    rows = extended.shape[0] - 3
    total = taps[0] * extended[3:]
    for offset in range(1, 4):
        total = total + taps[offset] * jnp.where(
            same_doc[offset][:, None], extended[3 - offset : 3 - offset + rows], 0.0
        )
    return total


def gate_terms(conv_float, pre_a, pre_x, decay_param, reset):
    log_a = -8.0 * jax.nn.sigmoid(pre_a) * jax.nn.softplus(decay_param)
    carry = jnp.where(reset, 0.0, jnp.exp(log_a))
    scale = jnp.where(reset, 1.0, jnp.sqrt(-jnp.expm1(2.0 * log_a)))
    return (carry, conv_float * jax.nn.sigmoid(pre_x) * scale)


def adam_step(weight, grad, first, second, rate, decay):
    first_new = BETA_ONE * first + (1.0 - BETA_ONE) * grad
    second_new = BETA_TWO * second + (1.0 - BETA_TWO) * grad * grad
    first_hat = first_new / (1.0 - BETA_ONE**STEP)
    second_hat = second_new / (1.0 - BETA_TWO**STEP)
    weight_new = weight - rate * (first_hat / (jnp.sqrt(second_hat) + ADAM_EPS) + decay * weight)
    return (first_new, second_new, weight_new)


def owned_slice(weight, data_index, count):
    share = weight.shape[1] // count
    return lax.dynamic_slice_in_dim(weight, data_index * share, share, 1).astype(jnp.float32)


def share_rows(grad):
    return lax.psum_scatter(
        grad.astype(jnp.bfloat16), "dp", scatter_dimension=0, tiled=True
    ).astype(jnp.float32)


def shards(
    tokens,
    cotangent,
    segments,
    gains,
    channel_params,
    branch_in,
    gate_blocks,
    out_proj,
    ffn_in,
    ffn_down,
    gains_first,
    gains_second,
    channel_first,
    channel_second,
    branch_first,
    branch_second,
    gate_first,
    gate_second,
    out_first,
    out_second,
    ffn_in_first,
    ffn_in_second,
    down_first,
    down_second,
):
    rows, width = ROWS, WIDTH
    data_index = lax.axis_index("dp")
    tensor_index = lax.axis_index("tensor")

    def own_rows(values):
        return lax.dynamic_slice_in_dim(values, tensor_index * OWN, OWN, 0)

    padded_ids = jnp.concatenate([jnp.full((3,), -1, jnp.int32), segments])
    local_ids = lax.dynamic_slice_in_dim(padded_ids, data_index * rows, rows + 3)
    same_doc = jnp.stack(
        [local_ids[3 - offset : 3 - offset + rows] == local_ids[3:] for offset in range(4)]
    )
    reset = (local_ids[3:] != local_ids[2 : 2 + rows])[:, None]
    x_float = tokens.astype(jnp.float32)
    normed_one = rms_norm(x_float, gains[0]).astype(jnp.bfloat16)
    branch_x = matmul(normed_one, branch_in[0]).astype(jnp.bfloat16)
    branch_y = matmul(normed_one, branch_in[1])
    previous = from_behind(branch_x[rows - 3 :], "dp", 1)
    extended = jnp.concatenate([previous, branch_x], 0).astype(jnp.float32)
    taps = channel_params[:4]
    decay_param = channel_params[4]
    conv_round = conv_mix(extended, taps, same_doc).astype(jnp.bfloat16)
    below = from_behind(conv_round[:, width - BLOCK :], "tensor", 1)
    above = from_behind(conv_round[:, :BLOCK], "tensor", -1)
    beside = jnp.concatenate([below, conv_round, above], 1)
    shift = lax.rem(tensor_index * width, BLOCK)
    start = BLOCK - shift
    window = lax.dynamic_slice_in_dim(beside, start, 2 * BLOCK, 1)
    second_block = (shift + jnp.arange(width) >= BLOCK)[None, None, :]
    zero_gate = jnp.zeros_like(gate_blocks)
    gate_wide = jnp.concatenate(
        [jnp.where(second_block, zero_gate, gate_blocks), jnp.where(second_block, gate_blocks, zero_gate)],
        1,
    )
    pre_a = matmul(window, gate_wide[0])
    pre_x = matmul(window, gate_wide[1])
    conv_float = conv_round.astype(jnp.float32)
    carry, update = gate_terms(conv_float, pre_a, pre_x, decay_param, reset)
    state, incoming = scan_forward(carry, update)
    gelu_y = gelu_tanh(branch_y)
    mixed = (state * gelu_y).astype(jnp.bfloat16)
    mixer_partial = matmul(mixed, out_proj).astype(jnp.bfloat16)
    tokens_own, cotangent_own = own_rows(tokens), own_rows(cotangent)
    residual_own, normed_two = mixer_norm(mixer_partial, tokens_own, gains[1:2])
    gate_pre = matmul(normed_two, ffn_in[0])
    up_pre = matmul(normed_two, ffn_in[1])
    hidden = (gelu_tanh(gate_pre) * up_pre).astype(jnp.bfloat16)
    ffn_partial = matmul(hidden, ffn_down).astype(jnp.bfloat16)
    grad_hidden = times_transposed(cotangent, ffn_down)
    down_share = share_rows(transposed_times(cotangent, hidden))
    _, hidden_pull = jax.vjp(
        lambda gate_value, up_value: gelu_tanh(gate_value) * up_value, gate_pre, up_pre
    )
    grad_gate, grad_up = hidden_pull(grad_hidden)
    grad_both = jnp.concatenate([grad_gate.astype(jnp.bfloat16), grad_up.astype(jnp.bfloat16)], 1)
    ffn_in_share = share_rows(transposed_times(normed_two, grad_both))
    normed_two_partial = times_transposed(grad_both[:, : F // N_T], ffn_in[0]) + times_transposed(
        grad_both[:, F // N_T :], ffn_in[1]
    )
    block_out, residual_grad, gain_two_part, residual_round = ffn_norm(
        normed_two_partial.astype(jnp.bfloat16), ffn_partial, residual_own, gains[1:2], cotangent_own
    )
    out_share = share_rows(transposed_times(residual_round, mixed))
    mixed_grad = times_transposed(residual_round, out_proj)
    state_grad_local = mixed_grad * gelu_y
    _, gelu_pull = jax.vjp(gelu_tanh, branch_y)
    (branch_y_grad,) = gelu_pull(mixed_grad * state)
    branch_y_round = branch_y_grad.astype(jnp.bfloat16)
    state_total_grad = scan_backward(carry, state_grad_local)
    previous_state = jnp.concatenate([incoming, state[:-1]], 0)
    carry_grad = state_total_grad * previous_state
    _, term_pull = jax.vjp(
        lambda conv_value, a_value, x_value, decay_value: gate_terms(
            conv_value, a_value, x_value, decay_value, reset
        ),
        conv_float,
        pre_a,
        pre_x,
        decay_param,
    )
    conv_grad_local, pre_a_grad, pre_x_grad, decay_grad = term_pull((carry_grad, state_total_grad))
    pre_a_round = pre_a_grad.astype(jnp.bfloat16)
    pre_x_round = pre_x_grad.astype(jnp.bfloat16)
    window_grad = times_transposed(pre_a_round, gate_wide[0]) + times_transposed(
        pre_x_round, gate_wide[1]
    )
    beside_grad = lax.dynamic_update_slice_in_dim(
        jnp.zeros((rows, width + 2 * BLOCK), jnp.float32), window_grad, start, 1
    )
    gate_both = transposed_times(window, jnp.concatenate([pre_a_round, pre_x_round], 1))
    second_twice = jnp.concatenate([second_block[0], second_block[0]], 1)
    gate_grad = jnp.where(second_twice, gate_both[BLOCK:], gate_both[:BLOCK])
    from_above = from_behind(beside_grad[:, :BLOCK], "tensor", -1)
    from_below = from_behind(beside_grad[:, BLOCK + width :], "tensor", 1)
    zero_gap = jnp.zeros((rows, width - BLOCK), jnp.float32)
    conv_gate_grad = (
        beside_grad[:, BLOCK : BLOCK + width]
        + jnp.concatenate([zero_gap, from_above], 1)
        + jnp.concatenate([from_below, zero_gap], 1)
    )
    conv_grad = conv_grad_local + conv_gate_grad
    _, conv_pull = jax.vjp(
        lambda ext_value, tap_value: conv_mix(ext_value, tap_value, same_doc), extended, taps
    )
    extended_grad, taps_grad = conv_pull(conv_grad)
    from_next = from_behind(extended_grad[:3], "dp", -1)
    branch_x_grad = extended_grad[3:] + jnp.concatenate(
        [jnp.zeros((rows - 3, width), jnp.float32), from_next], 0
    )
    branch_both = jnp.concatenate([branch_x_grad.astype(jnp.bfloat16), branch_y_round], 1)
    branch_share = share_rows(transposed_times(normed_one, branch_both))
    gate_share = lax.psum_scatter(gate_grad, "dp", scatter_dimension=0, tiled=True)
    normed_one_partial = times_transposed(branch_both[:, :width], branch_in[0]) + times_transposed(
        branch_both[:, width:], branch_in[1]
    )
    channel_local = jnp.concatenate([taps_grad, decay_grad[None]], 0)
    tokens_grad, gain_grad, channel_grad = last_norm(
        normed_one_partial.astype(jnp.bfloat16),
        tokens_own,
        gains[0:1],
        residual_grad,
        gain_two_part,
        channel_local,
    )
    channel_rate = jnp.array([1.0, 1.0, 1.0, 1.0, 3.0], jnp.float32)[:, None]
    gains_out = adam_step(gains, gain_grad, gains_first, gains_second, 1.0, 0.0)
    channel_out = adam_step(
        channel_params, channel_grad, channel_first, channel_second, channel_rate, 0.0
    )

    def split_pair(share):
        half = share.shape[1] // 2
        return jnp.stack([share[:, :half], share[:, half:]])

    branch_out = adam_step(
        owned_slice(branch_in, data_index, N_DP),
        split_pair(branch_share),
        branch_first,
        branch_second,
        3.0 * D ** (-0.5),
        0.1,
    )
    gate_out = adam_step(
        owned_slice(gate_blocks, data_index, N_DP),
        split_pair(gate_share),
        gate_first,
        gate_second,
        3.0 * BLOCK ** (-0.5),
        0.1,
    )
    proj_out = adam_step(
        owned_slice(out_proj, data_index, N_DP),
        out_share.T,
        out_first,
        out_second,
        3.0 * (L // 8) ** (-0.5),
        0.1,
    )
    ffn_out = adam_step(
        owned_slice(ffn_in, data_index, N_DP),
        split_pair(ffn_in_share),
        ffn_in_first,
        ffn_in_second,
        3.0 * D ** (-0.5),
        0.1,
    )
    down_out = adam_step(
        owned_slice(ffn_down, data_index, N_DP),
        down_share.T,
        down_first,
        down_second,
        3.0 * (F // 2) ** (-0.5),
        0.1,
    )
    return (
        block_out,
        tokens_grad,
        *gains_out,
        *channel_out,
        *branch_out,
        *gate_out,
        *proj_out,
        *ffn_out,
        *down_out,
    )


def solution(mesh):
    weights = [
        P(None, None, "tensor"),
        P(None, None, "tensor"),
        P("tensor", None),
        P(None, None, "tensor"),
        P("tensor", None),
    ]
    owned = [
        P(None, "dp", "tensor"),
        P(None, "dp", "tensor"),
        P("tensor", "dp"),
        P(None, "dp", "tensor"),
        P("tensor", "dp"),
    ]
    moments = [P(), P(None, "tensor")] + owned
    placed = [P("dp", None), P("dp", None), P(), P(), P(None, "tensor")] + weights
    for spec in moments:
        placed += [spec, spec]
    outs = [P(("dp", "tensor"), None)] * 2
    for spec in moments:
        outs += [spec, spec, spec]
    return jax.shard_map(
        shards, mesh=mesh, in_specs=tuple(placed), out_specs=tuple(outs), check_vma=False
    )
```

```python
import functools

import jax
import jax.numpy as jnp
from jax import lax
from jax.experimental import pallas as pl
from jax.experimental.pallas import tpu as pltpu
from jax.sharding import PartitionSpec as P

D = 2560
L = 2560
BLOCK = 256
F = 7680
STEP = 10
N_DP = 16
N_T = 8
ROWS = 512
OWN = ROWS // N_T
WIDTH = L // N_T
HIDE = F // N_T
HALF = 80
GATE_HALF = 8
MESH = pl.DeviceIdType.MESH

NORM_EPS = 1e-06
ADAM_EPS = 1e-08
BETA_ONE = 0.9
BETA_TWO = 0.95


def params(cid):
    return pltpu.CompilerParams(
        collective_id=cid, has_side_effects=True, vmem_limit_bytes=62 * 2**20
    )


def vmem(count):
    return [pl.BlockSpec(memory_space=pltpu.VMEM)] * count


def greet(peers):
    barrier = pltpu.get_barrier_semaphore()
    for peer in peers:
        pl.semaphore_signal(barrier, inc=1, device_id=peer, device_id_type=MESH)
    pl.semaphore_wait(barrier, len(peers))


def remote(source, target, send_sem, recv_sem, peer):
    return pltpu.make_async_remote_copy(
        src_ref=source,
        dst_ref=target,
        send_sem=send_sem,
        recv_sem=recv_sem,
        device_id=peer,
        device_id_type=MESH,
    )


def place():
    index = lax.axis_index("tensor")
    return index // 2, lax.rem(index, 2)


def at_x(x, core, by):
    return {"tensor": lax.rem(x + by, 4) * 2 + core}


def tensor_peers():
    x, core = place()
    return [{"tensor": x * 2 + 1 - core}] + [at_x(x, core, by) for by in (1, 2, 3)]


def chip_row(by, which):
    x, _ = place()
    return pl.multiple_of((lax.rem(x + by, 4) * 2 + which) * OWN, OWN)


class TensorSum:
    ORDER = (2, 1, 3, 0)

    def __init__(self, partial, pair, held, landed, pair_send, pair_recv, x_send, x_recv):
        self.partial, self.pair, self.held, self.landed = partial, pair, held, landed
        self.sems = pair_send, pair_recv, x_send, x_recv
        self.pair_copies, self.x_copies = {}, {}

    def give(self, by):
        x, core = place()
        copy = remote(
            self.partial.at[pl.ds(chip_row(by, 1 - core), OWN)],
            self.pair.at[by],
            self.sems[0].at[by],
            self.sems[1].at[by],
            {"tensor": x * 2 + 1 - core},
        )
        copy.start()
        self.pair_copies[by] = copy

    def pass_on(self, by):
        x, core = place()
        self.pair_copies[by].wait_recv()
        mine = self.partial[pl.ds(chip_row(by, core), OWN), :].astype(jnp.float32)
        self.held[by - 1] = (mine + self.pair[by].astype(jnp.float32)).astype(jnp.bfloat16)
        copy = remote(
            self.held.at[by - 1],
            self.landed.at[by - 1],
            self.sems[2].at[by - 1],
            self.sems[3].at[by - 1],
            at_x(x, core, by),
        )
        copy.start()
        self.x_copies[by] = copy

    def start(self, produce):
        for step, by in enumerate(self.ORDER):
            produce(by)
            self.give(by)
            if step:
                self.pass_on(self.ORDER[step - 1])

    def finish(self):
        _, core = place()
        self.pair_copies[0].wait_recv()
        total = self.partial[pl.ds(chip_row(0, core), OWN), :].astype(jnp.float32)
        total = total + self.pair[0].astype(jnp.float32)
        for by in (1, 3, 2):
            self.x_copies[by].wait_recv()
            total = total + self.landed[by - 1].astype(jnp.float32)
        for by in self.ORDER:
            self.pair_copies[by].wait_send()
        for by in (2, 1, 3):
            self.x_copies[by].wait_send()
        return total


def reduce_scratch():
    return [
        pltpu.VMEM((4, OWN, D), jnp.bfloat16),
        pltpu.VMEM((3, OWN, D), jnp.bfloat16),
        pltpu.VMEM((3, OWN, D), jnp.bfloat16),
        pltpu.SemaphoreType.DMA((4,)),
        pltpu.SemaphoreType.DMA((4,)),
        pltpu.SemaphoreType.DMA((3,)),
        pltpu.SemaphoreType.DMA((3,)),
    ]


class TensorGather:
    def __init__(self, whole, x_send, x_recv, pair_send, pair_recv):
        self.whole, self.sems = whole, (x_send, x_recv, pair_send, pair_recv)

    def start(self, block):
        x, core = place()
        self.whole[pl.ds(chip_row(0, core), OWN), :] = block
        mine = self.whole.at[pl.ds(chip_row(0, core), OWN)]
        self.sends = []
        for by in (2, 1, 3):
            copy = remote(
                mine, mine, self.sems[0].at[by - 1], self.sems[1].at[by - 1], at_x(x, core, by)
            )
            copy.start()
            self.sends.append(copy)
        first = remote(
            mine, mine, self.sems[2].at[0], self.sems[3].at[0], {"tensor": x * 2 + 1 - core}
        )
        first.start()
        self.pairs = [first]

    def finish(self):
        x, core = place()
        for by in (1, 3, 2):
            block = self.whole.at[pl.ds(chip_row(4 - by, core), OWN)]
            arrived = remote(
                block, block, self.sems[0].at[by - 1], self.sems[1].at[by - 1], at_x(x, core, by)
            )
            arrived.wait_recv()
            copy = remote(
                block,
                block,
                self.sems[2].at[by],
                self.sems[3].at[by],
                {"tensor": x * 2 + 1 - core},
            )
            copy.start()
            self.pairs.append(copy)
        for copy in self.sends:
            copy.wait_send()
        for copy in self.pairs:
            copy.wait()


class DataSum:
    LOW, HIGH = pl.ds(0, 2), pl.ds(2, 2)

    def __init__(self, grad, own, near, via, ring, last, send, recv, local, rows):
        self.grad, self.own, self.near, self.via = grad, own, near, via
        self.ring, self.last, self.rows = ring, last, rows
        self.send, self.recv, self.local = send, recv, local
        me = lax.axis_index("dp")
        z, y = me // 4, lax.rem(me, 4)
        self.first = (y, z)
        self.second = (z, y)

    def peer(self, half, first_by, second_by):
        a = lax.rem(self.first[half] + first_by + 4, 4)
        b = lax.rem(self.second[half] + second_by + 4, 4)
        return {"dp": b * 4 + a if half == 0 else a * 4 + b}

    def block(self, half, by, part):
        a = lax.rem(self.first[half] + by + 4, 4)
        return self.grad.at[part, a, 0] if half == 0 else self.grad.at[a, part, 1]

    def ship(self, half, slot, source, target, first_by, second_by):
        copy = remote(
            source,
            target,
            self.send.at[half, slot],
            self.recv.at[half, slot],
            self.peer(half, first_by, second_by),
        )
        copy.start()
        self.copies[half, slot] = copy

    def start(self):
        self.copies, self.locals = {}, {}
        for half in (0, 1):
            self.ship(half, 0, self.block(half, 2, self.LOW), self.via.at[half, 0], 1, 0)
            self.ship(half, 1, self.block(half, 2, self.HIGH), self.via.at[half, 1], -1, 0)
            pairs = (
                (self.block(half, 1, self.LOW), self.near.at[half, 0]),
                (self.block(half, -1, self.HIGH), self.near.at[half, 1]),
                (self.block(half, 0, pl.ds(0, 4)), self.own.at[half]),
            )
            for number, (source, target) in enumerate(pairs):
                copy = pltpu.make_async_copy(source, target, self.local.at[half, number])
                copy.start()
                self.locals[half, number] = copy
        for half in (0, 1):
            self.ship(half, 2, self.block(half, 1, self.HIGH), self.ring.at[half, 0], 1, 0)
            self.ship(half, 3, self.block(half, -1, self.LOW), self.ring.at[half, 1], -1, 0)

    def add(self, target, sources, blocks):
        size = 16 if self.rows % 16 == 0 else 8
        steps = self.rows // size

        def body(index, _):
            block = index // steps
            at = pl.ds(pl.multiple_of(lax.rem(index, steps) * size, size), size)
            total = target[block, at, :].astype(jnp.float32)
            for source in sources:
                total = total + source[block, at, :].astype(jnp.float32)
            target[block, at, :] = total.astype(target.dtype)
            return 0

        lax.fori_loop(0, blocks * steps, body, 0)

    def middle(self):
        for half in (0, 1):
            for side in (0, 1):
                self.locals[half, side].wait()
                self.copies[half, side].wait_recv()
                self.add(self.near.at[half, side], [self.via.at[half, side]], 2)
                self.ship(
                    half,
                    4 + side,
                    self.near.at[half, side],
                    self.ring.at[half, 2 + side],
                    1 - 2 * side,
                    0,
                )

    def turn(self):
        for half in (0, 1):
            self.locals[half, 2].wait()
            for slot in (2, 3, 4, 5):
                self.copies[half, slot].wait_recv()
            ring = self.ring
            self.add(self.own.at[half, self.LOW], [ring.at[half, 1], ring.at[half, 2]], 2)
            self.add(self.own.at[half, self.HIGH], [ring.at[half, 0], ring.at[half, 3]], 2)
            for by in (1, 2, 3):
                to = lax.rem(self.second[half] + by, 4)
                self.ship(
                    half, 5 + by, self.own.at[half, to], self.last.at[half, by - 1], 0, by
                )

    def finish(self, share):
        size = 16 if self.rows % 16 == 0 else 8
        for half in (0, 1):
            for by in (1, 2, 3):
                self.copies[half, 5 + by].wait_recv()

            def body(index, _, half=half):
                at = pl.ds(pl.multiple_of(index * size, size), size)
                total = self.own[half, self.second[half], at, :].astype(jnp.float32)
                for by in range(3):
                    total = total + self.last[half, by, at, :].astype(jnp.float32)
                share[pl.ds(pl.multiple_of(half * self.rows + index * size, size), size), :] = total
                return 0

            lax.fori_loop(0, self.rows // size, body, 0)
        for copy in self.copies.values():
            copy.wait_send()


def data_scratch(rows, columns, dtype):
    dma = pltpu.SemaphoreType.DMA
    return [
        pltpu.VMEM((2, 4, rows, columns), dtype),
        pltpu.VMEM((2, 2, 2, rows, columns), dtype),
        pltpu.VMEM((2, 2, 2, rows, columns), dtype),
        pltpu.VMEM((2, 4, 2, rows, columns), dtype),
        pltpu.VMEM((2, 3, rows, columns), dtype),
        dma((2, 9)),
        dma((2, 9)),
        dma((2, 3)),
    ]


def gather_scratch():
    return [
        pltpu.SemaphoreType.DMA((3,)),
        pltpu.SemaphoreType.DMA((3,)),
        pltpu.SemaphoreType.DMA((4,)),
        pltpu.SemaphoreType.DMA((4,)),
    ]


def dp_peers():
    me = lax.axis_index("dp")
    return [{"dp": lax.rem(me + by, N_DP)} for by in range(1, N_DP)]


def place_matrix(shift):
    row = lax.broadcasted_iota(jnp.int32, (WIDTH, 2 * BLOCK), 0)
    lane = lax.broadcasted_iota(jnp.int32, (WIDTH, 2 * BLOCK), 1)
    return jnp.where(lane == row + shift, 1.0, 0.0).astype(jnp.bfloat16)


def wide_gates(gates, wide, shift):
    row = lax.broadcasted_iota(jnp.int32, (WIDTH, BLOCK), 0)
    low = row + shift < BLOCK
    for gate in range(2):
        matrix = gates[gate].astype(jnp.float32)
        wide[gate, :, 0:BLOCK] = jnp.where(low, matrix, 0.0).astype(jnp.bfloat16)
        wide[gate, :, BLOCK : 2 * BLOCK] = jnp.where(low, 0.0, matrix).astype(jnp.bfloat16)


def one_less_exp(z):
    series = 1.0 + z / 7.0
    for term in (6.0, 5.0, 4.0, 3.0, 2.0):
        series = 1.0 + z / term * series
    return jnp.where(z > -0.35, -z * series, 1.0 - jnp.exp(z))


def tiles(count, size, body):
    def step(index, _):
        body(pl.multiple_of(index * size, size))
        return 0

    lax.fori_loop(0, count, step, 0)


def norm_rows(source, target, gain, rows):
    def body(first):
        at = pl.ds(first, 16)
        target[at, :] = rms_norm(source[at, :].astype(jnp.float32), gain).astype(jnp.bfloat16)

    tiles(rows // 16, 16, body)


def shifted(values, by, fill, reverse):
    count = values.shape[0]
    row = lax.broadcasted_iota(jnp.int32, values.shape, 0)
    if reverse:
        return jnp.where(row < count - by, pltpu.roll(values, count - by, 0), fill)
    return jnp.where(row >= by, pltpu.roll(values, by, 0), fill)


def local_scan(factor_at, term_at, values, prods, reverse):
    def step(index, held):
        prod, value = held
        first = pl.multiple_of((ROWS // 8 - 1 - index if reverse else index) * 8, 8)
        factor, term = factor_at(first), term_at(first)
        for by in (1, 2, 4):
            term = term + factor * shifted(term, by, 0.0, reverse)
            factor = factor * shifted(factor, by, 1.0, reverse)
        value = factor * value + term
        prod = factor * prod
        values[pl.ds(first, 8), :] = value
        prods[pl.ds(first, 8), :] = prod
        last = 0 if reverse else 7
        return (
            jnp.broadcast_to(prod[last : last + 1], prod.shape),
            jnp.broadcast_to(value[last : last + 1], value.shape),
        )

    ones = jnp.ones((8, WIDTH), jnp.float32)
    return lax.fori_loop(0, ROWS // 8, step, (ones, jnp.zeros_like(ones)), unroll=8)


def start_share(slots, send, recv):
    me = lax.axis_index("dp")
    copies = []
    for by in range(1, N_DP):
        copy = remote(
            slots.at[me], slots.at[me], send.at[by], recv.at[by], {"dp": lax.rem(me + by, N_DP)}
        )
        copy.start()
        copies.append(copy)
    return copies


def beside_peers():
    index = lax.axis_index("tensor")
    return {"tensor": lax.rem(index + 1, N_T)}, {"tensor": lax.rem(index + N_T - 1, N_T)}


def far_peer():
    index = lax.axis_index("tensor")
    _, core = place()
    return {"tensor": lax.rem(index + N_T - 1 + 2 * core, N_T)}


def gelu_parts(y):
    c = 0.7978845608028654
    inner = jnp.tanh(c * (y + 0.044715 * y * y * y))
    half = 0.5 * (1.0 + inner)
    slope = half + 0.5 * y * (1.0 - inner * inner) * c * (1.0 + 3 * 0.044715 * y * y)
    return y * half, slope


def forward_kernel(
    tokens, own, branch_hbm, gates, out_hbm, chan, gains, flags,
    residual, normed_two, normed_one, ext, window, pre_a, pre_x, carry, state, branch_y, mixed,
    branch_w, out_w, halo, halo_norm, wide, placing, update, values, prods, gelu_y, low, high, slots, partial,
    load_sem, halo_send, halo_recv, side_send, side_recv, slot_send, slot_recv, *scratch
):
    me, index = lax.axis_index("dp"), lax.axis_index("tensor")
    shift = lax.rem(index * WIDTH, BLOCK)
    loads = [
        pltpu.make_async_copy(branch_hbm.at[0], branch_w.at[0], load_sem.at[0]),
        pltpu.make_async_copy(branch_hbm.at[1], branch_w.at[1], load_sem.at[1]),
        pltpu.make_async_copy(out_hbm, out_w, load_sem.at[2]),
    ]
    for load in loads:
        load.start()
    greet(dp_peers() + tensor_peers() + [far_peer()])
    send_halo = remote(
        tokens.at[pl.ds(ROWS - 16, 16)],
        halo,
        halo_send,
        halo_recv,
        {"dp": lax.rem(me + 1, N_DP)},
    )
    send_halo.start()
    wide_gates(gates, wide, shift)
    placing[...] = place_matrix(shift)
    gain = gains[0:1, :]
    norm_rows(tokens, normed_one, gain, ROWS)
    loads[0].wait()

    def branch_tile(first):
        at = pl.ds(first, 128)
        value = times_transposed(normed_one[at, :], branch_w[0])
        ext[pl.ds(first + 16, 128), :] = value.astype(jnp.bfloat16).astype(jnp.float32)

    tiles(4, 128, branch_tile)
    send_halo.wait()
    norm_rows(halo, halo_norm, gain, 16)
    ext[0:16, :] = times_transposed(halo_norm[...], branch_w[0]).astype(jnp.bfloat16).astype(jnp.float32)

    def conv_tile(first):
        near = ext[pl.ds(first + 8, 136), :]
        total = chan[0:1, :] * near[8:]
        for tap in range(1, 4):
            counted = flags[pl.ds(first, 128), tap : tap + 1] > 0.0
            total = total + chan[tap : tap + 1, :] * jnp.where(counted, near[8 - tap : 136 - tap], 0.0)
        window[pl.ds(first, 128), :] = matmul(total.astype(jnp.bfloat16), placing[...]).astype(
            jnp.bfloat16
        )

    tiles(4, 128, conv_tile)
    up, down = beside_peers()
    to_up = remote(
        window.at[:, pl.ds(BLOCK, BLOCK)], low, side_send.at[0], side_recv.at[0], up
    )
    to_down = remote(window.at[:, pl.ds(0, BLOCK)], high, side_send.at[1], side_recv.at[1], down)
    to_up.start()
    to_down.start()
    loads[1].wait()

    def gelu_tile(first):
        at = pl.ds(first, 128)
        branch_y[at, :] = times_transposed(normed_one[at, :], branch_w[1])

    tiles(4, 128, gelu_tile)
    to_up.wait()
    to_down.wait()

    def window_tile(first):
        at = pl.ds(first, 128)
        own_conv = lax.dot_general(
            window[at, :], placing[...], (((1,), (1,)), ((), ())), preferred_element_type=jnp.float32
        )
        from_low = jnp.where(shift != 0, low[at, :].astype(jnp.float32), 0.0)
        from_high = jnp.where(shift != 192, high[at, :].astype(jnp.float32), 0.0)
        whole = window[at, :].astype(jnp.float32) + jnp.concatenate([from_low, from_high], 1)
        whole = whole.astype(jnp.bfloat16)
        window[at, :] = whole
        a = times_transposed(whole, wide[0])
        x = times_transposed(whole, wide[1])
        pre_a[at, :] = a
        pre_x[at, :] = x
        reset = flags[at, 4:5] > 0.0
        log_a = -8.0 * jax.nn.sigmoid(a) * chan[5:6, :]
        carry[at, :] = jnp.where(reset, 0.0, jnp.exp(log_a))
        scale = jnp.where(reset, 1.0, jnp.sqrt(one_less_exp(2.0 * log_a)))
        update[at, :] = own_conv * jax.nn.sigmoid(x) * scale

    tiles(4, 128, window_tile)
    prod, value = local_scan(
        lambda first: carry[pl.ds(first, 8), :],
        lambda first: update[pl.ds(first, 8), :],
        values,
        prods,
        False,
    )
    slots[me, 0:1, :] = prod[0:1]
    slots[me, 1:2, :] = value[0:1]
    copies = start_share(slots, slot_send, slot_recv)

    def activate(first):
        at = pl.ds(first, 64)
        y = branch_y[at, :]
        gelu_y[at, :] = gelu_parts(y)[0]

    tiles(8, 64, activate)
    for copy in copies:
        copy.wait()
    before = jnp.zeros((1, WIDTH), jnp.float32)
    for place_at in range(N_DP - 1):
        longer = slots[place_at, 0:1, :] * before + slots[place_at, 1:2, :]
        before = jnp.where(place_at < me, longer, before)

    state[0:8, :] = jnp.broadcast_to(before, (8, WIDTH))

    def finish(first):
        at = pl.ds(first, 64)
        total = values[at, :] + prods[at, :] * before
        state[pl.ds(first + 8, 64), :] = total
        mixed[at, :] = (total * gelu_y[at, :]).astype(jnp.bfloat16)

    tiles(8, 64, finish)
    loads[2].wait()

    def produce(by):
        at = pl.ds(pl.multiple_of(chip_row(by, 0), 128), 128)
        partial[at, :] = matmul(mixed[at, :], out_w[...]).astype(jnp.bfloat16)

    summed = TensorSum(partial, *scratch[:7])
    summed.start(produce)
    total = own[...].astype(jnp.float32) + summed.finish()
    residual[...] = total
    gather = TensorGather(normed_two, *scratch[7:])
    gather.start(rms_norm(total, gains[1:2, :]).astype(jnp.bfloat16))
    gather.finish()


def mixer_forward(tokens, own, branch_in, gate_blocks, out_proj, chan, gains, flags):
    wide_f32 = jax.ShapeDtypeStruct((ROWS, WIDTH), jnp.float32)
    f32, bf16 = jnp.float32, jnp.bfloat16
    dma = pltpu.SemaphoreType.DMA
    here = pl.BlockSpec(memory_space=pltpu.VMEM)
    there = pl.BlockSpec(memory_space=pl.ANY)
    return pl.pallas_call(
        forward_kernel,
        out_shape=(
            jax.ShapeDtypeStruct((OWN, D), f32),
            jax.ShapeDtypeStruct((ROWS, D), bf16),
            jax.ShapeDtypeStruct((ROWS, D), bf16),
            jax.ShapeDtypeStruct((ROWS + 16, WIDTH), f32),
            jax.ShapeDtypeStruct((ROWS, 2 * BLOCK), bf16),
            wide_f32,
            wide_f32,
            wide_f32,
            jax.ShapeDtypeStruct((ROWS + 8, WIDTH), f32),
            wide_f32,
            jax.ShapeDtypeStruct((ROWS, WIDTH), bf16),
        ),
        in_specs=[here, here, there, here, there, here, here, here],
        out_specs=tuple(vmem(11)),
        scratch_shapes=[
            pltpu.VMEM((2, WIDTH, D), bf16),
            pltpu.VMEM((WIDTH, D), bf16),
            pltpu.VMEM((16, D), bf16),
            pltpu.VMEM((16, D), bf16),
            pltpu.VMEM((2, WIDTH, 2 * BLOCK), bf16),
            pltpu.VMEM((WIDTH, 2 * BLOCK), bf16),
            pltpu.VMEM((ROWS, WIDTH), f32),
            pltpu.VMEM((ROWS, WIDTH), f32),
            pltpu.VMEM((ROWS, WIDTH), f32),
            pltpu.VMEM((ROWS, WIDTH), f32),
            pltpu.VMEM((ROWS, BLOCK), bf16),
            pltpu.VMEM((ROWS, BLOCK), bf16),
            pltpu.VMEM((N_DP, 8, WIDTH), f32),
            pltpu.VMEM((ROWS, D), bf16),
            dma((3,)),
            dma,
            dma,
            dma((2,)),
            dma((2,)),
            dma((N_DP,)),
            dma((N_DP,)),
        ]
        + reduce_scratch()
        + gather_scratch(),
        compiler_params=params(1),
    )(tokens, own, branch_in, gate_blocks, out_proj, chan, gains, flags)


def norm_back(value, gain, grad):
    scale = lax.rsqrt(jnp.mean(value * value, axis=-1, keepdims=True) + NORM_EPS)
    unit = value * scale
    scaled = grad * gain
    back = scale * (scaled - unit * jnp.mean(scaled * unit, axis=-1, keepdims=True))
    return back, jnp.sum(grad * unit, axis=0, keepdims=True)


def middle_kernel(
    normed, residual, dy, dy_own, gains, ffn_hbm, down_hbm,
    out, grad, grad_gain, rounded, gate_grad, up_grad, down_grad, down_share, up_share,
    ffn_w, down_w, hidden, to_gate, to_up, gate_pre, up_pre, grad_hidden, partial, stage,
    load_sem, stage_sem, *scratch
):
    loads = [
        pltpu.make_async_copy(down_hbm, down_w, load_sem.at[0]),
        pltpu.make_async_copy(ffn_hbm.at[pl.ds(0, HIDE)], ffn_w.at[pl.ds(0, HIDE)], load_sem.at[1]),
        pltpu.make_async_copy(
            ffn_hbm.at[pl.ds(HIDE, HIDE)], ffn_w.at[pl.ds(HIDE, HIDE)], load_sem.at[2]
        ),
    ]
    for load in loads:
        load.start()
    greet(dp_peers() + tensor_peers())
    summed = TensorSum(partial, *scratch[:7])
    summed_out = TensorSum(partial, *scratch[7:14])
    gather = TensorGather(rounded, *scratch[14:18])
    down_sum = DataSum(down_grad, *scratch[18:26], HALF)
    up_sum = DataSum(up_grad, *scratch[26:34], HALF)
    for number, (start, size) in enumerate(((0, 384), (384, 384), (768, 192))):
        units = pl.ds(start, size)
        if number == 0:
            loads[0].wait()
        grad_hidden[:, 0:size] = times_transposed(dy[...], down_w[units, :])
        if number == 0:
            loads[1].wait()
        gate_pre[:, 0:size] = times_transposed(normed[...], ffn_w[units, :])
        if number == 0:
            loads[2].wait()
        up_pre[:, 0:size] = times_transposed(normed[...], ffn_w[pl.ds(HIDE + start, size), :])

        def activate(first, units=units, size=size):
            at = pl.ds(first, 32)
            value, slope = gelu_parts(gate_pre[at, 0:size])
            up, back = up_pre[at, 0:size], grad_hidden[at, 0:size]
            hidden[at, units] = (value * up).astype(jnp.bfloat16)
            to_up[at, units] = (back * value).astype(jnp.bfloat16)
            to_gate[at, units] = (back * up * slope).astype(jnp.bfloat16)

        tiles(ROWS // 32, 32, activate)

    def produce(by):
        at = pl.ds(pl.multiple_of(chip_row(by, 0), 128), 128)
        total = matmul(to_gate[at, :], ffn_w[0:HIDE, :]) + matmul(
            to_up[at, :], ffn_w[HIDE : 2 * HIDE, :]
        )
        partial[at, :] = total.astype(jnp.bfloat16)

    summed.start(produce)

    def weight_grad(jobs):
        pending = {}
        for z in range(4):
            columns = pl.ds(z * 640, 640)
            for job, (left, right, target) in enumerate(jobs):
                slot = (z * len(jobs) + job) % 2
                if slot in pending:
                    pending[slot].wait()
                value = transposed_times(left[:, columns], right[...]).astype(jnp.bfloat16)
                stage[slot] = value.reshape(4, 2, HALF, HIDE)
                copy = pltpu.make_async_copy(stage.at[slot], target.at[z], stage_sem.at[slot])
                copy.start()
                pending[slot] = copy
        for copy in pending.values():
            copy.wait()

    weight_grad([(dy, hidden, down_grad)])
    down_sum.start()
    norm_grad = summed.finish()
    back, gain_part = norm_back(residual[...], gains[1:2, :], norm_grad)
    back = back + dy_own[...].astype(jnp.float32)
    grad[...] = back
    grad_gain[...] = gain_part
    gather.start(back.astype(jnp.bfloat16))

    def produce_out(by):
        at = pl.ds(pl.multiple_of(chip_row(by, 0), 128), 128)
        partial[at, :] = matmul(hidden[at, :], down_w[...]).astype(jnp.bfloat16)

    for by in summed_out.ORDER:
        produce_out(by)
        summed_out.give(by)
    weight_grad([(normed, to_up, up_grad), (normed, to_gate, gate_grad)])
    down_sum.middle()
    up_sum.start()
    gather.finish()
    for by in (2, 1, 3):
        summed_out.pass_on(by)
    down_sum.turn()
    up_sum.middle()
    out[...] = (residual[...] + summed_out.finish()).astype(jnp.bfloat16)
    down_sum.finish(down_share)
    up_sum.turn()
    up_sum.finish(up_share)


def ffn_middle(normed, residual, dy, dy_own, gains, ffn_t, down):
    f32, bf16 = jnp.float32, jnp.bfloat16
    dma = pltpu.SemaphoreType.DMA
    here = pl.BlockSpec(memory_space=pltpu.VMEM)
    there = pl.BlockSpec(memory_space=pl.ANY)
    shared = jax.ShapeDtypeStruct((4, 4, 2, HALF, HIDE), bf16)
    share = jax.ShapeDtypeStruct((2 * HALF, HIDE), f32)
    return pl.pallas_call(
        middle_kernel,
        out_shape=(
            jax.ShapeDtypeStruct((OWN, D), bf16),
            jax.ShapeDtypeStruct((OWN, D), f32),
            jax.ShapeDtypeStruct((1, D), f32),
            jax.ShapeDtypeStruct((ROWS, D), bf16),
            shared,
            shared,
            shared,
            share,
            share,
        ),
        in_specs=[here] * 5 + [there] * 2,
        out_specs=tuple([here] * 4 + [there] * 3 + [here] * 2),
        scratch_shapes=[
            pltpu.VMEM((2 * HIDE, D), bf16),
            pltpu.VMEM((HIDE, D), bf16),
            pltpu.VMEM((ROWS, HIDE), bf16),
            pltpu.VMEM((ROWS, HIDE), bf16),
            pltpu.VMEM((ROWS, HIDE), bf16),
            pltpu.VMEM((ROWS, 384), f32),
            pltpu.VMEM((ROWS, 384), f32),
            pltpu.VMEM((ROWS, 384), f32),
            pltpu.VMEM((ROWS, D), bf16),
            pltpu.VMEM((2, 4, 2, HALF, HIDE), bf16),
            dma((3,)),
            dma((2,)),
        ]
        + reduce_scratch()
        + reduce_scratch()
        + gather_scratch()
        + data_scratch(HALF, HIDE, bf16)
        + data_scratch(HALF, HIDE, bf16),
        compiler_params=params(2),
    )(normed, residual, dy, dy_own, gains, ffn_t, down)


def backward_kernel(
    rounded, normed_one, own, grad, grad_gain_two, chan, gains, flags, gates,
    ext, window, pre_a, pre_x, carry, state, branch_y, mixed, out_hbm, branch_hbm, gate_grad,
    tokens_grad, gain_sum, channel_sum, gate_share, outy_share, bx_share, blocks_share, outy_grad, bx_grad,
    out_w, branch_w, wide, to_y, to_x, back, local, sums, prods, to_a, to_gx, window_grad, low, high,
    low_in, high_in, conv_grad, slots, halo, halo_in, blocks_grad, partial, stage_y, stage_x,
    gain_t, gain_dp, chan_dp,
    load_sem, stage_sem, slot_send, slot_recv, side_send, side_recv, halo_send, halo_recv,
    t_send, t_recv, g_send, g_recv, c_send, c_recv, *scratch
):
    me, index = lax.axis_index("dp"), lax.axis_index("tensor")
    shift = lax.rem(index * WIDTH, BLOCK)
    loads = [
        pltpu.make_async_copy(out_hbm, out_w, load_sem.at[0]),
        pltpu.make_async_copy(branch_hbm, branch_w, load_sem.at[1]),
    ]
    for load in loads:
        load.start()
    greet(dp_peers() + tensor_peers() + [far_peer()])
    summed = TensorSum(partial, *scratch[:7])
    gate_sum = DataSum(gate_grad, *scratch[7:15], HALF)
    outy_sum = DataSum(outy_grad, *scratch[15:23], HALF)
    bx_sum = DataSum(bx_grad, *scratch[23:31], HALF)
    blocks_sum = DataSum(blocks_grad, *scratch[31:39], GATE_HALF)
    gate_sum.start()
    wide_gates(gates, wide, shift)
    loads[0].wait()

    def mixed_tile(first):
        at = pl.ds(first, 128)
        local[at, :] = times_transposed(rounded[at, :], out_w[...])

    tiles(4, 128, mixed_tile)

    def gelu_tile(first):
        at = pl.ds(first, 64)
        value, slope = gelu_parts(branch_y[at, :])
        mixed_grad = local[at, :]
        to_y[at, :] = (mixed_grad * state[pl.ds(first + 8, 64), :] * slope).astype(jnp.bfloat16)
        local[at, :] = mixed_grad * value

    tiles(8, 64, gelu_tile)
    back[0:ROWS, :] = carry[...]
    back[ROWS : ROWS + 8, :] = jnp.ones((8, WIDTH), jnp.float32)
    prod, value = local_scan(
        lambda first: back[pl.ds(first, 16), :][1:9],
        lambda first: local[pl.ds(first, 8), :],
        sums,
        prods,
        True,
    )
    slots[me, 0:1, :] = carry[0:1, :] * prod[0:1]
    slots[me, 1:2, :] = carry[0:1, :] * value[0:1]
    copies = start_share(slots, slot_send, slot_recv)

    def weight_grad(target, held, jobs):
        pending = {}
        for z in range(4):
            columns = pl.ds(z * 640, 640)
            if z >= 2:
                pending[z % 2].wait()
            parts = [transposed_times(left[:, columns], right[...]) for left, right in jobs]
            whole = parts[0] if len(parts) == 1 else jnp.concatenate(parts, 1)
            held[z % 2] = whole.astype(jnp.bfloat16).reshape(4, 2, HALF, whole.shape[1])
            copy = pltpu.make_async_copy(held.at[z % 2], target.at[z], stage_sem.at[z % 2])
            copy.start()
            pending[z % 2] = copy
        for copy in pending.values():
            copy.wait()

    weight_grad(outy_grad, stage_y, [(rounded, mixed), (normed_one, to_y)])
    gate_sum.middle()
    outy_sum.start()
    for copy in copies:
        copy.wait()
    later = jnp.zeros((1, WIDTH), jnp.float32)
    for place_at in range(N_DP - 1, 0, -1):
        longer = slots[place_at, 0:1, :] * later + slots[place_at, 1:2, :]
        later = jnp.where(place_at > me, longer, later)
    plus, decay_slope = chan[5:6, :], chan[6:7, :]
    zero_row = jnp.zeros((1, WIDTH), jnp.float32)

    def gate_tile(first, decay_grad):
        at = pl.ds(first, 64)
        total = sums[at, :] + prods[at, :] * later
        near = state[pl.ds(first, 72), :]
        conv = lax.dot_general(
            window[at, :], place_matrix(shift), (((1,), (1,)), ((), ())), preferred_element_type=jnp.float32
        )
        reset = flags[at, 4:5] > 0.0
        gate_a, gate_x = jax.nn.sigmoid(pre_a[at, :]), jax.nn.sigmoid(pre_x[at, :])
        log_a = -8.0 * gate_a * plus
        keep = jnp.exp(log_a)
        scale = jnp.sqrt(one_less_exp(2.0 * log_a))
        scale_here = jnp.where(reset, 1.0, scale)
        conv_grad[at, :] = total * gate_x * scale_here
        to_gx[at, :] = (total * conv * scale_here * gate_x * (1.0 - gate_x)).astype(jnp.bfloat16)
        log_grad = total * near[7:71] * keep - total * conv * gate_x * keep * keep / scale
        log_grad = jnp.where(reset, 0.0, log_grad)
        to_a[at, :] = (log_grad * (-8.0 * plus) * gate_a * (1.0 - gate_a)).astype(jnp.bfloat16)
        return decay_grad + jnp.sum(log_grad * (-8.0 * gate_a), axis=0, keepdims=True)

    decay_grad = lax.fori_loop(
        0, 8, lambda i, held: gate_tile(pl.multiple_of(i * 64, 64), held), zero_row
    )
    decay_grad = decay_grad * decay_slope

    def window_tile(first):
        at = pl.ds(first, 128)
        total = matmul(to_a[at, :], wide[0]) + matmul(to_gx[at, :], wide[1])
        window_grad[at, :] = total
        low[at, :] = total[:, 0:BLOCK].astype(jnp.bfloat16)
        high[at, :] = total[:, BLOCK : 2 * BLOCK].astype(jnp.bfloat16)

    tiles(4, 128, window_tile)
    up, down = beside_peers()
    to_up = remote(high, low_in, side_send.at[0], side_recv.at[0], up)
    to_down = remote(low, high_in, side_send.at[1], side_recv.at[1], down)
    to_up.start()
    to_down.start()
    column = lax.broadcasted_iota(jnp.int32, (BLOCK, WIDTH), 1)
    chosen = []
    for right in (to_a, to_gx):
        both = transposed_times(window[...], right[...])
        chosen.append(
            jnp.where(column + shift < BLOCK, both[0:BLOCK], both[BLOCK : 2 * BLOCK])
        )
    blocks_grad[...] = jnp.concatenate(chosen, 1).reshape(4, 4, 2, GATE_HALF, 2 * WIDTH)
    to_up.wait()
    to_down.wait()

    def conv_tile(first):
        at = pl.ds(first, 64)
        from_low = jnp.where(shift != 0, low_in[at, :].astype(jnp.float32), 0.0)
        from_high = jnp.where(shift != 192, high_in[at, :].astype(jnp.float32), 0.0)
        total = window_grad[at, :] + jnp.concatenate([from_low, from_high], 1)
        total = pltpu.roll(total, lax.rem(2 * BLOCK - shift, 2 * BLOCK), 1)
        conv_grad[at, :] = conv_grad[at, :] + total[:, 0:WIDTH]

    tiles(8, 64, conv_tile)
    conv_grad[ROWS : ROWS + 8, :] = jnp.zeros((8, WIDTH), jnp.float32)
    head = conv_grad[0:8, :]
    rows = []
    for row in range(3):
        total = zero_row
        for tap in range(3 - row, 4):
            from_row = row - 3 + tap
            counted = flags[from_row : from_row + 1, tap : tap + 1] > 0.0
            total = total + chan[tap : tap + 1, :] * jnp.where(
                counted, head[from_row : from_row + 1], 0.0
            )
        rows.append(total)
    halo[0:5, :] = jnp.zeros((5, WIDTH), jnp.float32)
    for row in range(3):
        halo[5 + row : 6 + row, :] = rows[row]
    send_halo = remote(halo, halo_in, halo_send, halo_recv, {"dp": lax.rem(me + N_DP - 1, N_DP)})
    send_halo.start()
    blocks_sum.start()

    def tap_tile(first, held):
        at = pl.ds(first, 64)
        near = conv_grad[pl.ds(first, 72), :]
        marks = flags[pl.ds(first, 72), :]
        behind = ext[pl.ds(first + 8, 72), :]
        total = chan[0:1, :] * near[0:64]
        taps = [held[0] + jnp.sum(near[0:64] * behind[8:72], axis=0, keepdims=True)]
        for tap in range(1, 4):
            counted = marks[tap : tap + 64, tap : tap + 1] > 0.0
            total = total + chan[tap : tap + 1, :] * jnp.where(counted, near[tap : tap + 64], 0.0)
            here = jnp.where(marks[0:64, tap : tap + 1] > 0.0, near[0:64], 0.0)
            taps.append(
                held[tap] + jnp.sum(here * behind[8 - tap : 72 - tap], axis=0, keepdims=True)
            )
        local[at, :] = total
        return tuple(taps)

    tap_grads = lax.fori_loop(
        0, 8, lambda i, held: tap_tile(pl.multiple_of(i * 64, 64), held), (zero_row,) * 4
    )
    for tap in range(4):
        chan_dp[me, tap : tap + 1, :] = tap_grads[tap]
    chan_dp[me, 4:5, :] = decay_grad
    chan_dp[me, 5:8, :] = jnp.zeros((3, WIDTH), jnp.float32)
    channel_copies = start_share(chan_dp, c_send, c_recv)
    send_halo.wait()
    local[ROWS - 8 : ROWS, :] = local[ROWS - 8 : ROWS, :] + halo_in[...]
    to_x[...] = local[...].astype(jnp.bfloat16)
    loads[1].wait()

    def produce(by):
        at = pl.ds(pl.multiple_of(chip_row(by, 0), 128), 128)
        total = matmul(to_x[at, :], branch_w[0]) + matmul(to_y[at, :], branch_w[1])
        partial[at, :] = total.astype(jnp.bfloat16)

    summed.start(produce)
    weight_grad(bx_grad, stage_x, [(normed_one, to_x)])
    outy_sum.middle()
    bx_sum.start()
    gate_sum.turn()
    blocks_sum.middle()
    norm_grad = summed.finish()
    before_norm, gain_part = norm_back(own[...].astype(jnp.float32), gains[0:1, :], norm_grad)
    tokens_grad[...] = (grad[...] + before_norm).astype(jnp.bfloat16)
    gain_t[index, 0:1, :] = gain_part
    gain_t[index, 1:2, :] = grad_gain_two[...]
    gain_copies = []
    for by in range(1, N_T):
        copy = remote(
            gain_t.at[index],
            gain_t.at[index],
            t_send.at[by],
            t_recv.at[by],
            {"tensor": lax.rem(index + by, N_T)},
        )
        copy.start()
        gain_copies.append(copy)
    bx_sum.middle()
    outy_sum.turn()
    blocks_sum.turn()
    for copy in gain_copies:
        copy.wait()
    total = gain_t[0]
    for by in range(1, N_T):
        total = total + gain_t[by]
    gain_dp[me] = total
    gain_copies = start_share(gain_dp, g_send, g_recv)
    gate_sum.finish(gate_share)
    bx_sum.turn()
    for copy in channel_copies + gain_copies:
        copy.wait()
    total, channels = gain_dp[0], chan_dp[0]
    for by in range(1, N_DP):
        total = total + gain_dp[by]
        channels = channels + chan_dp[by]
    gain_sum[...] = total
    channel_sum[...] = channels
    outy_sum.finish(outy_share)
    blocks_sum.finish(blocks_share)
    bx_sum.finish(bx_share)


def mixer_backward(
    rounded, normed_one, own, grad, grad_gain_two, chan, gains, flags, gates, saved, out_proj, branch_t, gate_grad
):
    f32, bf16 = jnp.float32, jnp.bfloat16
    dma = pltpu.SemaphoreType.DMA
    here = pl.BlockSpec(memory_space=pltpu.VMEM)
    there = pl.BlockSpec(memory_space=pl.ANY)
    wide_f32 = pltpu.VMEM((ROWS, WIDTH), f32)
    wide_bf16 = pltpu.VMEM((ROWS, WIDTH), bf16)
    block_bf16 = pltpu.VMEM((ROWS, BLOCK), bf16)
    longer = pltpu.VMEM((ROWS + 8, WIDTH), f32)
    return pl.pallas_call(
        backward_kernel,
        out_shape=(
            jax.ShapeDtypeStruct((OWN, D), bf16),
            jax.ShapeDtypeStruct((2, D), f32),
            jax.ShapeDtypeStruct((8, WIDTH), f32),
            jax.ShapeDtypeStruct((2 * HALF, HIDE), f32),
            jax.ShapeDtypeStruct((2 * HALF, 2 * WIDTH), f32),
            jax.ShapeDtypeStruct((2 * HALF, WIDTH), f32),
            jax.ShapeDtypeStruct((2 * GATE_HALF, 2 * WIDTH), f32),
            jax.ShapeDtypeStruct((4, 4, 2, HALF, 2 * WIDTH), bf16),
            jax.ShapeDtypeStruct((4, 4, 2, HALF, WIDTH), bf16),
        ),
        in_specs=[here] * 17 + [there] * 3,
        out_specs=tuple([here] * 7 + [there] * 2),
        scratch_shapes=[
            pltpu.VMEM((WIDTH, D), bf16),
            pltpu.VMEM((2, WIDTH, D), bf16),
            pltpu.VMEM((2, WIDTH, 2 * BLOCK), bf16),
            wide_bf16,
            wide_bf16,
            pltpu.VMEM((ROWS + 16, WIDTH), f32),
            wide_f32,
            wide_f32,
            wide_f32,
            wide_bf16,
            wide_bf16,
            pltpu.VMEM((ROWS, 2 * BLOCK), f32),
            block_bf16,
            block_bf16,
            block_bf16,
            block_bf16,
            longer,
            pltpu.VMEM((N_DP, 8, WIDTH), f32),
            pltpu.VMEM((8, WIDTH), f32),
            pltpu.VMEM((8, WIDTH), f32),
            pltpu.VMEM((4, 4, 2, GATE_HALF, 2 * WIDTH), f32),
            pltpu.VMEM((ROWS, D), bf16),
            pltpu.VMEM((2, 4, 2, HALF, 2 * WIDTH), bf16),
            pltpu.VMEM((2, 4, 2, HALF, WIDTH), bf16),
            pltpu.VMEM((N_T, 2, D), f32),
            pltpu.VMEM((N_DP, 2, D), f32),
            pltpu.VMEM((N_DP, 8, WIDTH), f32),
            dma((2,)),
            dma((2,)),
            dma((N_DP,)),
            dma((N_DP,)),
            dma((2,)),
            dma((2,)),
            dma,
            dma,
            dma((N_T,)),
            dma((N_T,)),
            dma((N_DP,)),
            dma((N_DP,)),
            dma((N_DP,)),
            dma((N_DP,)),
        ]
        + reduce_scratch()
        + data_scratch(HALF, HIDE, bf16)
        + data_scratch(HALF, 2 * WIDTH, bf16)
        + data_scratch(HALF, WIDTH, bf16)
        + data_scratch(GATE_HALF, 2 * WIDTH, f32),
        compiler_params=params(3),
    )(
        rounded, normed_one, own, grad, grad_gain_two, chan, gains, flags, gates, *saved, out_proj, branch_t, gate_grad
    )


def rms_norm(values, gain):
    return values * lax.rsqrt(jnp.mean(values * values, axis=-1, keepdims=True) + NORM_EPS) * gain


def matmul(left, right):
    return jnp.dot(left, right, preferred_element_type=jnp.float32)


def times_transposed(left, right):
    return lax.dot_general(
        left, right, (((1,), (1,)), ((), ())), preferred_element_type=jnp.float32
    )


def transposed_times(left, right):
    return lax.dot_general(
        left, right, (((0,), (0,)), ((), ())), preferred_element_type=jnp.float32
    )


def adam_step(weight, grad, first, second, rate, decay):
    first_new = BETA_ONE * first + (1.0 - BETA_ONE) * grad
    second_new = BETA_TWO * second + (1.0 - BETA_TWO) * grad * grad
    first_hat = first_new / (1.0 - BETA_ONE**STEP)
    second_hat = second_new / (1.0 - BETA_TWO**STEP)
    weight_new = weight - rate * (first_hat / (jnp.sqrt(second_hat) + ADAM_EPS) + decay * weight)
    return (first_new, second_new, weight_new)


def owned_slice(weight, data_index, count):
    share = weight.shape[1] // count
    return lax.dynamic_slice_in_dim(weight, data_index * share, share, 1).astype(jnp.float32)


def shards(
    tokens,
    cotangent,
    segments,
    gains,
    channel_params,
    branch_in,
    gate_blocks,
    out_proj,
    ffn_in,
    ffn_down,
    gains_first,
    gains_second,
    channel_first,
    channel_second,
    branch_first,
    branch_second,
    gate_first,
    gate_second,
    out_first,
    out_second,
    ffn_in_first,
    ffn_in_second,
    down_first,
    down_second,
):
    rows = ROWS
    data_index = lax.axis_index("dp")
    tensor_index = lax.axis_index("tensor")

    def own_rows(values):
        return lax.dynamic_slice_in_dim(values, tensor_index * OWN, OWN, 0)

    padded_ids = jnp.concatenate([jnp.full((3,), -1, jnp.int32), segments])
    local_ids = lax.dynamic_slice_in_dim(padded_ids, data_index * rows, rows + 3)
    marks = [local_ids[3 - tap : 3 - tap + rows] == local_ids[3:] for tap in range(4)]
    marks.append(local_ids[3:] != local_ids[2 : 2 + rows])
    flags = jnp.pad(jnp.stack(marks, 1).astype(jnp.float32), ((0, 8), (0, 3)))
    decay_param = channel_params[4:5]
    chan = jnp.concatenate(
        [channel_params, jax.nn.softplus(decay_param), jax.nn.sigmoid(decay_param), decay_param], 0
    )
    tokens_own, cotangent_own = own_rows(tokens), own_rows(cotangent)
    branch_t = branch_in.swapaxes(1, 2)
    gates_t = gate_blocks.swapaxes(1, 2)
    ffn_t = ffn_in.swapaxes(1, 2).reshape(2 * HIDE, D)
    residual_own, normed_two, normed_one, *saved = mixer_forward(
        tokens, tokens_own, branch_t, gates_t, out_proj, chan, gains, flags
    )
    block_out, residual_grad, gain_two_part, rounded, gate_grad, _, _, down_share, up_share = ffn_middle(
        normed_two, residual_own, cotangent, cotangent_own, gains, ffn_t, ffn_down
    )
    tokens_grad, gain_grad, channel_grad, ffn_gate_share, outy_share, bx_share, blocks_share, _, _ = (
        mixer_backward(
            rounded,
            normed_one,
            tokens_own,
            residual_grad,
            gain_two_part,
            chan,
            gains,
            flags,
            gates_t,
            saved,
            out_proj,
            branch_t,
            gate_grad,
        )
    )
    channel_rate = jnp.array([1.0, 1.0, 1.0, 1.0, 3.0], jnp.float32)[:, None]
    gains_out = adam_step(gains, gain_grad, gains_first, gains_second, 1.0, 0.0)
    channel_out = adam_step(
        channel_params, channel_grad[:5], channel_first, channel_second, channel_rate, 0.0
    )
    branch_out = adam_step(
        owned_slice(branch_in, data_index, N_DP),
        jnp.stack([bx_share, outy_share[:, WIDTH:]]),
        branch_first,
        branch_second,
        3.0 * D ** (-0.5),
        0.1,
    )
    gate_out = adam_step(
        owned_slice(gate_blocks, data_index, N_DP),
        jnp.stack([blocks_share[:, :WIDTH], blocks_share[:, WIDTH:]]),
        gate_first,
        gate_second,
        3.0 * BLOCK ** (-0.5),
        0.1,
    )
    proj_out = adam_step(
        owned_slice(out_proj, data_index, N_DP).T,
        outy_share[:, :WIDTH],
        out_first.T,
        out_second.T,
        3.0 * (L // 8) ** (-0.5),
        0.1,
    )
    ffn_out = adam_step(
        owned_slice(ffn_in, data_index, N_DP),
        jnp.stack([ffn_gate_share, up_share]),
        ffn_in_first,
        ffn_in_second,
        3.0 * D ** (-0.5),
        0.1,
    )
    down_out = adam_step(
        owned_slice(ffn_down, data_index, N_DP).T,
        down_share,
        down_first.T,
        down_second.T,
        3.0 * (F // 2) ** (-0.5),
        0.1,
    )
    return (
        block_out,
        tokens_grad,
        *gains_out,
        *channel_out,
        *branch_out,
        *gate_out,
        *(value.T for value in proj_out),
        *ffn_out,
        *(value.T for value in down_out),
    )


def solution(mesh):
    weights = [
        P(None, None, "tensor"),
        P(None, None, "tensor"),
        P("tensor", None),
        P(None, None, "tensor"),
        P("tensor", None),
    ]
    owned = [
        P(None, "dp", "tensor"),
        P(None, "dp", "tensor"),
        P("tensor", "dp"),
        P(None, "dp", "tensor"),
        P("tensor", "dp"),
    ]
    moments = [P(), P(None, "tensor")] + owned
    placed = [P("dp", None), P("dp", None), P(), P(), P(None, "tensor")] + weights
    for spec in moments:
        placed += [spec, spec]
    outs = [P(("dp", "tensor"), None)] * 2
    for spec in moments:
        outs += [spec, spec, spec]
    return jax.shard_map(
        shards, mesh=mesh, in_specs=tuple(placed), out_specs=tuple(outs), check_vma=False
    )
```

```python
import functools

import jax
import jax.numpy as jnp
from jax import lax
from jax.experimental import pallas as pl
from jax.experimental.pallas import tpu as pltpu
from jax.sharding import PartitionSpec as P

D = 2560
L = 2560
BLOCK = 256
F = 7680
STEP = 10
N_DP = 16
N_T = 8
ROWS = 512
OWN = ROWS // N_T
WIDTH = L // N_T
HIDE = F // N_T
HALF = 80
GATE_HALF = 8
MESH = pl.DeviceIdType.MESH

NORM_EPS = 1e-06
ADAM_EPS = 1e-08
BETA_ONE = 0.9
BETA_TWO = 0.95


def params(cid):
    return pltpu.CompilerParams(
        collective_id=cid, has_side_effects=True, vmem_limit_bytes=63 * 2**20
    )


def vmem(count):
    return [pl.BlockSpec(memory_space=pltpu.VMEM)] * count


def announce(peers):
    barrier = pltpu.get_barrier_semaphore()
    for peer in peers:
        pl.semaphore_signal(barrier, inc=1, device_id=peer, device_id_type=MESH)
    return lambda: pl.semaphore_wait(barrier, len(peers))


def remote(source, target, send_sem, recv_sem, peer):
    return pltpu.make_async_remote_copy(
        src_ref=source,
        dst_ref=target,
        send_sem=send_sem,
        recv_sem=recv_sem,
        device_id=peer,
        device_id_type=MESH,
    )


def place():
    index = lax.axis_index("tensor")
    return index // 2, lax.rem(index, 2)


def at_x(x, core, by):
    return {"tensor": lax.rem(x + by, 4) * 2 + core}


def tensor_peers():
    x, core = place()
    return [{"tensor": x * 2 + 1 - core}] + [at_x(x, core, by) for by in (1, 2, 3)]


def chip_row(by, which):
    x, _ = place()
    return pl.multiple_of((lax.rem(x + by, 4) * 2 + which) * OWN, OWN)


ARRIVAL = {0: 0, 1: 1, 3: 2, 2: 3}


def arrival_row(by, which):
    return pl.multiple_of((ARRIVAL[by % 4] * 2 + which) * OWN, OWN)


class TensorSum:
    ORDER = (2, 1, 3, 0)

    def __init__(self, row, partial, pair, held, landed, pair_send, pair_recv, x_send, x_recv):
        self.row = row
        self.partial, self.pair, self.held, self.landed = partial, pair, held, landed
        self.sems = pair_send, pair_recv, x_send, x_recv
        self.pair_copies, self.x_copies = {}, {}

    def give(self, by):
        x, core = place()
        copy = remote(
            self.partial.at[pl.ds(self.row(by, 1 - core), OWN)],
            self.pair.at[by],
            self.sems[0].at[by],
            self.sems[1].at[by],
            {"tensor": x * 2 + 1 - core},
        )
        copy.start()
        self.pair_copies[by] = copy

    def pass_on(self, by):
        x, core = place()
        self.pair_copies[by].wait_recv()
        mine = self.partial[pl.ds(self.row(by, core), OWN), :].astype(jnp.float32)
        self.held[by - 1] = (mine + self.pair[by].astype(jnp.float32)).astype(jnp.bfloat16)
        copy = remote(
            self.held.at[by - 1],
            self.landed.at[by - 1],
            self.sems[2].at[by - 1],
            self.sems[3].at[by - 1],
            at_x(x, core, by),
        )
        copy.start()
        self.x_copies[by] = copy

    def start(self, produce):
        for step, by in enumerate(self.ORDER):
            produce(by)
            self.give(by)
            if step:
                self.pass_on(self.ORDER[step - 1])

    def finish(self):
        _, core = place()
        self.pair_copies[0].wait_recv()
        total = self.partial[pl.ds(self.row(0, core), OWN), :].astype(jnp.float32)
        total = total + self.pair[0].astype(jnp.float32)
        for by in (1, 3, 2):
            self.x_copies[by].wait_recv()
            total = total + self.landed[by - 1].astype(jnp.float32)
        for by in self.ORDER:
            self.pair_copies[by].wait_send()
        for by in (2, 1, 3):
            self.x_copies[by].wait_send()
        return total


def reduce_scratch():
    return [
        pltpu.VMEM((4, OWN, D), jnp.bfloat16),
        pltpu.VMEM((3, OWN, D), jnp.bfloat16),
        pltpu.VMEM((3, OWN, D), jnp.bfloat16),
        pltpu.SemaphoreType.DMA((4,)),
        pltpu.SemaphoreType.DMA((4,)),
        pltpu.SemaphoreType.DMA((3,)),
        pltpu.SemaphoreType.DMA((3,)),
    ]


class TensorGather:
    def __init__(self, row, whole, x_send, x_recv, pair_send, pair_recv):
        self.row, self.whole, self.sems = row, whole, (x_send, x_recv, pair_send, pair_recv)

    def at(self, by):
        _, core = place()
        return self.whole.at[pl.ds(self.row(by, core), OWN)]

    def start(self, block):
        x, core = place()
        self.whole[pl.ds(self.row(0, core), OWN), :] = block
        mine = self.at(0)
        self.sends, self.pairs = [], {}
        for by in (1, 3, 2):
            target = mine if self.row is chip_row else self.at(4 - by)
            copy = remote(
                mine, target, self.sems[0].at[by - 1], self.sems[1].at[by - 1], at_x(x, core, by)
            )
            copy.start()
            self.sends.append(copy)
        self.hand(0)

    def hand(self, by):
        x, core = place()
        block = self.at(by)
        copy = remote(
            block,
            block,
            self.sems[2].at[by],
            self.sems[3].at[by],
            {"tensor": x * 2 + 1 - core},
        )
        copy.start()
        self.pairs[by] = copy

    def arrive(self, by):
        x, core = place()
        sender = 4 - by
        block = self.at(by)
        remote(
            block,
            block,
            self.sems[0].at[sender - 1],
            self.sems[1].at[sender - 1],
            at_x(x, core, sender),
        ).wait_recv()
        self.hand(by)

    def settle(self, by):
        self.pairs[by].wait_recv()

    def finish(self):
        for copy in self.sends:
            copy.wait_send()
        for copy in self.pairs.values():
            copy.wait_send()


class DataSum:
    LOW, HIGH = pl.ds(0, 2), pl.ds(2, 2)

    def __init__(self, grad, own, near, via, ring, last, send, recv, local, rows):
        self.grad, self.own, self.near, self.via = grad, own, near, via
        self.ring, self.last, self.rows = ring, last, rows
        self.send, self.recv, self.local = send, recv, local
        me = lax.axis_index("dp")
        z, y = me // 4, lax.rem(me, 4)
        self.first = (y, z)
        self.second = (z, y)

    def peer(self, half, first_by, second_by):
        a = lax.rem(self.first[half] + first_by + 4, 4)
        b = lax.rem(self.second[half] + second_by + 4, 4)
        return {"dp": b * 4 + a if half == 0 else a * 4 + b}

    def block(self, half, by, part):
        a = lax.rem(self.first[half] + by + 4, 4)
        return self.grad.at[part, a, 0] if half == 0 else self.grad.at[a, part, 1]

    def ship(self, half, slot, source, target, first_by, second_by):
        copy = remote(
            source,
            target,
            self.send.at[half, slot],
            self.recv.at[half, slot],
            self.peer(half, first_by, second_by),
        )
        copy.start()
        self.copies[half, slot] = copy

    def start(self):
        self.copies, self.locals = {}, {}
        for half in (0, 1):
            self.ship(half, 0, self.block(half, 2, self.LOW), self.via.at[half, 0], 1, 0)
            self.ship(half, 1, self.block(half, 2, self.HIGH), self.via.at[half, 1], -1, 0)
            pairs = (
                (self.block(half, 1, self.LOW), self.near.at[half, 0]),
                (self.block(half, -1, self.HIGH), self.near.at[half, 1]),
                (self.block(half, 0, pl.ds(0, 4)), self.own.at[half]),
            )
            for number, (source, target) in enumerate(pairs):
                copy = pltpu.make_async_copy(source, target, self.local.at[half, number])
                copy.start()
                self.locals[half, number] = copy
        for half in (0, 1):
            self.ship(half, 2, self.block(half, 1, self.HIGH), self.ring.at[half, 0], 1, 0)
            self.ship(half, 3, self.block(half, -1, self.LOW), self.ring.at[half, 1], -1, 0)

    def add(self, target, sources, blocks):
        size = 16 if self.rows % 16 == 0 else 8
        steps = self.rows // size

        def body(index, _):
            block = index // steps
            at = pl.ds(pl.multiple_of(lax.rem(index, steps) * size, size), size)
            total = target[block, at, :].astype(jnp.float32)
            for source in sources:
                total = total + source[block, at, :].astype(jnp.float32)
            target[block, at, :] = total.astype(target.dtype)
            return 0

        lax.fori_loop(0, blocks * steps, body, 0)

    def middle(self):
        for half in (0, 1):
            for side in (0, 1):
                self.locals[half, side].wait()
                self.copies[half, side].wait_recv()
                self.add(self.near.at[half, side], [self.via.at[half, side]], 2)
                self.ship(
                    half,
                    4 + side,
                    self.near.at[half, side],
                    self.ring.at[half, 2 + side],
                    1 - 2 * side,
                    0,
                )

    def turn(self):
        for half in (0, 1):
            self.locals[half, 2].wait()
            for slot in (2, 3, 4, 5):
                self.copies[half, slot].wait_recv()
            ring = self.ring
            self.add(self.own.at[half, self.LOW], [ring.at[half, 1], ring.at[half, 2]], 2)
            self.add(self.own.at[half, self.HIGH], [ring.at[half, 0], ring.at[half, 3]], 2)
            for by in (1, 2, 3):
                to = lax.rem(self.second[half] + by, 4)
                self.ship(
                    half, 5 + by, self.own.at[half, to], self.last.at[half, by - 1], 0, by
                )

    def finish(self, share):
        size = 16 if self.rows % 16 == 0 else 8
        for half in (0, 1):
            for by in (1, 2, 3):
                self.copies[half, 5 + by].wait_recv()

            def body(index, _, half=half):
                at = pl.ds(pl.multiple_of(index * size, size), size)
                total = self.own[half, self.second[half], at, :].astype(jnp.float32)
                for by in range(3):
                    total = total + self.last[half, by, at, :].astype(jnp.float32)
                share[pl.ds(pl.multiple_of(half * self.rows + index * size, size), size), :] = total
                return 0

            lax.fori_loop(0, self.rows // size, body, 0)
        for copy in self.copies.values():
            copy.wait_send()


def data_scratch(rows, columns, dtype):
    dma = pltpu.SemaphoreType.DMA
    return [
        pltpu.VMEM((2, 4, rows, columns), dtype),
        pltpu.VMEM((2, 2, 2, rows, columns), dtype),
        pltpu.VMEM((2, 2, 2, rows, columns), dtype),
        pltpu.VMEM((2, 4, 2, rows, columns), dtype),
        pltpu.VMEM((2, 3, rows, columns), dtype),
        dma((2, 9)),
        dma((2, 9)),
        dma((2, 3)),
    ]


def gather_scratch():
    return [
        pltpu.SemaphoreType.DMA((3,)),
        pltpu.SemaphoreType.DMA((3,)),
        pltpu.SemaphoreType.DMA((4,)),
        pltpu.SemaphoreType.DMA((4,)),
    ]


def dp_peers():
    me = lax.axis_index("dp")
    return [{"dp": lax.rem(me + by, N_DP)} for by in range(1, N_DP)]


def place_matrix(shift):
    row = lax.broadcasted_iota(jnp.int32, (WIDTH, 2 * BLOCK), 0)
    lane = lax.broadcasted_iota(jnp.int32, (WIDTH, 2 * BLOCK), 1)
    return jnp.where(lane == row + shift, 1.0, 0.0).astype(jnp.bfloat16)


def wide_gates(gates, wide, shift):
    row = lax.broadcasted_iota(jnp.int32, (WIDTH, BLOCK), 0)
    low = row + shift < BLOCK
    for gate in range(2):
        matrix = gates[gate].astype(jnp.float32)
        wide[gate, :, 0:BLOCK] = jnp.where(low, matrix, 0.0).astype(jnp.bfloat16)
        wide[gate, :, BLOCK : 2 * BLOCK] = jnp.where(low, 0.0, matrix).astype(jnp.bfloat16)


def one_less_exp(z):
    series = 1.0 + z / 7.0
    for term in (6.0, 5.0, 4.0, 3.0, 2.0):
        series = 1.0 + z / term * series
    return jnp.where(z > -0.35, -z * series, 1.0 - jnp.exp(z))


def tiles(count, size, body, unroll=1):
    def step(index, _):
        body(pl.multiple_of(index * size, size))
        return 0

    lax.fori_loop(0, count, step, 0, unroll=unroll)


def norm_rows(source, target, gain, rows):
    def body(first):
        at = pl.ds(first, 16)
        target[at, :] = rms_norm(source[at, :].astype(jnp.float32), gain).astype(jnp.bfloat16)

    tiles(rows // 16, 16, body, min(4, rows // 16))


def shifted(values, by, fill, reverse):
    count = values.shape[0]
    row = lax.broadcasted_iota(jnp.int32, values.shape, 0)
    if reverse:
        return jnp.where(row < count - by, pltpu.roll(values, count - by, 0), fill)
    return jnp.where(row >= by, pltpu.roll(values, by, 0), fill)


def local_scan(factor_at, term_at, values, prods, reverse):
    def step(index, held):
        prod, value = held
        first = pl.multiple_of((ROWS // 8 - 1 - index if reverse else index) * 8, 8)
        factor, term = factor_at(first), term_at(first)
        for by in (1, 2, 4):
            term = term + factor * shifted(term, by, 0.0, reverse)
            factor = factor * shifted(factor, by, 1.0, reverse)
        value = factor * value + term
        prod = factor * prod
        values[pl.ds(first, 8), :] = value
        prods[pl.ds(first, 8), :] = prod
        last = 0 if reverse else 7
        return (
            jnp.broadcast_to(prod[last : last + 1], prod.shape),
            jnp.broadcast_to(value[last : last + 1], value.shape),
        )

    ones = jnp.ones((8, WIDTH), jnp.float32)
    return lax.fori_loop(0, ROWS // 8, step, (ones, jnp.zeros_like(ones)), unroll=8)


def start_share(slots, send, recv):
    me = lax.axis_index("dp")
    copies = []
    for by in range(1, N_DP):
        copy = remote(
            slots.at[me], slots.at[me], send.at[by], recv.at[by], {"dp": lax.rem(me + by, N_DP)}
        )
        copy.start()
        copies.append(copy)
    return copies


def beside_peers():
    index = lax.axis_index("tensor")
    return {"tensor": lax.rem(index + 1, N_T)}, {"tensor": lax.rem(index + N_T - 1, N_T)}


def far_peer():
    index = lax.axis_index("tensor")
    _, core = place()
    return {"tensor": lax.rem(index + N_T - 1 + 2 * core, N_T)}


def gelu_parts(y):
    c = 0.7978845608028654
    inner = jnp.tanh(c * (y + 0.044715 * y * y * y))
    half = 0.5 * (1.0 + inner)
    slope = half + 0.5 * y * (1.0 - inner * inner) * c * (1.0 + 3 * 0.044715 * y * y)
    return y * half, slope


def forward_kernel(
    tokens, branch_hbm, gates, out_hbm, chan, gains, flags, residual, block, *rest
):
    outs = rest[:9]
    (
        normed_one, ext, window, pre_a, pre_x, carry, state, branch_y, mixed,
        branch_w, out_w, halo, halo_norm, wide, placing, update, values, prods, gelu_y, low, high, slots, partial,
        load_sem, store_sem, halo_send, halo_recv, side_send, side_recv, slot_send, slot_recv, *scratch
    ) = rest[9:]
    me, index = lax.axis_index("dp"), lax.axis_index("tensor")
    shift = lax.rem(index * WIDTH, BLOCK)
    loads = [
        pltpu.make_async_copy(branch_hbm.at[0], branch_w.at[0], load_sem.at[0]),
        pltpu.make_async_copy(branch_hbm.at[1], branch_w.at[1], load_sem.at[1]),
        pltpu.make_async_copy(out_hbm, out_w, load_sem.at[2]),
    ]
    for load in loads:
        load.start()
    ready = announce(dp_peers() + tensor_peers() + [far_peer()])
    stores = []

    def store(number, source, target):
        copy = pltpu.make_async_copy(source, target, store_sem.at[number])
        copy.start()
        stores.append(copy)

    send_halo = remote(
        tokens.at[pl.ds(ROWS - 16, 16)],
        halo,
        halo_send,
        halo_recv,
        {"dp": lax.rem(me + 1, N_DP)},
    )
    wide_gates(gates, wide, shift)
    placing[...] = place_matrix(shift)
    gain = gains[0:1, :]
    norm_rows(tokens, normed_one, gain, ROWS)
    ready()
    send_halo.start()
    store(0, normed_one, outs[0])
    loads[0].wait()

    def branch_tile(first):
        at = pl.ds(first, 128)
        value = times_transposed(normed_one[at, :], branch_w[0])
        ext[pl.ds(first + 16, 128), :] = value.astype(jnp.bfloat16).astype(jnp.float32)

    tiles(4, 128, branch_tile)
    send_halo.wait()
    norm_rows(halo, halo_norm, gain, 16)
    ext[0:16, :] = times_transposed(halo_norm[...], branch_w[0]).astype(jnp.bfloat16).astype(jnp.float32)

    def conv_tile(first):
        near = ext[pl.ds(first + 8, 136), :]
        total = chan[0:1, :] * near[8:]
        for tap in range(1, 4):
            counted = flags[pl.ds(first, 128), tap : tap + 1] > 0.0
            total = total + chan[tap : tap + 1, :] * jnp.where(counted, near[8 - tap : 136 - tap], 0.0)
        window[pl.ds(first, 128), :] = matmul(total.astype(jnp.bfloat16), placing[...]).astype(
            jnp.bfloat16
        )

    tiles(4, 128, conv_tile)
    store(1, ext, outs[1])
    up, down = beside_peers()
    to_up = remote(
        window.at[:, pl.ds(BLOCK, BLOCK)], low, side_send.at[0], side_recv.at[0], up
    )
    to_down = remote(window.at[:, pl.ds(0, BLOCK)], high, side_send.at[1], side_recv.at[1], down)
    to_up.start()
    to_down.start()
    loads[1].wait()

    def gelu_tile(first):
        at = pl.ds(first, 128)
        branch_y[at, :] = times_transposed(normed_one[at, :], branch_w[1])

    tiles(4, 128, gelu_tile)
    store(2, branch_y, outs[6])
    to_up.wait()
    to_down.wait()

    def window_tile(first):
        at = pl.ds(first, 128)
        own_conv = lax.dot_general(
            window[at, :], placing[...], (((1,), (1,)), ((), ())), preferred_element_type=jnp.float32
        )
        from_low = jnp.where(shift != 0, low[at, :].astype(jnp.float32), 0.0)
        from_high = jnp.where(shift != 192, high[at, :].astype(jnp.float32), 0.0)
        whole = window[at, :].astype(jnp.float32) + jnp.concatenate([from_low, from_high], 1)
        whole = whole.astype(jnp.bfloat16)
        window[at, :] = whole
        a = times_transposed(whole, wide[0])
        x = times_transposed(whole, wide[1])
        pre_a[at, :] = a
        pre_x[at, :] = x
        reset = flags[at, 4:5] > 0.0
        log_a = -8.0 * jax.nn.sigmoid(a) * chan[5:6, :]
        carry[at, :] = jnp.where(reset, 0.0, jnp.exp(log_a))
        scale = jnp.where(reset, 1.0, jnp.sqrt(one_less_exp(2.0 * log_a)))
        update[at, :] = own_conv * jax.nn.sigmoid(x) * scale

    tiles(4, 128, window_tile)
    store(3, window, outs[2])
    store(4, pre_a, outs[3])
    store(5, pre_x, outs[4])
    carry[ROWS : ROWS + 8, :] = jnp.ones((8, WIDTH), jnp.float32)
    store(6, carry, outs[5])
    prod, value = local_scan(
        lambda first: carry[pl.ds(first, 8), :],
        lambda first: update[pl.ds(first, 8), :],
        values,
        prods,
        False,
    )
    slots[me, 0:1, :] = prod[0:1]
    slots[me, 1:2, :] = value[0:1]
    copies = start_share(slots, slot_send, slot_recv)

    def activate(first):
        at = pl.ds(first, 64)
        y = branch_y[at, :]
        gelu_y[at, :] = gelu_parts(y)[0]

    tiles(8, 64, activate)
    for copy in copies:
        copy.wait()
    before = jnp.zeros((1, WIDTH), jnp.float32)
    for place_at in range(N_DP - 1):
        longer = slots[place_at, 0:1, :] * before + slots[place_at, 1:2, :]
        before = jnp.where(place_at < me, longer, before)

    state[0:8, :] = jnp.broadcast_to(before, (8, WIDTH))

    def finish(first):
        at = pl.ds(first, 64)
        total = values[at, :] + prods[at, :] * before
        state[pl.ds(first + 8, 64), :] = total
        mixed[at, :] = (total * gelu_y[at, :]).astype(jnp.bfloat16)

    tiles(8, 64, finish)
    store(7, state, outs[7])
    store(8, mixed, outs[8])
    loads[2].wait()

    def produce(by):
        at = pl.ds(pl.multiple_of(chip_row(by, 0), 128), 128)
        partial[at, :] = matmul(mixed[at, :], out_w[...]).astype(jnp.bfloat16)

    summed = TensorSum(chip_row, partial, *scratch)
    summed.start(produce)
    _, core = place()
    total = tokens[pl.ds(chip_row(0, core), OWN), :].astype(jnp.float32) + summed.finish()
    residual[...] = total
    block[...] = rms_norm(total, gains[1:2, :]).astype(jnp.bfloat16)
    for copy in stores:
        copy.wait()


def saved_shapes():
    f32, bf16 = jnp.float32, jnp.bfloat16
    return (
        ((ROWS, D), bf16),
        ((ROWS + 16, WIDTH), f32),
        ((ROWS, 2 * BLOCK), bf16),
        ((ROWS, WIDTH), f32),
        ((ROWS, WIDTH), f32),
        ((ROWS + 8, WIDTH), f32),
        ((ROWS, WIDTH), f32),
        ((ROWS + 8, WIDTH), f32),
        ((ROWS, WIDTH), bf16),
    )


def mixer_forward(tokens, branch_in, gate_blocks, out_proj, chan, gains, flags):
    f32, bf16 = jnp.float32, jnp.bfloat16
    dma = pltpu.SemaphoreType.DMA
    here = pl.BlockSpec(memory_space=pltpu.VMEM)
    there = pl.BlockSpec(memory_space=pl.ANY)
    shapes = saved_shapes()
    inside = shapes[:6] + (shapes[7], shapes[6], shapes[8])
    return pl.pallas_call(
        forward_kernel,
        out_shape=(
            jax.ShapeDtypeStruct((OWN, D), f32),
            jax.ShapeDtypeStruct((OWN, D), bf16),
            *(jax.ShapeDtypeStruct(*shape) for shape in shapes),
        ),
        in_specs=[here, there, here, there, here, here, here],
        out_specs=tuple([here] * 2 + [there] * 9),
        scratch_shapes=[pltpu.VMEM(*shape) for shape in inside]
        + [
            pltpu.VMEM((2, WIDTH, D), bf16),
            pltpu.VMEM((WIDTH, D), bf16),
            pltpu.VMEM((16, D), bf16),
            pltpu.VMEM((16, D), bf16),
            pltpu.VMEM((2, WIDTH, 2 * BLOCK), bf16),
            pltpu.VMEM((WIDTH, 2 * BLOCK), bf16),
            pltpu.VMEM((ROWS, WIDTH), f32),
            pltpu.VMEM((ROWS, WIDTH), f32),
            pltpu.VMEM((ROWS, WIDTH), f32),
            pltpu.VMEM((ROWS, WIDTH), f32),
            pltpu.VMEM((ROWS, BLOCK), bf16),
            pltpu.VMEM((ROWS, BLOCK), bf16),
            pltpu.VMEM((N_DP, 8, WIDTH), f32),
            pltpu.VMEM((ROWS, D), bf16),
            dma((3,)),
            dma((9,)),
            dma,
            dma,
            dma((2,)),
            dma((2,)),
            dma((N_DP,)),
            dma((N_DP,)),
        ]
        + reduce_scratch(),
        compiler_params=params(1),
    )(tokens, branch_in, gate_blocks, out_proj, chan, gains, flags)


def norm_back(value, gain, grad):
    scale = lax.rsqrt(jnp.mean(value * value, axis=-1, keepdims=True) + NORM_EPS)
    unit = value * scale
    scaled = grad * gain
    back = scale * (scaled - unit * jnp.mean(scaled * unit, axis=-1, keepdims=True))
    return back, jnp.sum(grad * unit, axis=0, keepdims=True)


def middle_kernel(
    block, residual, dy_hbm, gains, ffn_hbm, down_hbm,
    grad, grad_gain, rounded, gate_grad, up_grad, down_grad, out_partial, down_share,
    normed, dy, ffn_w, down_w, hidden, to_gate, to_up, gate_pre, up_pre, grad_hidden, partial, stage,
    load_sem, stage_sem, *scratch
):
    x, core = place()
    loads = []

    def load(source, target):
        copy = pltpu.make_async_copy(source, target, load_sem.at[len(loads)])
        copy.start()
        loads.append(copy)

    for by, spot in ARRIVAL.items():
        load(
            dy_hbm.at[pl.ds(pl.multiple_of(lax.rem(x + by, 4) * 128, 128), 128)],
            dy.at[pl.ds(spot * 128, 128)],
        )
    load(down_hbm, down_w)
    load(ffn_hbm.at[pl.ds(0, HIDE)], ffn_w.at[pl.ds(0, HIDE)])
    load(ffn_hbm.at[pl.ds(HIDE, HIDE)], ffn_w.at[pl.ds(HIDE, HIDE)])
    ready = announce(dp_peers() + tensor_peers())
    before = TensorGather(arrival_row, normed, *scratch[:4])
    after = TensorGather(chip_row, rounded, *scratch[4:8])
    summed = TensorSum(arrival_row, partial, *scratch[8:15])
    down_sum = DataSum(down_grad, *scratch[15:23], HALF)
    pieces = ((0, 384), (384, 384), (768, 192))
    ready()
    before.start(block[...])
    for copy in loads[:5]:
        copy.wait()
    for start, size in pieces:
        units = pl.ds(start, size)
        grad_hidden[:, units] = times_transposed(dy[...], down_w[units, :])
    for copy in loads[5:]:
        copy.wait()
    before.arrive(1)
    before.settle(0)
    before.settle(1)
    for group in range(2):
        if group:
            before.arrive(3)
            before.arrive(2)
            before.settle(3)
            before.settle(2)
        rows = pl.ds(group * 256, 256)
        for start, size in pieces:
            units = pl.ds(start, size)
            gate_pre[:, 0:size] = times_transposed(normed[rows, :], ffn_w[units, :])
            up_pre[:, 0:size] = times_transposed(normed[rows, :], ffn_w[pl.ds(HIDE + start, size), :])

            def activate(first, units=units, size=size, group=group):
                here = pl.ds(first, 32)
                at = pl.ds(pl.multiple_of(group * 256 + first, 32), 32)
                value, slope = gelu_parts(gate_pre[here, 0:size])
                up, back = up_pre[here, 0:size], grad_hidden[at, units]
                hidden[at, units] = (value * up).astype(jnp.bfloat16)
                to_up[at, units] = (back * value).astype(jnp.bfloat16)
                to_gate[at, units] = (back * up * slope).astype(jnp.bfloat16)

            tiles(256 // 32, 32, activate)
    before.finish()

    def produce(by):
        at = pl.ds(arrival_row(by, 0), 128)
        total = matmul(to_gate[at, :], ffn_w[0:HIDE, :]) + matmul(
            to_up[at, :], ffn_w[HIDE : 2 * HIDE, :]
        )
        partial[at, :] = total.astype(jnp.bfloat16)

    summed.start(produce)

    def weight_grad(jobs):
        pending = {}
        for z in range(4):
            columns = pl.ds(z * 640, 640)
            for job, (left, right, target) in enumerate(jobs):
                slot = (z * len(jobs) + job) % 2
                if slot in pending:
                    pending[slot].wait()
                value = transposed_times(left[:, columns], right[...]).astype(jnp.bfloat16)
                stage[slot] = value.reshape(4, 2, HALF, HIDE)
                copy = pltpu.make_async_copy(stage.at[slot], target.at[z], stage_sem.at[slot])
                copy.start()
                pending[slot] = copy
        for copy in pending.values():
            copy.wait()

    weight_grad([(dy, hidden, down_grad)])
    down_sum.start()
    weight_grad([(normed, to_up, up_grad)])
    down_sum.middle()
    norm_grad = summed.finish()
    back, gain_part = norm_back(residual[...], gains[1:2, :], norm_grad)
    back = back + dy[pl.ds(arrival_row(0, core), OWN), :].astype(jnp.float32)
    grad[...] = back
    grad_gain[...] = gain_part
    after.start(back.astype(jnp.bfloat16))

    def produce_out(first):
        at = pl.ds(first, 128)
        partial[at, :] = matmul(hidden[at, :], down_w[...]).astype(jnp.bfloat16)

    tiles(4, 128, produce_out)
    keep = pltpu.make_async_copy(partial, out_partial, load_sem.at[0])
    keep.start()
    weight_grad([(normed, to_gate, gate_grad)])
    for by in (1, 3):
        after.arrive(by)
    down_sum.turn()
    after.arrive(2)
    for by in (0, 1, 3, 2):
        after.settle(by)
    after.finish()
    keep.wait()
    down_sum.finish(down_share)


def ffn_middle(block, residual, dy, gains, ffn_t, down):
    f32, bf16 = jnp.float32, jnp.bfloat16
    dma = pltpu.SemaphoreType.DMA
    here = pl.BlockSpec(memory_space=pltpu.VMEM)
    there = pl.BlockSpec(memory_space=pl.ANY)
    shared = jax.ShapeDtypeStruct((4, 4, 2, HALF, HIDE), bf16)
    share = jax.ShapeDtypeStruct((2 * HALF, HIDE), f32)
    return pl.pallas_call(
        middle_kernel,
        out_shape=(
            jax.ShapeDtypeStruct((OWN, D), f32),
            jax.ShapeDtypeStruct((1, D), f32),
            jax.ShapeDtypeStruct((ROWS, D), bf16),
            shared,
            shared,
            shared,
            jax.ShapeDtypeStruct((ROWS, D), bf16),
            share,
        ),
        in_specs=[here, here, there, here, there, there],
        out_specs=tuple([here] * 3 + [there] * 4 + [here]),
        scratch_shapes=[
            pltpu.VMEM((ROWS, D), bf16),
            pltpu.VMEM((ROWS, D), bf16),
            pltpu.VMEM((2 * HIDE, D), bf16),
            pltpu.VMEM((HIDE, D), bf16),
            pltpu.VMEM((ROWS, HIDE), bf16),
            pltpu.VMEM((ROWS, HIDE), bf16),
            pltpu.VMEM((ROWS, HIDE), bf16),
            pltpu.VMEM((256, 384), f32),
            pltpu.VMEM((256, 384), f32),
            pltpu.VMEM((ROWS, HIDE), f32),
            pltpu.VMEM((ROWS, D), bf16),
            pltpu.VMEM((2, 4, 2, HALF, HIDE), bf16),
            dma((7,)),
            dma((2,)),
        ]
        + gather_scratch()
        + gather_scratch()
        + reduce_scratch()
        + data_scratch(HALF, HIDE, bf16),
        compiler_params=params(2),
    )(block, residual, dy, gains, ffn_t, down)


def backward_kernel(
    rounded, tokens, grad, residual, grad_gain_two, chan, gains, flags, gates,
    normed_one, ext, window, pre_a, pre_x, carry, branch_y, state, mixed,
    out_partial, out_hbm, branch_hbm, gate_grad, up_grad,
    tokens_grad, out, gain_sum, channel_sum, gate_share, up_share, outy_share, bx_share, blocks_share, outy_grad, bx_grad,
    out_w, branch_w, wide, to_y, local, sums, prods, to_a, to_gx, window_grad, low, high,
    low_in, high_in, conv_grad, slots, halo, halo_in, blocks_grad, partial, stage, own,
    gain_t, gain_dp, chan_dp,
    load_sem, stage_sem, slot_send, slot_recv, side_send, side_recv, halo_send, halo_recv,
    t_send, t_recv, g_send, g_recv, c_send, c_recv, *scratch
):
    me, index = lax.axis_index("dp"), lax.axis_index("tensor")
    shift = lax.rem(index * WIDTH, BLOCK)
    loads = [
        pltpu.make_async_copy(out_hbm, out_w, load_sem.at[0]),
        pltpu.make_async_copy(branch_hbm, branch_w, load_sem.at[1]),
        pltpu.make_async_copy(out_partial, partial, load_sem.at[2]),
        pltpu.make_async_copy(
            tokens.at[pl.ds(chip_row(0, place()[1]), OWN)], own, load_sem.at[3]
        ),
    ]
    for load in loads:
        load.start()
    ready = announce(dp_peers() + tensor_peers() + [far_peer()])
    pair, held, *others = scratch[:7]
    summed = TensorSum(chip_row, partial, pair, held, *others)
    summed_out = TensorSum(arrival_row, partial, scratch[39], held, *scratch[40:45])
    gate_sum = DataSum(gate_grad, *scratch[7:15], HALF)
    up_sum = DataSum(up_grad, *scratch[45:53], HALF)
    outy_sum = DataSum(outy_grad, *scratch[15:23], HALF)
    bx_sum = DataSum(bx_grad, *scratch[23:31], HALF)
    blocks_sum = DataSum(blocks_grad, *scratch[31:39], GATE_HALF)
    ready()
    up_sum.start()
    gate_sum.start()
    loads[2].wait()
    summed_out.start(lambda by: None)
    wide_gates(gates, wide, shift)
    loads[0].wait()

    def mixed_tile(first):
        at = pl.ds(first, 128)
        local[at, :] = times_transposed(rounded[at, :], out_w[...])

    tiles(4, 128, mixed_tile)

    def gelu_tile(first):
        at = pl.ds(first, 64)
        value, slope = gelu_parts(branch_y[at, :])
        mixed_grad = local[at, :]
        to_y[at, :] = (mixed_grad * state[pl.ds(first + 8, 64), :] * slope).astype(jnp.bfloat16)
        local[at, :] = mixed_grad * value

    tiles(8, 64, gelu_tile)
    prod, value = local_scan(
        lambda first: carry[pl.ds(first, 16), :][1:9],
        lambda first: local[pl.ds(first, 8), :],
        sums,
        prods,
        True,
    )
    slots[me, 0:1, :] = carry[0:1, :] * prod[0:1]
    slots[me, 1:2, :] = carry[0:1, :] * value[0:1]
    copies = start_share(slots, slot_send, slot_recv)

    def weight_grad(target, jobs):
        pending = {}
        for z in range(4):
            columns = pl.ds(z * 640, 640)
            if z >= 2:
                pending[z % 2].wait()
            parts = [transposed_times(left[:, columns], right[...]) for left, right in jobs]
            whole = parts[0] if len(parts) == 1 else jnp.concatenate(parts, 1)
            lanes = pl.ds(0, target.shape[4])
            stage[z % 2, :, :, :, 0 : whole.shape[1]] = whole.astype(jnp.bfloat16).reshape(
                4, 2, HALF, whole.shape[1]
            )
            copy = pltpu.make_async_copy(
                stage.at[z % 2, :, :, :, lanes], target.at[z], stage_sem.at[z % 2]
            )
            copy.start()
            pending[z % 2] = copy
        for copy in pending.values():
            copy.wait()

    weight_grad(outy_grad, [(rounded, mixed), (normed_one, to_y)])
    outy_sum.start()
    for copy in copies:
        copy.wait()
    later = jnp.zeros((1, WIDTH), jnp.float32)
    for place_at in range(N_DP - 1, 0, -1):
        longer = slots[place_at, 0:1, :] * later + slots[place_at, 1:2, :]
        later = jnp.where(place_at > me, longer, later)
    plus, decay_slope = chan[5:6, :], chan[6:7, :]
    zero_row = jnp.zeros((1, WIDTH), jnp.float32)

    def gate_tile(first, decay_grad):
        at = pl.ds(first, 64)
        total = sums[at, :] + prods[at, :] * later
        near = state[pl.ds(first, 72), :]
        conv = lax.dot_general(
            window[at, :], place_matrix(shift), (((1,), (1,)), ((), ())), preferred_element_type=jnp.float32
        )
        reset = flags[at, 4:5] > 0.0
        gate_a, gate_x = jax.nn.sigmoid(pre_a[at, :]), jax.nn.sigmoid(pre_x[at, :])
        log_a = -8.0 * gate_a * plus
        keep = jnp.exp(log_a)
        scale = jnp.sqrt(one_less_exp(2.0 * log_a))
        scale_here = jnp.where(reset, 1.0, scale)
        conv_grad[at, :] = total * gate_x * scale_here
        to_gx[at, :] = (total * conv * scale_here * gate_x * (1.0 - gate_x)).astype(jnp.bfloat16)
        log_grad = total * near[7:71] * keep - total * conv * gate_x * keep * keep / scale
        log_grad = jnp.where(reset, 0.0, log_grad)
        to_a[at, :] = (log_grad * (-8.0 * plus) * gate_a * (1.0 - gate_a)).astype(jnp.bfloat16)
        return decay_grad + jnp.sum(log_grad * (-8.0 * gate_a), axis=0, keepdims=True)

    decay_grad = lax.fori_loop(
        0, 8, lambda i, held: gate_tile(pl.multiple_of(i * 64, 64), held), zero_row
    )
    decay_grad = decay_grad * decay_slope

    def window_tile(first):
        at = pl.ds(first, 128)
        total = matmul(to_a[at, :], wide[0]) + matmul(to_gx[at, :], wide[1])
        window_grad[at, :] = total
        low[at, :] = total[:, 0:BLOCK].astype(jnp.bfloat16)
        high[at, :] = total[:, BLOCK : 2 * BLOCK].astype(jnp.bfloat16)

    tiles(4, 128, window_tile)
    up, down = beside_peers()
    to_up = remote(high, low_in, side_send.at[0], side_recv.at[0], up)
    to_down = remote(low, high_in, side_send.at[1], side_recv.at[1], down)
    to_up.start()
    to_down.start()
    column = lax.broadcasted_iota(jnp.int32, (BLOCK, WIDTH), 1)
    chosen = []
    for right in (to_a, to_gx):
        both = transposed_times(window[...], right[...])
        chosen.append(
            jnp.where(column + shift < BLOCK, both[0:BLOCK], both[BLOCK : 2 * BLOCK])
        )
    blocks_grad[...] = jnp.concatenate(chosen, 1).reshape(4, 4, 2, GATE_HALF, 2 * WIDTH)
    up_sum.middle()
    to_up.wait()
    to_down.wait()

    def conv_tile(first):
        at = pl.ds(first, 64)
        from_low = jnp.where(shift != 0, low_in[at, :].astype(jnp.float32), 0.0)
        from_high = jnp.where(shift != 192, high_in[at, :].astype(jnp.float32), 0.0)
        total = window_grad[at, :] + jnp.concatenate([from_low, from_high], 1)
        total = pltpu.roll(total, lax.rem(2 * BLOCK - shift, 2 * BLOCK), 1)
        conv_grad[at, :] = conv_grad[at, :] + total[:, 0:WIDTH]

    tiles(8, 64, conv_tile)
    conv_grad[ROWS : ROWS + 8, :] = jnp.zeros((8, WIDTH), jnp.float32)
    head = conv_grad[0:8, :]
    rows = []
    for row in range(3):
        total = zero_row
        for tap in range(3 - row, 4):
            from_row = row - 3 + tap
            counted = flags[from_row : from_row + 1, tap : tap + 1] > 0.0
            total = total + chan[tap : tap + 1, :] * jnp.where(
                counted, head[from_row : from_row + 1], 0.0
            )
        rows.append(total)
    halo[0:5, :] = jnp.zeros((5, WIDTH), jnp.float32)
    for row in range(3):
        halo[5 + row : 6 + row, :] = rows[row]
    send_halo = remote(halo, halo_in, halo_send, halo_recv, {"dp": lax.rem(me + N_DP - 1, N_DP)})
    send_halo.start()
    blocks_sum.start()

    def tap_tile(first, held):
        at = pl.ds(first, 64)
        near = conv_grad[pl.ds(first, 72), :]
        marks = flags[pl.ds(first, 72), :]
        behind = ext[pl.ds(first + 8, 72), :]
        total = chan[0:1, :] * near[0:64]
        taps = [held[0] + jnp.sum(near[0:64] * behind[8:72], axis=0, keepdims=True)]
        for tap in range(1, 4):
            counted = marks[tap : tap + 64, tap : tap + 1] > 0.0
            total = total + chan[tap : tap + 1, :] * jnp.where(counted, near[tap : tap + 64], 0.0)
            here = jnp.where(marks[0:64, tap : tap + 1] > 0.0, near[0:64], 0.0)
            taps.append(
                held[tap] + jnp.sum(here * behind[8 - tap : 72 - tap], axis=0, keepdims=True)
            )
        local[at, :] = total
        return tuple(taps)

    tap_grads = lax.fori_loop(
        0, 8, lambda i, held: tap_tile(pl.multiple_of(i * 64, 64), held), (zero_row,) * 4
    )
    for tap in range(4):
        chan_dp[me, tap : tap + 1, :] = tap_grads[tap]
    chan_dp[me, 4:5, :] = decay_grad
    chan_dp[me, 5:8, :] = jnp.zeros((3, WIDTH), jnp.float32)
    channel_copies = start_share(chan_dp, c_send, c_recv)
    gate_sum.middle()
    out[...] = (residual[...] + summed_out.finish()).astype(jnp.bfloat16)
    send_halo.wait()
    local[ROWS - 8 : ROWS, :] = local[ROWS - 8 : ROWS, :] + halo_in[...]
    to_x = to_a
    to_x[...] = local[...].astype(jnp.bfloat16)
    loads[1].wait()
    loads[3].wait()

    def produce(by):
        at = pl.ds(pl.multiple_of(chip_row(by, 0), 128), 128)
        total = matmul(to_x[at, :], branch_w[0]) + matmul(to_y[at, :], branch_w[1])
        partial[at, :] = total.astype(jnp.bfloat16)

    summed.start(produce)
    weight_grad(bx_grad, [(normed_one, to_x)])
    bx_sum.start()
    outy_sum.middle()
    up_sum.turn()
    blocks_sum.middle()
    norm_grad = summed.finish()
    before_norm, gain_part = norm_back(own[...].astype(jnp.float32), gains[0:1, :], norm_grad)
    tokens_grad[...] = (grad[...] + before_norm).astype(jnp.bfloat16)
    gain_t[index, 0:1, :] = gain_part
    gain_t[index, 1:2, :] = grad_gain_two[...]
    gain_copies = []
    for by in range(1, N_T):
        copy = remote(
            gain_t.at[index],
            gain_t.at[index],
            t_send.at[by],
            t_recv.at[by],
            {"tensor": lax.rem(index + by, N_T)},
        )
        copy.start()
        gain_copies.append(copy)
    gate_sum.turn()
    bx_sum.middle()
    for copy in gain_copies:
        copy.wait()
    total = gain_t[0]
    for by in range(1, N_T):
        total = total + gain_t[by]
    gain_dp[me] = total
    gain_copies = start_share(gain_dp, g_send, g_recv)
    up_sum.finish(up_share)
    outy_sum.turn()
    blocks_sum.turn()
    gate_sum.finish(gate_share)
    bx_sum.turn()
    for copy in channel_copies + gain_copies:
        copy.wait()
    total, channels = gain_dp[0], chan_dp[0]
    for by in range(1, N_DP):
        total = total + gain_dp[by]
        channels = channels + chan_dp[by]
    gain_sum[...] = total
    channel_sum[...] = channels
    outy_sum.finish(outy_share)
    blocks_sum.finish(blocks_share)
    bx_sum.finish(bx_share)


def mixer_backward(
    rounded, tokens, grad, residual, grad_gain_two, chan, gains, flags, gates, saved, out_partial, out_proj, branch_t, gate_grad, up_grad
):
    f32, bf16 = jnp.float32, jnp.bfloat16
    dma = pltpu.SemaphoreType.DMA
    here = pl.BlockSpec(memory_space=pltpu.VMEM)
    there = pl.BlockSpec(memory_space=pl.ANY)
    wide_f32 = pltpu.VMEM((ROWS, WIDTH), f32)
    wide_bf16 = pltpu.VMEM((ROWS, WIDTH), bf16)
    block_bf16 = pltpu.VMEM((ROWS, BLOCK), bf16)
    longer = pltpu.VMEM((ROWS + 8, WIDTH), f32)
    return pl.pallas_call(
        backward_kernel,
        out_shape=(
            jax.ShapeDtypeStruct((OWN, D), bf16),
            jax.ShapeDtypeStruct((OWN, D), bf16),
            jax.ShapeDtypeStruct((2, D), f32),
            jax.ShapeDtypeStruct((8, WIDTH), f32),
            jax.ShapeDtypeStruct((2 * HALF, HIDE), f32),
            jax.ShapeDtypeStruct((2 * HALF, HIDE), f32),
            jax.ShapeDtypeStruct((2 * HALF, 2 * WIDTH), f32),
            jax.ShapeDtypeStruct((2 * HALF, 384), f32),
            jax.ShapeDtypeStruct((2 * GATE_HALF, 2 * WIDTH), f32),
            jax.ShapeDtypeStruct((4, 4, 2, HALF, 2 * WIDTH), bf16),
            jax.ShapeDtypeStruct((4, 4, 2, HALF, 384), bf16),
        ),
        in_specs=[here, there] + [here] * 16 + [there] * 5,
        out_specs=tuple([here] * 9 + [there] * 2),
        scratch_shapes=[
            pltpu.VMEM((WIDTH, D), bf16),
            pltpu.VMEM((2, WIDTH, D), bf16),
            pltpu.VMEM((2, WIDTH, 2 * BLOCK), bf16),
            wide_bf16,
            wide_f32,
            wide_f32,
            wide_f32,
            wide_bf16,
            wide_bf16,
            pltpu.VMEM((ROWS, 2 * BLOCK), f32),
            block_bf16,
            block_bf16,
            block_bf16,
            block_bf16,
            longer,
            pltpu.VMEM((N_DP, 8, WIDTH), f32),
            pltpu.VMEM((8, WIDTH), f32),
            pltpu.VMEM((8, WIDTH), f32),
            pltpu.VMEM((4, 4, 2, GATE_HALF, 2 * WIDTH), f32),
            pltpu.VMEM((ROWS, D), bf16),
            pltpu.VMEM((2, 4, 2, HALF, 2 * WIDTH), bf16),
            pltpu.VMEM((OWN, D), bf16),
            pltpu.VMEM((N_T, 2, D), f32),
            pltpu.VMEM((N_DP, 2, D), f32),
            pltpu.VMEM((N_DP, 8, WIDTH), f32),
            dma((4,)),
            dma((2,)),
            dma((N_DP,)),
            dma((N_DP,)),
            dma((2,)),
            dma((2,)),
            dma,
            dma,
            dma((N_T,)),
            dma((N_T,)),
            dma((N_DP,)),
            dma((N_DP,)),
            dma((N_DP,)),
            dma((N_DP,)),
        ]
        + reduce_scratch()
        + data_scratch(HALF, HIDE, bf16)
        + data_scratch(HALF, 2 * WIDTH, bf16)
        + data_scratch(HALF, 384, bf16)
        + data_scratch(GATE_HALF, 2 * WIDTH, f32)
        + reduce_scratch()[:1]
        + reduce_scratch()[2:]
        + data_scratch(HALF, HIDE, bf16),
        compiler_params=params(3),
    )(
        rounded, tokens, grad, residual, grad_gain_two, chan, gains, flags, gates, *saved, out_partial, out_proj, branch_t, gate_grad, up_grad
    )


def rms_norm(values, gain):
    return values * lax.rsqrt(jnp.mean(values * values, axis=-1, keepdims=True) + NORM_EPS) * gain


def matmul(left, right):
    return jnp.dot(left, right, preferred_element_type=jnp.float32)


def times_transposed(left, right):
    return lax.dot_general(
        left, right, (((1,), (1,)), ((), ())), preferred_element_type=jnp.float32
    )


def transposed_times(left, right):
    return lax.dot_general(
        left, right, (((0,), (0,)), ((), ())), preferred_element_type=jnp.float32
    )


def adam_step(weight, grad, first, second, rate, decay):
    first_new = BETA_ONE * first + (1.0 - BETA_ONE) * grad
    second_new = BETA_TWO * second + (1.0 - BETA_TWO) * grad * grad
    first_hat = first_new / (1.0 - BETA_ONE**STEP)
    second_hat = second_new / (1.0 - BETA_TWO**STEP)
    weight_new = weight - rate * (first_hat / (jnp.sqrt(second_hat) + ADAM_EPS) + decay * weight)
    return (first_new, second_new, weight_new)


SHARE = 2 * HALF
SPAN = 384
DECAY = 0.1
BRANCH_RATE, GATE_RATE, OUT_RATE = 3.0 * D**-0.5, 3.0 * BLOCK**-0.5, 3.0 * (L // 8) ** -0.5
FFN_RATE, DOWN_RATE = 3.0 * D**-0.5, 3.0 * (F // 2) ** -0.5


def update_jobs():
    return (
        ("down", None, 0, 0, HIDE, 0, DOWN_RATE),
        ("ffn", 1, 1, 0, HIDE, HIDE, FFN_RATE),
        ("ffn", 0, 2, 0, HIDE, 0, FFN_RATE),
        ("out", None, 3, 0, WIDTH, 0, OUT_RATE),
        ("branch", 1, 3, WIDTH, WIDTH, WIDTH, BRANCH_RATE),
        ("branch", 0, 4, 0, WIDTH, 0, BRANCH_RATE),
        ("gate", 0, 5, 0, WIDTH, 0, GATE_RATE),
        ("gate", 1, 5, WIDTH, WIDTH, WIDTH, GATE_RATE),
    )


ARRAYS = ("down", "ffn", "out", "branch", "gate")


def update_kernel(*refs):
    shares, weights = refs[:6], dict(zip(ARRAYS, refs[6:11]))
    moments = {name: refs[11 + 2 * i : 13 + 2 * i] for i, name in enumerate(ARRAYS)}
    outs = {name: refs[21 + 3 * i : 24 + 3 * i] for i, name in enumerate(ARRAYS)}
    windows = dict(zip(ARRAYS, refs[36:41]))
    held = refs[41:49]
    in_sem, window_sem, out_sem = refs[49:]
    me = lax.axis_index("dp")
    begin = jnp.minimum(me * SHARE // 128 * 128, D - SPAN)
    copies = {}

    def copy(key, source, target, sem):
        copies[key] = pltpu.make_async_copy(source, target, sem)
        copies[key].start()

    jobs = update_jobs()
    waiting = list(ARRAYS)
    for number, (name, part, *_) in enumerate(jobs):
        if name not in copies:
            source = weights[name]
            if name != "gate":
                source = source.at[:, pl.ds(pl.multiple_of(begin, 128), SPAN)]
            copy(name, source, windows[name], window_sem.at[ARRAYS.index(name)])
        for which in range(2):
            source = moments[name][which]
            source = source if part is None else source.at[part]
            copy((number, which), source, held[number].at[which], in_sem.at[number, which])
    for number, (name, part, share, lane, width, row, rate) in enumerate(jobs):
        if name in waiting:
            waiting.remove(name)
            copies[name].wait()
        count = 16 if name == "gate" else SHARE
        span = BLOCK if name == "gate" else SPAN
        offset = me * count if name == "gate" else me * SHARE - begin
        mine = lax.broadcasted_iota(jnp.int32, (count, span), 0) + offset
        lanes = lax.broadcasted_iota(jnp.int32, (count, span), 1)
        chosen = jnp.where(lanes == mine, 1.0, 0.0).astype(jnp.bfloat16)
        box = held[number]
        box[2] = times_transposed(chosen, windows[name][row : row + width, :])
        for which in range(2):
            copies[number, which].wait()

        def body(first, box=box, share=share, lane=lane, width=width, rate=rate):
            at = pl.ds(first, 16)
            grad = shares[share][at, lane : lane + width]
            new = adam_step(box[2, at, :], grad, box[0, at, :], box[1, at, :], rate, DECAY)
            for which in range(3):
                box[which, at, :] = new[which]

        tiles(count // 16, 16, body)
        for which in range(3):
            target = outs[name][which]
            target = target if part is None else target.at[part]
            copy((number, which), box.at[which], target, out_sem.at[number, which])
    for number in range(len(jobs)):
        for which in range(3):
            copies[number, which].wait()


def update_weights(shares, weights, moments):
    f32, bf16 = jnp.float32, jnp.bfloat16
    dma = pltpu.SemaphoreType.DMA
    here = pl.BlockSpec(memory_space=pltpu.VMEM)
    there = pl.BlockSpec(memory_space=pl.ANY)
    jobs = update_jobs()
    return pl.pallas_call(
        update_kernel,
        out_shape=tuple(
            jax.ShapeDtypeStruct(moments[2 * i].shape, f32) for i in range(5) for _ in range(3)
        ),
        in_specs=[here] * 6 + [there] * 15,
        out_specs=tuple([there] * 15),
        scratch_shapes=[
            pltpu.VMEM((weight.shape[0], BLOCK if name == "gate" else SPAN), bf16)
            for name, weight in zip(ARRAYS, weights)
        ]
        + [pltpu.VMEM((3, 16 if job[0] == "gate" else SHARE, job[4]), f32) for job in jobs]
        + [dma((len(jobs), 2)), dma((5,)), dma((len(jobs), 3))],
        compiler_params=pltpu.CompilerParams(vmem_limit_bytes=63 * 2**20),
    )(*shares, *weights, *moments)


def shards(
    tokens,
    cotangent,
    segments,
    gains,
    channel_params,
    branch_in,
    gate_blocks,
    out_proj,
    ffn_in,
    ffn_down,
    gains_first,
    gains_second,
    channel_first,
    channel_second,
    branch_first,
    branch_second,
    gate_first,
    gate_second,
    out_first,
    out_second,
    ffn_in_first,
    ffn_in_second,
    down_first,
    down_second,
):
    rows = ROWS
    data_index = lax.axis_index("dp")

    padded_ids = jnp.concatenate([jnp.full((3,), -1, jnp.int32), segments])
    local_ids = lax.dynamic_slice_in_dim(padded_ids, data_index * rows, rows + 3)
    marks = [local_ids[3 - tap : 3 - tap + rows] == local_ids[3:] for tap in range(4)]
    marks.append(local_ids[3:] != local_ids[2 : 2 + rows])
    flags = jnp.pad(jnp.stack(marks, 1).astype(jnp.float32), ((0, 8), (0, 3)))
    decay_param = channel_params[4:5]
    chan = jnp.concatenate(
        [channel_params, jax.nn.softplus(decay_param), jax.nn.sigmoid(decay_param), decay_param], 0
    )
    branch_t = branch_in.swapaxes(1, 2)
    gates_t = gate_blocks.swapaxes(1, 2)
    ffn_t = ffn_in.swapaxes(1, 2).reshape(2 * HIDE, D)
    residual_own, block, *saved = mixer_forward(
        tokens, branch_t, gates_t, out_proj, chan, gains, flags
    )
    residual_grad, gain_two_part, rounded, gate_grad, up_grad, _, out_partial, down_share = ffn_middle(
        block, residual_own, cotangent, gains, ffn_t, ffn_down
    )
    (
        tokens_grad, block_out, gain_grad, channel_grad, gate_share, up_share, outy_share, bx_share, blocks_share, _, _,
    ) = mixer_backward(
        rounded,
        tokens,
        residual_grad,
        residual_own,
        gain_two_part,
        chan,
        gains,
        flags,
        gates_t,
        saved,
        out_partial,
        out_proj,
        branch_t,
        gate_grad,
        up_grad,
    )
    channel_rate = jnp.array([1.0, 1.0, 1.0, 1.0, 3.0], jnp.float32)[:, None]
    gains_out = adam_step(gains, gain_grad, gains_first, gains_second, 1.0, 0.0)
    channel_out = adam_step(
        channel_params, channel_grad[:5], channel_first, channel_second, channel_rate, 0.0
    )
    new = update_weights(
        (down_share, up_share, gate_share, outy_share, bx_share, blocks_share),
        (
            ffn_down,
            ffn_t,
            out_proj,
            branch_t.reshape(2 * WIDTH, D),
            gates_t.reshape(2 * WIDTH, BLOCK),
        ),
        (
            down_first.T,
            down_second.T,
            ffn_in_first,
            ffn_in_second,
            out_first.T,
            out_second.T,
            branch_first,
            branch_second,
            gate_first,
            gate_second,
        ),
    )
    return (
        block_out,
        tokens_grad,
        *gains_out,
        *channel_out,
        *new[9:12],
        *new[12:15],
        *(value.T for value in new[6:9]),
        *new[3:6],
        *(value.T for value in new[0:3]),
    )


def solution(mesh):
    weights = [
        P(None, None, "tensor"),
        P(None, None, "tensor"),
        P("tensor", None),
        P(None, None, "tensor"),
        P("tensor", None),
    ]
    owned = [
        P(None, "dp", "tensor"),
        P(None, "dp", "tensor"),
        P("tensor", "dp"),
        P(None, "dp", "tensor"),
        P("tensor", "dp"),
    ]
    moments = [P(), P(None, "tensor")] + owned
    placed = [P("dp", None), P("dp", None), P(), P(), P(None, "tensor")] + weights
    for spec in moments:
        placed += [spec, spec]
    outs = [P(("dp", "tensor"), None)] * 2
    for spec in moments:
        outs += [spec, spec, spec]
    return jax.shard_map(
        shards, mesh=mesh, in_specs=tuple(placed), out_specs=tuple(outs), check_vma=False
    )
```

```python
import functools

import jax
import jax.numpy as jnp
from jax import lax
from jax.experimental import pallas as pl
from jax.experimental.pallas import tpu as pltpu
from jax.sharding import PartitionSpec as P

D = 2560
L = 2560
BLOCK = 256
F = 7680
STEP = 10
N_DP = 16
N_T = 8
ROWS = 512
OWN = ROWS // N_T
WIDTH = L // N_T
HIDE = F // N_T
HALF = 80
GATE_HALF = 8
MESH = pl.DeviceIdType.MESH

NORM_EPS = 1e-06
ADAM_EPS = 1e-08
BETA_ONE = 0.9
BETA_TWO = 0.95


def params(cid):
    return pltpu.CompilerParams(
        collective_id=cid, has_side_effects=True, vmem_limit_bytes=63 * 2**20
    )


def vmem(count):
    return [pl.BlockSpec(memory_space=pltpu.VMEM)] * count


def announce(peers):
    barrier = pltpu.get_barrier_semaphore()
    for peer in peers:
        pl.semaphore_signal(barrier, inc=1, device_id=peer, device_id_type=MESH)
    return lambda: pl.semaphore_wait(barrier, len(peers))


def remote(source, target, send_sem, recv_sem, peer):
    return pltpu.make_async_remote_copy(
        src_ref=source,
        dst_ref=target,
        send_sem=send_sem,
        recv_sem=recv_sem,
        device_id=peer,
        device_id_type=MESH,
    )


class Later:
    def __init__(self, make):
        self.make = make

    def start(self):
        self.make().start()

    def wait(self):
        self.make().wait()

    def wait_send(self):
        self.make().wait_send()

    def wait_recv(self):
        self.make().wait_recv()


def place():
    index = lax.axis_index("tensor")
    return index // 2, lax.rem(index, 2)


def at_x(x, core, by):
    return {"tensor": lax.rem(x + by, 4) * 2 + core}


def tensor_peers():
    x, core = place()
    return [{"tensor": x * 2 + 1 - core}] + [at_x(x, core, by) for by in (1, 2, 3)]


def chip_row(by, which):
    x, _ = place()
    return pl.multiple_of((lax.rem(x + by, 4) * 2 + which) * OWN, OWN)


ARRIVAL = {0: 0, 1: 1, 3: 2, 2: 3}


def arrival_row(by, which):
    return pl.multiple_of((ARRIVAL[by % 4] * 2 + which) * OWN, OWN)


class TensorSum:
    ORDER = (2, 1, 3, 0)

    def __init__(self, row, partial, pair, held, landed, pair_send, pair_recv, x_send, x_recv):
        self.row = row
        self.partial, self.pair, self.held, self.landed = partial, pair, held, landed
        self.sems = pair_send, pair_recv, x_send, x_recv
        self.pair_copies, self.x_copies = {}, {}

    def give(self, by):
        def make():
            x, core = place()
            return remote(
                self.partial.at[pl.ds(self.row(by, 1 - core), OWN)],
                self.pair.at[by],
                self.sems[0].at[by],
                self.sems[1].at[by],
                {"tensor": x * 2 + 1 - core},
            )

        self.pair_copies[by] = Later(make)
        self.pair_copies[by].start()

    def pass_on(self, by):
        _, core = place()
        self.pair_copies[by].wait_recv()
        mine = self.partial[pl.ds(self.row(by, core), OWN), :].astype(jnp.float32)
        self.held[by - 1] = (mine + self.pair[by].astype(jnp.float32)).astype(jnp.bfloat16)

        def make():
            x, core = place()
            return remote(
                self.held.at[by - 1],
                self.landed.at[by - 1],
                self.sems[2].at[by - 1],
                self.sems[3].at[by - 1],
                at_x(x, core, by),
            )

        self.x_copies[by] = Later(make)
        self.x_copies[by].start()

    def start(self, produce):
        for step, by in enumerate(self.ORDER):
            produce(by)
            self.give(by)
            if step:
                self.pass_on(self.ORDER[step - 1])

    def finish(self):
        _, core = place()
        self.pair_copies[0].wait_recv()
        total = self.partial[pl.ds(self.row(0, core), OWN), :].astype(jnp.float32)
        total = total + self.pair[0].astype(jnp.float32)
        for by in (1, 3, 2):
            self.x_copies[by].wait_recv()
            total = total + self.landed[by - 1].astype(jnp.float32)
        for by in self.ORDER:
            self.pair_copies[by].wait_send()
        for by in (2, 1, 3):
            self.x_copies[by].wait_send()
        return total


def reduce_scratch():
    return [
        pltpu.VMEM((4, OWN, D), jnp.bfloat16),
        pltpu.VMEM((3, OWN, D), jnp.bfloat16),
        pltpu.VMEM((3, OWN, D), jnp.bfloat16),
        pltpu.SemaphoreType.DMA((4,)),
        pltpu.SemaphoreType.DMA((4,)),
        pltpu.SemaphoreType.DMA((3,)),
        pltpu.SemaphoreType.DMA((3,)),
    ]


class TensorGather:
    def __init__(self, row, whole, x_send, x_recv, pair_send, pair_recv):
        self.row, self.whole, self.sems = row, whole, (x_send, x_recv, pair_send, pair_recv)

    def at(self, by):
        _, core = place()
        return self.whole.at[pl.ds(self.row(by, core), OWN)]

    def start(self, block):
        _, core = place()
        self.whole[pl.ds(self.row(0, core), OWN), :] = block
        self.sends, self.pairs = [], {}
        for by in (1, 3, 2):

            def make(by=by):
                x, core = place()
                mine = self.at(0)
                target = mine if self.row is chip_row else self.at(4 - by)
                return remote(
                    mine,
                    target,
                    self.sems[0].at[by - 1],
                    self.sems[1].at[by - 1],
                    at_x(x, core, by),
                )

            self.sends.append(Later(make))
            self.sends[-1].start()
        self.hand(0)

    def hand(self, by):
        def make():
            x, core = place()
            block = self.at(by)
            return remote(
                block,
                block,
                self.sems[2].at[by],
                self.sems[3].at[by],
                {"tensor": x * 2 + 1 - core},
            )

        self.pairs[by] = Later(make)
        self.pairs[by].start()

    def arrive(self, by):
        x, core = place()
        sender = 4 - by
        block = self.at(by)
        remote(
            block,
            block,
            self.sems[0].at[sender - 1],
            self.sems[1].at[sender - 1],
            at_x(x, core, sender),
        ).wait_recv()
        self.hand(by)

    def settle(self, by):
        self.pairs[by].wait_recv()

    def finish(self):
        for copy in self.sends:
            copy.wait_send()
        for copy in self.pairs.values():
            copy.wait_send()


class DataSum:
    LOW, HIGH = pl.ds(0, 2), pl.ds(2, 2)

    def __init__(self, grad, own, via, ring, last, near, send, recv, local, rows):
        self.grad, self.own, self.near, self.via = grad, own, near, via
        self.ring, self.last, self.rows = ring, last, rows
        self.send, self.recv, self.local = send, recv, local
        self.copies = {}

    def spots(self, half):
        me = lax.axis_index("dp")
        z, y = me // 4, lax.rem(me, 4)
        return (y, z) if half == 0 else (z, y)

    def peer(self, half, first_by, second_by):
        first, second = self.spots(half)
        a, b = lax.rem(first + first_by + 4, 4), lax.rem(second + second_by + 4, 4)
        return {"dp": b * 4 + a if half == 0 else a * 4 + b}

    def block(self, half, by, part):
        a = lax.rem(self.spots(half)[0] + by + 4, 4)
        return self.grad.at[part, a, 0] if half == 0 else self.grad.at[a, part, 1]

    def ship(self, half, slot, source, target, first_by, second_by):
        def make():
            return remote(
                source(),
                target(),
                self.send.at[half, slot],
                self.recv.at[half, slot],
                self.peer(half, first_by, second_by),
            )

        self.copies[half, slot] = Later(make)
        self.copies[half, slot].start()

    def own_load(self, half):
        return pltpu.make_async_copy(
            self.block(half, 0, pl.ds(0, 4)), self.own.at[half], self.local.at[half, 2]
        )

    def start(self):
        for half in (0, 1):
            self.ship(
                half, 0, lambda half=half: self.block(half, 2, self.LOW), lambda half=half: self.via.at[half, 0], 1, 0
            )
            self.ship(
                half, 1, lambda half=half: self.block(half, 2, self.HIGH), lambda half=half: self.via.at[half, 1], -1, 0
            )
            self.own_load(half).start()
        for half in (0, 1):
            self.ship(
                half, 2, lambda half=half: self.block(half, 1, self.HIGH), lambda half=half: self.ring.at[half, 0], 1, 0
            )
            self.ship(
                half, 3, lambda half=half: self.block(half, -1, self.LOW), lambda half=half: self.ring.at[half, 1], -1, 0
            )

    def add(self, target, sources, blocks):
        for block in range(blocks):
            if len(sources) == 1:
                target[block] = target[block] + sources[0][block]
                continue
            total = target[block].astype(jnp.float32)
            for source in sources:
                total = total + source[block].astype(jnp.float32)
            target[block] = total.astype(target.dtype)

    def middle(self):
        for half in (0, 1):
            loads = []
            for side, (by, part) in enumerate(((1, self.LOW), (-1, self.HIGH))):
                load = pltpu.make_async_copy(
                    self.block(half, by, part), self.near.at[side], self.local.at[half, side]
                )
                load.start()
                loads.append(load)
            for side in (0, 1):
                loads[side].wait()
                self.copies[half, side].wait_recv()
                via = self.via.at[half, side]
                self.add(via, [self.near.at[side]], 2)
                self.ship(
                    half,
                    4 + side,
                    lambda half=half, side=side: self.via.at[half, side],
                    lambda half=half, side=side: self.ring.at[half, 2 + side],
                    1 - 2 * side,
                    0,
                )

    def turn(self):
        for half in (0, 1):
            self.own_load(half).wait()
            for slot in (2, 3, 4, 5):
                self.copies[half, slot].wait_recv()
            ring = self.ring
            self.add(self.own.at[half, self.LOW], [ring.at[half, 1], ring.at[half, 2]], 2)
            self.add(self.own.at[half, self.HIGH], [ring.at[half, 0], ring.at[half, 3]], 2)
            for by in (1, 2, 3):
                self.ship(
                    half,
                    5 + by,
                    lambda half=half, by=by: self.own.at[
                        half, lax.rem(self.spots(half)[1] + by, 4)
                    ],
                    lambda half=half, by=by: self.last.at[half, by - 1],
                    0,
                    by,
                )

    def finish(self, share):
        for half in (0, 1):
            for by in (1, 2, 3):
                self.copies[half, 5 + by].wait_recv()
            total = self.own[half, self.spots(half)[1]].astype(jnp.float32)
            for by in range(3):
                total = total + self.last[half, by].astype(jnp.float32)
            share[half * self.rows : (half + 1) * self.rows, :] = total
        for copy in self.copies.values():
            copy.wait_send()


def data_buffers(rows, columns, dtype):
    return [
        pltpu.VMEM((2, 4, rows, columns), dtype),
        pltpu.VMEM((2, 2, 2, rows, columns), dtype),
        pltpu.VMEM((2, 4, 2, rows, columns), dtype),
        pltpu.VMEM((2, 3, rows, columns), dtype),
    ]


def data_sems():
    dma = pltpu.SemaphoreType.DMA
    return [dma((2, 9)), dma((2, 9)), dma((2, 3))]


def ring_peers():
    me = lax.axis_index("dp")
    z, y = me // 4, lax.rem(me, 4)
    along_y = [{"dp": z * 4 + lax.rem(y + by, 4)} for by in (1, 2, 3)]
    return along_y + [{"dp": lax.rem(z + by, 4) * 4 + y} for by in (1, 2, 3)]


def gather_scratch():
    return [
        pltpu.SemaphoreType.DMA((3,)),
        pltpu.SemaphoreType.DMA((3,)),
        pltpu.SemaphoreType.DMA((4,)),
        pltpu.SemaphoreType.DMA((4,)),
    ]


def dp_peers():
    me = lax.axis_index("dp")
    return [{"dp": lax.rem(me + by, N_DP)} for by in range(1, N_DP)]


def place_matrix(shift):
    row = lax.broadcasted_iota(jnp.int32, (WIDTH, 2 * BLOCK), 0)
    lane = lax.broadcasted_iota(jnp.int32, (WIDTH, 2 * BLOCK), 1)
    return jnp.where(lane == row + shift, 1.0, 0.0).astype(jnp.bfloat16)


def wide_gates(gates, wide, shift):
    row = lax.broadcasted_iota(jnp.int32, (WIDTH, BLOCK), 0)
    low = row + shift < BLOCK
    for gate in range(2):
        matrix = gates[gate].astype(jnp.float32)
        wide[gate, :, 0:BLOCK] = jnp.where(low, matrix, 0.0).astype(jnp.bfloat16)
        wide[gate, :, BLOCK : 2 * BLOCK] = jnp.where(low, 0.0, matrix).astype(jnp.bfloat16)


def one_less_exp(z):
    series = 1.0 + z / 7.0
    for term in (6.0, 5.0, 4.0, 3.0, 2.0):
        series = 1.0 + z / term * series
    return jnp.where(z > -0.35, -z * series, 1.0 - jnp.exp(z))


def tiles(count, size, body, unroll=1):
    def step(index, _):
        body(pl.multiple_of(index * size, size))
        return 0

    lax.fori_loop(0, count, step, 0, unroll=unroll)


def norm_rows(source, target, gain, rows):
    def body(first):
        at = pl.ds(first, 16)
        target[at, :] = rms_norm(source[at, :].astype(jnp.float32), gain).astype(jnp.bfloat16)

    tiles(rows // 16, 16, body, min(4, rows // 16))


def shifted(values, by, fill, reverse):
    count = values.shape[0]
    row = lax.broadcasted_iota(jnp.int32, values.shape, 0)
    if reverse:
        return jnp.where(row < count - by, pltpu.roll(values, count - by, 0), fill)
    return jnp.where(row >= by, pltpu.roll(values, by, 0), fill)


def local_scan(factor_at, term_at, values, prods, reverse):
    def step(index, held):
        prod, value = held
        first = pl.multiple_of((ROWS // 8 - 1 - index if reverse else index) * 8, 8)
        factor, term = factor_at(first), term_at(first)
        for by in (1, 2, 4):
            term = term + factor * shifted(term, by, 0.0, reverse)
            factor = factor * shifted(factor, by, 1.0, reverse)
        value = factor * value + term
        prod = factor * prod
        values[pl.ds(first, 8), :] = value
        prods[pl.ds(first, 8), :] = prod
        last = 0 if reverse else 7
        return (
            jnp.broadcast_to(prod[last : last + 1], prod.shape),
            jnp.broadcast_to(value[last : last + 1], value.shape),
        )

    ones = jnp.ones((8, WIDTH), jnp.float32)
    return lax.fori_loop(0, ROWS // 8, step, (ones, jnp.zeros_like(ones)), unroll=8)


def start_share(slots, send, recv):
    me = lax.axis_index("dp")
    copies = []
    for by in range(1, N_DP):
        copy = remote(
            slots.at[me], slots.at[me], send.at[by], recv.at[by], {"dp": lax.rem(me + by, N_DP)}
        )
        copy.start()
        copies.append(copy)
    return copies


def beside_peers():
    index = lax.axis_index("tensor")
    return {"tensor": lax.rem(index + 1, N_T)}, {"tensor": lax.rem(index + N_T - 1, N_T)}


def far_peer():
    index = lax.axis_index("tensor")
    _, core = place()
    return {"tensor": lax.rem(index + N_T - 1 + 2 * core, N_T)}


def gelu_parts(y):
    c = 0.7978845608028654
    inner = jnp.tanh(c * (y + 0.044715 * y * y * y))
    half = 0.5 * (1.0 + inner)
    slope = half + 0.5 * y * (1.0 - inner * inner) * c * (1.0 + 3 * 0.044715 * y * y)
    return y * half, slope


def forward_kernel(
    tokens, branch_hbm, gates, out_hbm, chan, gains, flags, residual, block, *rest
):
    outs = rest[:9]
    (
        normed_one, ext, window, pre_a, pre_x, carry, state, branch_y, mixed,
        branch_w, out_w, halo, halo_norm, wide, placing, update, values, prods, gelu_y, low, high, slots, partial,
        load_sem, store_sem, halo_send, halo_recv, side_send, side_recv, slot_send, slot_recv, *scratch
    ) = rest[9:]
    me, index = lax.axis_index("dp"), lax.axis_index("tensor")
    shift = lax.rem(index * WIDTH, BLOCK)
    loads = [
        pltpu.make_async_copy(branch_hbm.at[0], branch_w.at[0], load_sem.at[0]),
        pltpu.make_async_copy(branch_hbm.at[1], branch_w.at[1], load_sem.at[1]),
        pltpu.make_async_copy(out_hbm, out_w, load_sem.at[2]),
    ]
    for load in loads:
        load.start()
    ready = announce(dp_peers() + tensor_peers() + [far_peer()])
    stores = []

    def store(number, source, target):
        copy = pltpu.make_async_copy(source, target, store_sem.at[number])
        copy.start()
        stores.append(copy)

    send_halo = remote(
        tokens.at[pl.ds(ROWS - 16, 16)],
        halo,
        halo_send,
        halo_recv,
        {"dp": lax.rem(me + 1, N_DP)},
    )
    wide_gates(gates, wide, shift)
    placing[...] = place_matrix(shift)
    gain = gains[0:1, :]
    norm_rows(tokens, normed_one, gain, ROWS)
    ready()
    send_halo.start()
    store(0, normed_one, outs[0])
    loads[0].wait()

    def branch_tile(first):
        at = pl.ds(first, 128)
        value = times_transposed(normed_one[at, :], branch_w[0])
        ext[pl.ds(first + 16, 128), :] = value.astype(jnp.bfloat16).astype(jnp.float32)

    tiles(4, 128, branch_tile)
    send_halo.wait()
    norm_rows(halo, halo_norm, gain, 16)
    ext[0:16, :] = times_transposed(halo_norm[...], branch_w[0]).astype(jnp.bfloat16).astype(jnp.float32)

    def conv_tile(first):
        near = ext[pl.ds(first + 8, 136), :]
        total = chan[0:1, :] * near[8:]
        for tap in range(1, 4):
            counted = flags[pl.ds(first, 128), tap : tap + 1] > 0.0
            total = total + chan[tap : tap + 1, :] * jnp.where(counted, near[8 - tap : 136 - tap], 0.0)
        window[pl.ds(first, 128), :] = matmul(total.astype(jnp.bfloat16), placing[...]).astype(
            jnp.bfloat16
        )

    tiles(4, 128, conv_tile)
    store(1, ext, outs[1])
    up, down = beside_peers()
    to_up = remote(
        window.at[:, pl.ds(BLOCK, BLOCK)], low, side_send.at[0], side_recv.at[0], up
    )
    to_down = remote(window.at[:, pl.ds(0, BLOCK)], high, side_send.at[1], side_recv.at[1], down)
    to_up.start()
    to_down.start()
    loads[1].wait()

    def gelu_tile(first):
        at = pl.ds(first, 128)
        branch_y[at, :] = times_transposed(normed_one[at, :], branch_w[1])

    tiles(4, 128, gelu_tile)
    store(2, branch_y, outs[6])
    to_up.wait()
    to_down.wait()

    def window_tile(first):
        at = pl.ds(first, 128)
        own_conv = lax.dot_general(
            window[at, :], placing[...], (((1,), (1,)), ((), ())), preferred_element_type=jnp.float32
        )
        from_low = jnp.where(shift != 0, low[at, :].astype(jnp.float32), 0.0)
        from_high = jnp.where(shift != 192, high[at, :].astype(jnp.float32), 0.0)
        whole = window[at, :].astype(jnp.float32) + jnp.concatenate([from_low, from_high], 1)
        whole = whole.astype(jnp.bfloat16)
        window[at, :] = whole
        a = times_transposed(whole, wide[0])
        x = times_transposed(whole, wide[1])
        pre_a[at, :] = a
        pre_x[at, :] = x
        reset = flags[at, 4:5] > 0.0
        log_a = -8.0 * jax.nn.sigmoid(a) * chan[5:6, :]
        carry[at, :] = jnp.where(reset, 0.0, jnp.exp(log_a))
        scale = jnp.where(reset, 1.0, jnp.sqrt(one_less_exp(2.0 * log_a)))
        update[at, :] = own_conv * jax.nn.sigmoid(x) * scale

    tiles(4, 128, window_tile)
    store(3, window, outs[2])
    store(4, pre_a, outs[3])
    store(5, pre_x, outs[4])
    carry[ROWS : ROWS + 8, :] = jnp.ones((8, WIDTH), jnp.float32)
    store(6, carry, outs[5])
    prod, value = local_scan(
        lambda first: carry[pl.ds(first, 8), :],
        lambda first: update[pl.ds(first, 8), :],
        values,
        prods,
        False,
    )
    slots[me, 0:1, :] = prod[0:1]
    slots[me, 1:2, :] = value[0:1]
    copies = start_share(slots, slot_send, slot_recv)

    def activate(first):
        at = pl.ds(first, 64)
        y = branch_y[at, :]
        gelu_y[at, :] = gelu_parts(y)[0]

    tiles(8, 64, activate)
    for copy in copies:
        copy.wait()
    before = jnp.zeros((1, WIDTH), jnp.float32)
    for place_at in range(N_DP - 1):
        longer = slots[place_at, 0:1, :] * before + slots[place_at, 1:2, :]
        before = jnp.where(place_at < me, longer, before)

    state[0:8, :] = jnp.broadcast_to(before, (8, WIDTH))

    def finish(first):
        at = pl.ds(first, 64)
        total = values[at, :] + prods[at, :] * before
        state[pl.ds(first + 8, 64), :] = total
        mixed[at, :] = (total * gelu_y[at, :]).astype(jnp.bfloat16)

    tiles(8, 64, finish)
    store(7, state, outs[7])
    store(8, mixed, outs[8])
    loads[2].wait()

    def produce(by):
        at = pl.ds(pl.multiple_of(chip_row(by, 0), 128), 128)
        partial[at, :] = matmul(mixed[at, :], out_w[...]).astype(jnp.bfloat16)

    summed = TensorSum(chip_row, partial, *scratch)
    summed.start(produce)
    _, core = place()
    total = tokens[pl.ds(chip_row(0, core), OWN), :].astype(jnp.float32) + summed.finish()
    residual[...] = total
    block[...] = rms_norm(total, gains[1:2, :]).astype(jnp.bfloat16)
    for copy in stores:
        copy.wait()


def saved_shapes():
    f32, bf16 = jnp.float32, jnp.bfloat16
    return (
        ((ROWS, D), bf16),
        ((ROWS + 16, WIDTH), f32),
        ((ROWS, 2 * BLOCK), bf16),
        ((ROWS, WIDTH), f32),
        ((ROWS, WIDTH), f32),
        ((ROWS + 8, WIDTH), f32),
        ((ROWS, WIDTH), f32),
        ((ROWS + 8, WIDTH), f32),
        ((ROWS, WIDTH), bf16),
    )


def mixer_forward(tokens, branch_in, gate_blocks, out_proj, chan, gains, flags):
    f32, bf16 = jnp.float32, jnp.bfloat16
    dma = pltpu.SemaphoreType.DMA
    here = pl.BlockSpec(memory_space=pltpu.VMEM)
    there = pl.BlockSpec(memory_space=pl.ANY)
    shapes = saved_shapes()
    inside = shapes[:6] + (shapes[7], shapes[6], shapes[8])
    return pl.pallas_call(
        forward_kernel,
        out_shape=(
            jax.ShapeDtypeStruct((OWN, D), f32),
            jax.ShapeDtypeStruct((OWN, D), bf16),
            *(jax.ShapeDtypeStruct(*shape) for shape in shapes),
        ),
        in_specs=[here, there, here, there, here, here, here],
        out_specs=tuple([here] * 2 + [there] * 9),
        scratch_shapes=[pltpu.VMEM(*shape) for shape in inside]
        + [
            pltpu.VMEM((2, WIDTH, D), bf16),
            pltpu.VMEM((WIDTH, D), bf16),
            pltpu.VMEM((16, D), bf16),
            pltpu.VMEM((16, D), bf16),
            pltpu.VMEM((2, WIDTH, 2 * BLOCK), bf16),
            pltpu.VMEM((WIDTH, 2 * BLOCK), bf16),
            pltpu.VMEM((ROWS, WIDTH), f32),
            pltpu.VMEM((ROWS, WIDTH), f32),
            pltpu.VMEM((ROWS, WIDTH), f32),
            pltpu.VMEM((ROWS, WIDTH), f32),
            pltpu.VMEM((ROWS, BLOCK), bf16),
            pltpu.VMEM((ROWS, BLOCK), bf16),
            pltpu.VMEM((N_DP, 8, WIDTH), f32),
            pltpu.VMEM((ROWS, D), bf16),
            dma((3,)),
            dma((9,)),
            dma,
            dma,
            dma((2,)),
            dma((2,)),
            dma((N_DP,)),
            dma((N_DP,)),
        ]
        + reduce_scratch(),
        compiler_params=params(1),
    )(tokens, branch_in, gate_blocks, out_proj, chan, gains, flags)


def norm_back(value, gain, grad):
    scale = lax.rsqrt(jnp.mean(value * value, axis=-1, keepdims=True) + NORM_EPS)
    unit = value * scale
    scaled = grad * gain
    back = scale * (scaled - unit * jnp.mean(scaled * unit, axis=-1, keepdims=True))
    return back, jnp.sum(grad * unit, axis=0, keepdims=True)


def back_kernel(
    block, residual, gains, chan, flags, dy_hbm, ffn_hbm, down_hbm, tokens, out_hbm, branch_hbm, gates_hbm, *rest
):
    saved, rest = rest[:9], rest[9:]
    tokens_grad, out, gain_sum, channel_sum, blocks_share, *rest = rest
    shares, (down_grad, up_grad, gate_grad, outy_grad, bx_grad), rest = rest[:4], rest[4:9], rest[9:]
    (
        normed, rounded, grad, grad_gain_two, partial, stage, share_stage, near, near_blocks,
        low_in, high_in, slots, halo, halo_in, gain_t, gain_dp, chan_dp, blocks_grad,
        load_sem, stage_sem, share_sem, slot_send, slot_recv, side_send, side_recv, halo_send, halo_recv,
        t_send, t_recv, g_send, g_recv, c_send, c_recv, reuse_sem, free_sem, *scratch
    ) = rest
    me, index = lax.axis_index("dp"), lax.axis_index("tensor")
    x, core = place()
    shift = lax.rem(index * WIDTH, BLOCK)
    ready = announce(dp_peers() + tensor_peers() + [far_peer()])

    def take(count):
        taken = scratch[:count]
        del scratch[:count]
        return taken

    sum_scratch = take(7)
    summed = TensorSum(arrival_row, partial, *sum_scratch)
    summed_out = TensorSum(arrival_row, partial, *sum_scratch)
    summed_last = TensorSum(chip_row, partial, *sum_scratch)
    before = TensorGather(arrival_row, normed, *take(4))
    after = TensorGather(chip_row, rounded, *take(4))
    first = take(4)
    down_sum = DataSum(down_grad, *first, near, *take(3), HALF)
    up_sum = DataSum(up_grad, *take(4), near, *take(3), HALF)
    gate_sum = DataSum(gate_grad, *take(4), near, *take(3), HALF)
    wide_part = [buffer.at[..., pl.ds(0, 640)] for buffer in first]
    bx_part = [buffer.at[..., pl.ds(640, 384)] for buffer in first]
    outy_sum = DataSum(outy_grad, *wide_part, near.at[..., pl.ds(0, 640)], *take(3), HALF)
    bx_sum = DataSum(bx_grad, *bx_part, near.at[..., pl.ds(640, 384)], *take(3), HALF)
    blocks_sum = DataSum(blocks_grad, *take(4), near_blocks, *take(3), GATE_HALF)
    stage[...] = jnp.zeros_like(stage)

    def weight_grad(target, jobs):
        pending = None
        for z in range(4):
            columns = pl.ds(z * 640, 640)
            parts = [transposed_times(left[:, columns], right[...]) for left, right in jobs]
            whole = parts[0] if len(parts) == 1 else jnp.concatenate(parts, 1)
            if pending is not None:
                pending.wait()
            stage[:, :, :, 0 : whole.shape[1]] = whole.astype(jnp.bfloat16).reshape(
                4, 2, HALF, whole.shape[1]
            )
            lanes = pl.ds(0, target.shape[4])
            pending = pltpu.make_async_copy(stage.at[:, :, :, lanes], target.at[z], stage_sem)
            pending.start()
        pending.wait()

    def keep_share(number):
        copy = pltpu.make_async_copy(share_stage, shares[number], share_sem)
        copy.start()
        copy.wait()

    def ffn_part(dy, ffn_w, down_w, hidden, to_gate, to_up, gate_pre, up_pre, grad_hidden):
        loads = []

        def load(source, target):
            copy = pltpu.make_async_copy(source, target, load_sem.at[len(loads)])
            copy.start()
            loads.append(copy)

        for by, spot in ARRIVAL.items():
            load(
                dy_hbm.at[pl.ds(pl.multiple_of(lax.rem(x + by, 4) * 128, 128), 128)],
                dy.at[pl.ds(spot * 128, 128)],
            )
        load(down_hbm, down_w)
        load(ffn_hbm.at[pl.ds(0, HIDE)], ffn_w.at[pl.ds(0, HIDE)])
        load(ffn_hbm.at[pl.ds(HIDE, HIDE)], ffn_w.at[pl.ds(HIDE, HIDE)])
        pieces = ((0, 384), (384, 384), (768, 192))
        ready()
        before.start(block[...])
        for copy in loads[:5]:
            copy.wait()
        for start, size in pieces:
            units = pl.ds(start, size)
            grad_hidden[:, units] = times_transposed(dy[...], down_w[units, :]).astype(jnp.bfloat16)
        for copy in loads[5:]:
            copy.wait()
        before.arrive(1)
        before.settle(0)
        before.settle(1)
        for group in range(2):
            if group:
                before.arrive(3)
                before.arrive(2)
                before.settle(3)
                before.settle(2)
            rows = pl.ds(group * 256, 256)
            for start, size in pieces:
                units = pl.ds(start, size)
                gate_pre[:, 0:size] = times_transposed(normed[rows, :], ffn_w[units, :])
                up_pre[:, 0:size] = times_transposed(normed[rows, :], ffn_w[pl.ds(HIDE + start, size), :])

                def activate(first, units=units, size=size, group=group):
                    here = pl.ds(first, 32)
                    at = pl.ds(pl.multiple_of(group * 256 + first, 32), 32)
                    value, slope = gelu_parts(gate_pre[here, 0:size])
                    up, back = up_pre[here, 0:size], grad_hidden[at, units].astype(jnp.float32)
                    hidden[at, units] = (value * up).astype(jnp.bfloat16)
                    to_up[at, units] = (back * value).astype(jnp.bfloat16)
                    to_gate[at, units] = (back * up * slope).astype(jnp.bfloat16)

                tiles(256 // 32, 32, activate)
        before.finish()

        def produce(by):
            at = pl.ds(arrival_row(by, 0), 128)
            total = matmul(to_gate[at, :], ffn_w[0:HIDE, :]) + matmul(
                to_up[at, :], ffn_w[HIDE : 2 * HIDE, :]
            )
            partial[at, :] = total.astype(jnp.bfloat16)

        summed.start(produce)

        weight_grad(down_grad, [(dy, hidden)])
        down_sum.start()
        weight_grad(up_grad, [(normed, to_up)])
        up_sum.start()
        down_sum.middle()
        norm_grad = summed.finish()
        back, gain_part = norm_back(residual[...], gains[1:2, :], norm_grad)
        back = back + dy[pl.ds(arrival_row(0, core), OWN), :].astype(jnp.float32)
        grad[...] = back
        grad_gain_two[...] = gain_part
        after.start(back.astype(jnp.bfloat16))

        def produce_out(first):
            at = pl.ds(first, 128)
            partial[at, :] = matmul(hidden[at, :], down_w[...]).astype(jnp.bfloat16)

        tiles(4, 128, produce_out)
        weight_grad(gate_grad, [(normed, to_gate)])
        gate_sum.start()

    f32, bf16 = jnp.float32, jnp.bfloat16
    pl.run_scoped(
        ffn_part,
        pltpu.VMEM((ROWS, D), bf16),
        pltpu.VMEM((2 * HIDE, D), bf16),
        pltpu.VMEM((HIDE, D), bf16),
        pltpu.VMEM((ROWS, HIDE), bf16),
        pltpu.VMEM((ROWS, HIDE), bf16),
        pltpu.VMEM((ROWS, HIDE), bf16),
        pltpu.VMEM((256, 384), f32),
        pltpu.VMEM((256, 384), f32),
        pltpu.VMEM((ROWS, HIDE), bf16),
    )

    def mixer_part(
        normed_one, ext, window, pre_a, pre_x, carry, branch_y, state, mixed,
        out_w, branch_w, gates, own, wide, to_y, local, sums, prods, to_a, to_gx, window_grad, low, high, conv_grad,
    ):
        targets = (
            normed_one, ext, window, pre_a, pre_x, carry, branch_y, state, mixed, out_w, branch_w, gates, own,
        )
        sources = (
            *saved,
            out_hbm,
            branch_hbm,
            gates_hbm,
            tokens.at[pl.ds(chip_row(0, core), OWN)],
        )
        loads = []
        for source, target in zip(sources, targets):
            loads.append(pltpu.make_async_copy(source, target, load_sem.at[len(loads)]))
            loads[-1].start()
        for by in (1, 3, 2):
            after.arrive(by)
        for by in (0, 1, 3, 2):
            after.settle(by)
        after.finish()
        for step, by in enumerate(summed_out.ORDER):
            summed_out.give(by)
        for by in (2, 1, 3):
            summed_out.pass_on(by)
        for copy in loads:
            copy.wait()
        wide_gates(gates, wide, shift)

        def mixed_tile(first):
            at = pl.ds(first, 128)
            local[at, :] = times_transposed(rounded[at, :], out_w[...])

        tiles(4, 128, mixed_tile)

        def gelu_tile(first):
            at = pl.ds(first, 64)
            value, slope = gelu_parts(branch_y[at, :])
            mixed_grad = local[at, :]
            to_y[at, :] = (mixed_grad * state[pl.ds(first + 8, 64), :] * slope).astype(jnp.bfloat16)
            local[at, :] = mixed_grad * value

        tiles(8, 64, gelu_tile)
        prod, value = local_scan(
            lambda first: carry[pl.ds(first, 16), :][1:9],
            lambda first: local[pl.ds(first, 8), :],
            sums,
            prods,
            True,
        )
        slots[me, 0:1, :] = carry[0:1, :] * prod[0:1]
        slots[me, 1:2, :] = carry[0:1, :] * value[0:1]
        copies = start_share(slots, slot_send, slot_recv)
        down_sum.turn()

        weight_grad(outy_grad, [(rounded, mixed), (normed_one, to_y)])
        for copy in copies:
            copy.wait()
        up_sum.middle()
        later = jnp.zeros((1, WIDTH), jnp.float32)
        for place_at in range(N_DP - 1, 0, -1):
            longer = slots[place_at, 0:1, :] * later + slots[place_at, 1:2, :]
            later = jnp.where(place_at > me, longer, later)
        plus, decay_slope = chan[5:6, :], chan[6:7, :]
        zero_row = jnp.zeros((1, WIDTH), jnp.float32)

        def gate_tile(first, decay_grad):
            at = pl.ds(first, 64)
            total = sums[at, :] + prods[at, :] * later
            near = state[pl.ds(first, 72), :]
            conv = lax.dot_general(
                window[at, :], place_matrix(shift), (((1,), (1,)), ((), ())), preferred_element_type=jnp.float32
            )
            reset = flags[at, 4:5] > 0.0
            gate_a, gate_x = jax.nn.sigmoid(pre_a[at, :]), jax.nn.sigmoid(pre_x[at, :])
            log_a = -8.0 * gate_a * plus
            keep = jnp.exp(log_a)
            scale = jnp.sqrt(one_less_exp(2.0 * log_a))
            scale_here = jnp.where(reset, 1.0, scale)
            conv_grad[at, :] = total * gate_x * scale_here
            to_gx[at, :] = (total * conv * scale_here * gate_x * (1.0 - gate_x)).astype(jnp.bfloat16)
            log_grad = total * near[7:71] * keep - total * conv * gate_x * keep * keep / scale
            log_grad = jnp.where(reset, 0.0, log_grad)
            to_a[at, :] = (log_grad * (-8.0 * plus) * gate_a * (1.0 - gate_a)).astype(jnp.bfloat16)
            return decay_grad + jnp.sum(log_grad * (-8.0 * gate_a), axis=0, keepdims=True)

        decay_grad = lax.fori_loop(
            0, 8, lambda i, held: gate_tile(pl.multiple_of(i * 64, 64), held), zero_row
        )
        decay_grad = decay_grad * decay_slope

        def window_tile(first):
            at = pl.ds(first, 128)
            total = matmul(to_a[at, :], wide[0]) + matmul(to_gx[at, :], wide[1])
            window_grad[at, :] = total
            low[at, :] = total[:, 0:BLOCK].astype(jnp.bfloat16)
            high[at, :] = total[:, BLOCK : 2 * BLOCK].astype(jnp.bfloat16)

        tiles(4, 128, window_tile)
        up, down = beside_peers()
        to_up = remote(high, low_in, side_send.at[0], side_recv.at[0], up)
        to_down = remote(low, high_in, side_send.at[1], side_recv.at[1], down)
        to_up.start()
        to_down.start()
        column = lax.broadcasted_iota(jnp.int32, (BLOCK, WIDTH), 1)
        chosen = []
        for right in (to_a, to_gx):
            both = transposed_times(window[...], right[...])
            chosen.append(
                jnp.where(column + shift < BLOCK, both[0:BLOCK], both[BLOCK : 2 * BLOCK])
            )
        blocks_grad[...] = jnp.concatenate(chosen, 1).reshape(4, 4, 2, GATE_HALF, 2 * WIDTH)
        down_sum.finish(share_stage)
        keep_share(0)
        for peer in ring_peers():
            pl.semaphore_signal(reuse_sem, inc=1, device_id=peer, device_id_type=MESH)
        to_up.wait()
        to_down.wait()

        def conv_tile(first):
            at = pl.ds(first, 64)
            from_low = jnp.where(shift != 0, low_in[at, :].astype(jnp.float32), 0.0)
            from_high = jnp.where(shift != 192, high_in[at, :].astype(jnp.float32), 0.0)
            total = window_grad[at, :] + jnp.concatenate([from_low, from_high], 1)
            total = pltpu.roll(total, lax.rem(2 * BLOCK - shift, 2 * BLOCK), 1)
            conv_grad[at, :] = conv_grad[at, :] + total[:, 0:WIDTH]

        tiles(8, 64, conv_tile)
        conv_grad[ROWS : ROWS + 8, :] = jnp.zeros((8, WIDTH), jnp.float32)
        head = conv_grad[0:8, :]
        rows = []
        for row in range(3):
            total = zero_row
            for tap in range(3 - row, 4):
                from_row = row - 3 + tap
                counted = flags[from_row : from_row + 1, tap : tap + 1] > 0.0
                total = total + chan[tap : tap + 1, :] * jnp.where(
                    counted, head[from_row : from_row + 1], 0.0
                )
            rows.append(total)
        halo[0:5, :] = jnp.zeros((5, WIDTH), jnp.float32)
        for row in range(3):
            halo[5 + row : 6 + row, :] = rows[row]
        send_halo = remote(halo, halo_in, halo_send, halo_recv, {"dp": lax.rem(me + N_DP - 1, N_DP)})
        send_halo.start()
        blocks_sum.start()

        def tap_tile(first, held):
            at = pl.ds(first, 64)
            near = conv_grad[pl.ds(first, 72), :]
            marks = flags[pl.ds(first, 72), :]
            behind = ext[pl.ds(first + 8, 72), :]
            total = chan[0:1, :] * near[0:64]
            taps = [held[0] + jnp.sum(near[0:64] * behind[8:72], axis=0, keepdims=True)]
            for tap in range(1, 4):
                counted = marks[tap : tap + 64, tap : tap + 1] > 0.0
                total = total + chan[tap : tap + 1, :] * jnp.where(counted, near[tap : tap + 64], 0.0)
                here = jnp.where(marks[0:64, tap : tap + 1] > 0.0, near[0:64], 0.0)
                taps.append(
                    held[tap] + jnp.sum(here * behind[8 - tap : 72 - tap], axis=0, keepdims=True)
                )
            local[at, :] = total
            return tuple(taps)

        tap_grads = lax.fori_loop(
            0, 8, lambda i, held: tap_tile(pl.multiple_of(i * 64, 64), held), (zero_row,) * 4
        )
        for tap in range(4):
            chan_dp[me, tap : tap + 1, :] = tap_grads[tap]
        chan_dp[me, 4:5, :] = decay_grad
        chan_dp[me, 5:8, :] = jnp.zeros((3, WIDTH), jnp.float32)
        channel_copies = start_share(chan_dp, c_send, c_recv)
        pl.semaphore_wait(reuse_sem, 6)
        outy_sum.start()
        gate_sum.middle()
        out[...] = (residual[...] + summed_out.finish()).astype(jnp.bfloat16)
        for peer in tensor_peers():
            pl.semaphore_signal(free_sem, inc=1, device_id=peer, device_id_type=MESH)
        send_halo.wait()
        local[ROWS - 8 : ROWS, :] = local[ROWS - 8 : ROWS, :] + halo_in[...]
        to_x = to_a
        to_x[...] = local[...].astype(jnp.bfloat16)

        def produce(by):
            at = pl.ds(pl.multiple_of(chip_row(by, 0), 128), 128)
            total = matmul(to_x[at, :], branch_w[0]) + matmul(to_y[at, :], branch_w[1])
            partial[at, :] = total.astype(jnp.bfloat16)

        pl.semaphore_wait(free_sem, 4)
        summed_last.start(produce)
        weight_grad(bx_grad, [(normed_one, to_x)])
        bx_sum.start()
        outy_sum.middle()
        up_sum.turn()
        blocks_sum.middle()
        norm_grad = summed_last.finish()
        before_norm, gain_part = norm_back(own[...].astype(jnp.float32), gains[0:1, :], norm_grad)
        tokens_grad[...] = (grad[...] + before_norm).astype(jnp.bfloat16)
        gain_t[index, 0:1, :] = gain_part
        gain_t[index, 1:2, :] = grad_gain_two[...]
        gain_copies = []
        for by in range(1, N_T):
            copy = remote(
                gain_t.at[index],
                gain_t.at[index],
                t_send.at[by],
                t_recv.at[by],
                {"tensor": lax.rem(index + by, N_T)},
            )
            copy.start()
            gain_copies.append(copy)
        gate_sum.turn()
        bx_sum.middle()
        for copy in gain_copies:
            copy.wait()
        total = gain_t[0]
        for by in range(1, N_T):
            total = total + gain_t[by]
        gain_dp[me] = total
        gain_copies = start_share(gain_dp, g_send, g_recv)
        up_sum.finish(share_stage)
        keep_share(1)
        outy_sum.turn()
        blocks_sum.turn()
        gate_sum.finish(share_stage)
        keep_share(2)
        bx_sum.turn()
        for copy in channel_copies + gain_copies:
            copy.wait()
        total, channels = gain_dp[0], chan_dp[0]
        for by in range(1, N_DP):
            total = total + gain_dp[by]
            channels = channels + chan_dp[by]
        gain_sum[...] = total
        channel_sum[...] = channels
        outy_sum.finish(share_stage.at[:, pl.ds(0, 640)])
        blocks_sum.finish(blocks_share)
        bx_sum.finish(share_stage.at[:, pl.ds(640, 384)])
        keep_share(3)


    wide_f32 = pltpu.VMEM((ROWS, WIDTH), f32)
    wide_bf16 = pltpu.VMEM((ROWS, WIDTH), bf16)
    pl.run_scoped(
        mixer_part,
        *(pltpu.VMEM(*shape) for shape in saved_shapes()),
        pltpu.VMEM((WIDTH, D), bf16),
        pltpu.VMEM((2, WIDTH, D), bf16),
        pltpu.VMEM((2, WIDTH, BLOCK), bf16),
        pltpu.VMEM((OWN, D), bf16),
        pltpu.VMEM((2, WIDTH, 2 * BLOCK), bf16),
        wide_bf16,
        wide_f32,
        wide_f32,
        wide_f32,
        wide_bf16,
        wide_bf16,
        pltpu.VMEM((ROWS, 2 * BLOCK), f32),
        pltpu.VMEM((ROWS, BLOCK), bf16),
        pltpu.VMEM((ROWS, BLOCK), bf16),
        pltpu.VMEM((ROWS + 8, WIDTH), f32),
    )


def backward(block, residual, gains, chan, flags, dy, ffn_t, down, tokens, out_proj, branch_t, gates_t, saved):
    f32, bf16 = jnp.float32, jnp.bfloat16
    dma = pltpu.SemaphoreType.DMA
    here = pl.BlockSpec(memory_space=pltpu.VMEM)
    there = pl.BlockSpec(memory_space=pl.ANY)
    share = jax.ShapeDtypeStruct((2 * HALF, 1024), f32)

    def shared(columns):
        return jax.ShapeDtypeStruct((4, 4, 2, HALF, columns), bf16)

    return pl.pallas_call(
        back_kernel,
        out_shape=(
            jax.ShapeDtypeStruct((OWN, D), bf16),
            jax.ShapeDtypeStruct((OWN, D), bf16),
            jax.ShapeDtypeStruct((2, D), f32),
            jax.ShapeDtypeStruct((8, WIDTH), f32),
            jax.ShapeDtypeStruct((2 * GATE_HALF, 2 * WIDTH), f32),
            *[share] * 4,
            *[shared(1024)] * 3,
            shared(640),
            shared(384),
        ),
        in_specs=[here] * 5 + [there] * 16,
        out_specs=tuple([here] * 5 + [there] * 9),
        scratch_shapes=[
            pltpu.VMEM((ROWS, D), bf16),
            pltpu.VMEM((ROWS, D), bf16),
            pltpu.VMEM((OWN, D), f32),
            pltpu.VMEM((1, D), f32),
            pltpu.VMEM((ROWS, D), bf16),
            pltpu.VMEM((4, 2, HALF, 1024), bf16),
            pltpu.VMEM((2 * HALF, 1024), f32),
            pltpu.VMEM((2, 2, HALF, 1024), bf16),
            pltpu.VMEM((2, 2, GATE_HALF, 2 * WIDTH), f32),
            pltpu.VMEM((ROWS, BLOCK), bf16),
            pltpu.VMEM((ROWS, BLOCK), bf16),
            pltpu.VMEM((N_DP, 8, WIDTH), f32),
            pltpu.VMEM((8, WIDTH), f32),
            pltpu.VMEM((8, WIDTH), f32),
            pltpu.VMEM((N_T, 2, D), f32),
            pltpu.VMEM((N_DP, 2, D), f32),
            pltpu.VMEM((N_DP, 8, WIDTH), f32),
            pltpu.VMEM((4, 4, 2, GATE_HALF, 2 * WIDTH), f32),
            dma((13,)),
            dma,
            dma,
            dma((N_DP,)),
            dma((N_DP,)),
            dma((2,)),
            dma((2,)),
            dma,
            dma,
            dma((N_T,)),
            dma((N_T,)),
            dma((N_DP,)),
            dma((N_DP,)),
            dma((N_DP,)),
            dma((N_DP,)),
            pltpu.SemaphoreType.REGULAR,
            pltpu.SemaphoreType.REGULAR,
        ]
        + reduce_scratch()
        + gather_scratch()
        + gather_scratch()
        + data_buffers(HALF, 1024, bf16)
        + data_sems()
        + data_buffers(HALF, 1024, bf16)
        + data_sems()
        + data_buffers(HALF, 1024, bf16)
        + data_sems()
        + data_sems()
        + data_sems()
        + data_buffers(GATE_HALF, 2 * WIDTH, f32)
        + data_sems(),
        compiler_params=params(2),
    )(block, residual, gains, chan, flags, dy, ffn_t, down, tokens, out_proj, branch_t, gates_t, *saved)


def rms_norm(values, gain):
    return values * lax.rsqrt(jnp.mean(values * values, axis=-1, keepdims=True) + NORM_EPS) * gain


def matmul(left, right):
    return jnp.dot(left, right, preferred_element_type=jnp.float32)


def times_transposed(left, right):
    return lax.dot_general(
        left, right, (((1,), (1,)), ((), ())), preferred_element_type=jnp.float32
    )


def transposed_times(left, right):
    return lax.dot_general(
        left, right, (((0,), (0,)), ((), ())), preferred_element_type=jnp.float32
    )


def adam_step(weight, grad, first, second, rate, decay):
    first_new = BETA_ONE * first + (1.0 - BETA_ONE) * grad
    second_new = BETA_TWO * second + (1.0 - BETA_TWO) * grad * grad
    first_hat = first_new / (1.0 - BETA_ONE**STEP)
    second_hat = second_new / (1.0 - BETA_TWO**STEP)
    weight_new = weight - rate * (first_hat / (jnp.sqrt(second_hat) + ADAM_EPS) + decay * weight)
    return (first_new, second_new, weight_new)


SHARE = 2 * HALF
SPAN = 384
DECAY = 0.1
BRANCH_RATE, GATE_RATE, OUT_RATE = 3.0 * D**-0.5, 3.0 * BLOCK**-0.5, 3.0 * (L // 8) ** -0.5
FFN_RATE, DOWN_RATE = 3.0 * D**-0.5, 3.0 * (F // 2) ** -0.5


def update_jobs():
    return (
        ("down", None, 0, 0, HIDE, 0, DOWN_RATE),
        ("ffn", 1, 1, 0, HIDE, HIDE, FFN_RATE),
        ("ffn", 0, 2, 0, HIDE, 0, FFN_RATE),
        ("out", None, 3, 0, WIDTH, 0, OUT_RATE),
        ("branch", 1, 3, WIDTH, WIDTH, WIDTH, BRANCH_RATE),
        ("branch", 0, 3, 2 * WIDTH, WIDTH, 0, BRANCH_RATE),
        ("gate", 0, 4, 0, WIDTH, 0, GATE_RATE),
        ("gate", 1, 4, WIDTH, WIDTH, WIDTH, GATE_RATE),
    )


ARRAYS = ("down", "ffn", "out", "branch", "gate")


def update_kernel(*refs):
    shares, weights = refs[:5], dict(zip(ARRAYS, refs[5:10]))
    moments = {name: refs[10 + 2 * i : 12 + 2 * i] for i, name in enumerate(ARRAYS)}
    outs = {name: refs[20 + 3 * i : 23 + 3 * i] for i, name in enumerate(ARRAYS)}
    windows = dict(zip(ARRAYS, refs[35:40]))
    held = refs[40:48]
    in_sem, window_sem, out_sem = refs[48:]
    me = lax.axis_index("dp")
    begin = jnp.minimum(me * SHARE // 128 * 128, D - SPAN)
    copies = {}

    def copy(key, source, target, sem):
        copies[key] = pltpu.make_async_copy(source, target, sem)
        copies[key].start()

    jobs = update_jobs()
    waiting = list(ARRAYS)
    for number, (name, part, *_) in enumerate(jobs):
        if name not in copies:
            source = weights[name]
            if name != "gate":
                source = source.at[:, pl.ds(pl.multiple_of(begin, 128), SPAN)]
            copy(name, source, windows[name], window_sem.at[ARRAYS.index(name)])
        for which in range(2):
            source = moments[name][which]
            source = source if part is None else source.at[part]
            copy((number, which), source, held[number].at[which], in_sem.at[number, which])
    for number, (name, part, share, lane, width, row, rate) in enumerate(jobs):
        if name in waiting:
            waiting.remove(name)
            copies[name].wait()
        count = 16 if name == "gate" else SHARE
        span = BLOCK if name == "gate" else SPAN
        offset = me * count if name == "gate" else me * SHARE - begin
        mine = lax.broadcasted_iota(jnp.int32, (count, span), 0) + offset
        lanes = lax.broadcasted_iota(jnp.int32, (count, span), 1)
        chosen = jnp.where(lanes == mine, 1.0, 0.0).astype(jnp.bfloat16)
        box = held[number]
        box[2] = times_transposed(chosen, windows[name][row : row + width, :])
        for which in range(2):
            copies[number, which].wait()

        def body(first, box=box, share=share, lane=lane, width=width, rate=rate):
            at = pl.ds(first, 16)
            grad = shares[share][at, lane : lane + width]
            new = adam_step(box[2, at, :], grad, box[0, at, :], box[1, at, :], rate, DECAY)
            for which in range(3):
                box[which, at, :] = new[which]

        tiles(count // 16, 16, body)
        for which in range(3):
            target = outs[name][which]
            target = target if part is None else target.at[part]
            copy((number, which), box.at[which], target, out_sem.at[number, which])
    for number in range(len(jobs)):
        for which in range(3):
            copies[number, which].wait()


def update_weights(shares, weights, moments):
    f32, bf16 = jnp.float32, jnp.bfloat16
    dma = pltpu.SemaphoreType.DMA
    here = pl.BlockSpec(memory_space=pltpu.VMEM)
    there = pl.BlockSpec(memory_space=pl.ANY)
    jobs = update_jobs()
    return pl.pallas_call(
        update_kernel,
        out_shape=tuple(
            jax.ShapeDtypeStruct(moments[2 * i].shape, f32) for i in range(5) for _ in range(3)
        ),
        in_specs=[here] * 5 + [there] * 15,
        out_specs=tuple([there] * 15),
        scratch_shapes=[
            pltpu.VMEM((weight.shape[0], BLOCK if name == "gate" else SPAN), bf16)
            for name, weight in zip(ARRAYS, weights)
        ]
        + [pltpu.VMEM((3, 16 if job[0] == "gate" else SHARE, job[4]), f32) for job in jobs]
        + [dma((len(jobs), 2)), dma((5,)), dma((len(jobs), 3))],
        compiler_params=pltpu.CompilerParams(vmem_limit_bytes=63 * 2**20),
    )(*shares, *weights, *moments)


def shards(
    tokens,
    cotangent,
    segments,
    gains,
    channel_params,
    branch_in,
    gate_blocks,
    out_proj,
    ffn_in,
    ffn_down,
    gains_first,
    gains_second,
    channel_first,
    channel_second,
    branch_first,
    branch_second,
    gate_first,
    gate_second,
    out_first,
    out_second,
    ffn_in_first,
    ffn_in_second,
    down_first,
    down_second,
):
    rows = ROWS
    data_index = lax.axis_index("dp")

    padded_ids = jnp.concatenate([jnp.full((3,), -1, jnp.int32), segments])
    local_ids = lax.dynamic_slice_in_dim(padded_ids, data_index * rows, rows + 3)
    marks = [local_ids[3 - tap : 3 - tap + rows] == local_ids[3:] for tap in range(4)]
    marks.append(local_ids[3:] != local_ids[2 : 2 + rows])
    flags = jnp.pad(jnp.stack(marks, 1).astype(jnp.float32), ((0, 8), (0, 3)))
    decay_param = channel_params[4:5]
    chan = jnp.concatenate(
        [channel_params, jax.nn.softplus(decay_param), jax.nn.sigmoid(decay_param), decay_param], 0
    )
    branch_t = branch_in.swapaxes(1, 2)
    gates_t = gate_blocks.swapaxes(1, 2)
    ffn_t = ffn_in.swapaxes(1, 2).reshape(2 * HIDE, D)
    residual_own, block, *saved = mixer_forward(
        tokens, branch_t, gates_t, out_proj, chan, gains, flags
    )
    tokens_grad, block_out, gain_grad, channel_grad, blocks_share, down_share, up_share, gate_share, mixer_share, *_ = (
        backward(
            block,
            residual_own,
            gains,
            chan,
            flags,
            cotangent,
            ffn_t,
            ffn_down,
            tokens,
            out_proj,
            branch_t,
            gates_t,
            saved,
        )
    )
    channel_rate = jnp.array([1.0, 1.0, 1.0, 1.0, 3.0], jnp.float32)[:, None]
    gains_out = adam_step(gains, gain_grad, gains_first, gains_second, 1.0, 0.0)
    channel_out = adam_step(
        channel_params, channel_grad[:5], channel_first, channel_second, channel_rate, 0.0
    )
    new = update_weights(
        (down_share, up_share, gate_share, mixer_share, blocks_share),
        (
            ffn_down,
            ffn_t,
            out_proj,
            branch_t.reshape(2 * WIDTH, D),
            gates_t.reshape(2 * WIDTH, BLOCK),
        ),
        (
            down_first.T,
            down_second.T,
            ffn_in_first,
            ffn_in_second,
            out_first.T,
            out_second.T,
            branch_first,
            branch_second,
            gate_first,
            gate_second,
        ),
    )
    return (
        block_out,
        tokens_grad,
        *gains_out,
        *channel_out,
        *new[9:12],
        *new[12:15],
        *(value.T for value in new[6:9]),
        *new[3:6],
        *(value.T for value in new[0:3]),
    )


def solution(mesh):
    weights = [
        P(None, None, "tensor"),
        P(None, None, "tensor"),
        P("tensor", None),
        P(None, None, "tensor"),
        P("tensor", None),
    ]
    owned = [
        P(None, "dp", "tensor"),
        P(None, "dp", "tensor"),
        P("tensor", "dp"),
        P(None, "dp", "tensor"),
        P("tensor", "dp"),
    ]
    moments = [P(), P(None, "tensor")] + owned
    placed = [P("dp", None), P("dp", None), P(), P(), P(None, "tensor")] + weights
    for spec in moments:
        placed += [spec, spec]
    outs = [P(("dp", "tensor"), None)] * 2
    for spec in moments:
        outs += [spec, spec, spec]
    return jax.shard_map(
        shards, mesh=mesh, in_specs=tuple(placed), out_specs=tuple(outs), check_vma=False
    )
```

```python
import functools

import jax
import jax.numpy as jnp
from jax import lax
from jax.experimental import pallas as pl
from jax.experimental.pallas import tpu as pltpu
from jax.sharding import PartitionSpec as P

D = 2560
L = 2560
BLOCK = 256
F = 7680
STEP = 10
N_DP = 16
N_T = 8
ROWS = 512
OWN = ROWS // N_T
WIDTH = L // N_T
HIDE = F // N_T
HALF = 80
GATE_HALF = 8
MESH = pl.DeviceIdType.MESH

NORM_EPS = 1e-06
ADAM_EPS = 1e-08
BETA_ONE = 0.9
BETA_TWO = 0.95


def params(cid):
    return pltpu.CompilerParams(
        collective_id=cid, has_side_effects=True, vmem_limit_bytes=63 * 2**20
    )


def vmem(count):
    return [pl.BlockSpec(memory_space=pltpu.VMEM)] * count


def announce(peers):
    barrier = pltpu.get_barrier_semaphore()
    for peer in peers:
        pl.semaphore_signal(barrier, inc=1, device_id=peer, device_id_type=MESH)
    return lambda: pl.semaphore_wait(barrier, len(peers))


def remote(source, target, send_sem, recv_sem, peer):
    return pltpu.make_async_remote_copy(
        src_ref=source,
        dst_ref=target,
        send_sem=send_sem,
        recv_sem=recv_sem,
        device_id=peer,
        device_id_type=MESH,
    )


class Later:
    def __init__(self, make):
        self.make = make

    def start(self):
        self.make().start()

    def wait(self):
        self.make().wait()

    def wait_send(self):
        self.make().wait_send()

    def wait_recv(self):
        self.make().wait_recv()


def place():
    index = lax.axis_index("tensor")
    return index // 2, lax.rem(index, 2)


def at_x(x, core, by):
    return {"tensor": lax.rem(x + by, 4) * 2 + core}


def tensor_peers():
    x, core = place()
    return [{"tensor": x * 2 + 1 - core}] + [at_x(x, core, by) for by in (1, 2, 3)]


def chip_row(by, which):
    x, _ = place()
    return pl.multiple_of((lax.rem(x + by, 4) * 2 + which) * OWN, OWN)


ARRIVAL = {0: 0, 1: 1, 3: 2, 2: 3}


def arrival_row(by, which):
    return pl.multiple_of((ARRIVAL[by % 4] * 2 + which) * OWN, OWN)


class TensorSum:
    ORDER = (2, 1, 3, 0)

    def __init__(self, row, partial, pair, held, landed, pair_send, pair_recv, x_send, x_recv):
        self.row = row
        self.partial, self.pair, self.held, self.landed = partial, pair, held, landed
        self.sems = pair_send, pair_recv, x_send, x_recv
        self.pair_copies, self.x_copies = {}, {}

    def give(self, by):
        def make():
            x, core = place()
            return remote(
                self.partial.at[pl.ds(self.row(by, 1 - core), OWN)],
                self.pair.at[by],
                self.sems[0].at[by],
                self.sems[1].at[by],
                {"tensor": x * 2 + 1 - core},
            )

        self.pair_copies[by] = Later(make)
        self.pair_copies[by].start()

    def pass_on(self, by):
        _, core = place()
        self.pair_copies[by].wait_recv()
        mine = self.partial[pl.ds(self.row(by, core), OWN), :].astype(jnp.float32)
        self.held[by - 1] = (mine + self.pair[by].astype(jnp.float32)).astype(jnp.bfloat16)

        def make():
            x, core = place()
            return remote(
                self.held.at[by - 1],
                self.landed.at[by - 1],
                self.sems[2].at[by - 1],
                self.sems[3].at[by - 1],
                at_x(x, core, by),
            )

        self.x_copies[by] = Later(make)
        self.x_copies[by].start()

    def start(self, produce):
        for step, by in enumerate(self.ORDER):
            produce(by)
            self.give(by)
            if step:
                self.pass_on(self.ORDER[step - 1])

    def finish(self):
        _, core = place()
        self.pair_copies[0].wait_recv()
        total = self.partial[pl.ds(self.row(0, core), OWN), :].astype(jnp.float32)
        total = total + self.pair[0].astype(jnp.float32)
        for by in (1, 3, 2):
            self.x_copies[by].wait_recv()
            total = total + self.landed[by - 1].astype(jnp.float32)
        for by in self.ORDER:
            self.pair_copies[by].wait_send()
        for by in (2, 1, 3):
            self.x_copies[by].wait_send()
        return total


def reduce_scratch():
    return [
        pltpu.VMEM((4, OWN, D), jnp.bfloat16),
        pltpu.VMEM((3, OWN, D), jnp.bfloat16),
        pltpu.VMEM((3, OWN, D), jnp.bfloat16),
        pltpu.SemaphoreType.DMA((4,)),
        pltpu.SemaphoreType.DMA((4,)),
        pltpu.SemaphoreType.DMA((3,)),
        pltpu.SemaphoreType.DMA((3,)),
    ]


class TensorGather:
    def __init__(self, row, whole, x_send, x_recv, pair_send, pair_recv):
        self.row, self.whole, self.sems = row, whole, (x_send, x_recv, pair_send, pair_recv)

    def at(self, by):
        _, core = place()
        return self.whole.at[pl.ds(self.row(by, core), OWN)]

    def start(self, block):
        _, core = place()
        self.whole[pl.ds(self.row(0, core), OWN), :] = block
        self.sends, self.pairs = [], {}
        for by in (1, 3, 2):

            def make(by=by):
                x, core = place()
                mine = self.at(0)
                target = mine if self.row is chip_row else self.at(4 - by)
                return remote(
                    mine,
                    target,
                    self.sems[0].at[by - 1],
                    self.sems[1].at[by - 1],
                    at_x(x, core, by),
                )

            self.sends.append(Later(make))
            self.sends[-1].start()
        self.hand(0)

    def hand(self, by):
        def make():
            x, core = place()
            block = self.at(by)
            return remote(
                block,
                block,
                self.sems[2].at[by],
                self.sems[3].at[by],
                {"tensor": x * 2 + 1 - core},
            )

        self.pairs[by] = Later(make)
        self.pairs[by].start()

    def arrive(self, by):
        x, core = place()
        sender = 4 - by
        block = self.at(by)
        remote(
            block,
            block,
            self.sems[0].at[sender - 1],
            self.sems[1].at[sender - 1],
            at_x(x, core, sender),
        ).wait_recv()
        self.hand(by)

    def settle(self, by):
        self.pairs[by].wait_recv()

    def finish(self):
        for copy in self.sends:
            copy.wait_send()
        for copy in self.pairs.values():
            copy.wait_send()


class DataSum:
    LOW, HIGH = pl.ds(0, 2), pl.ds(2, 2)

    def __init__(self, grad, own, via, ring, last, near, send, recv, local, rows):
        self.grad, self.own, self.near, self.via = grad, own, near, via
        self.ring, self.last, self.rows = ring, last, rows
        self.send, self.recv, self.local = send, recv, local
        self.copies = {}

    def spots(self, half):
        me = lax.axis_index("dp")
        z, y = me // 4, lax.rem(me, 4)
        return (y, z) if half == 0 else (z, y)

    def peer(self, half, first_by, second_by):
        first, second = self.spots(half)
        a, b = lax.rem(first + first_by + 4, 4), lax.rem(second + second_by + 4, 4)
        return {"dp": b * 4 + a if half == 0 else a * 4 + b}

    def block(self, half, by, part):
        a = lax.rem(self.spots(half)[0] + by + 4, 4)
        return self.grad.at[part, a, 0] if half == 0 else self.grad.at[a, part, 1]

    def ship(self, half, slot, source, target, first_by, second_by):
        def make():
            return remote(
                source(),
                target(),
                self.send.at[half, slot],
                self.recv.at[half, slot],
                self.peer(half, first_by, second_by),
            )

        self.copies[half, slot] = Later(make)
        self.copies[half, slot].start()

    def own_load(self, half):
        return pltpu.make_async_copy(
            self.block(half, 0, pl.ds(0, 4)), self.own.at[half], self.local.at[half, 2]
        )

    def start(self):
        for half in (0, 1):
            self.ship(
                half, 0, lambda half=half: self.block(half, 2, self.LOW), lambda half=half: self.via.at[half, 0], 1, 0
            )
            self.ship(
                half, 1, lambda half=half: self.block(half, 2, self.HIGH), lambda half=half: self.via.at[half, 1], -1, 0
            )
            self.own_load(half).start()
        for half in (0, 1):
            self.ship(
                half, 2, lambda half=half: self.block(half, 1, self.HIGH), lambda half=half: self.ring.at[half, 0], 1, 0
            )
            self.ship(
                half, 3, lambda half=half: self.block(half, -1, self.LOW), lambda half=half: self.ring.at[half, 1], -1, 0
            )

    def add(self, target, sources, blocks):
        for block in range(blocks):
            if len(sources) == 1:
                target[block] = target[block] + sources[0][block]
                continue
            total = target[block].astype(jnp.float32)
            for source in sources:
                total = total + source[block].astype(jnp.float32)
            target[block] = total.astype(target.dtype)

    def middle(self):
        for half in (0, 1):
            loads = []
            for side, (by, part) in enumerate(((1, self.LOW), (-1, self.HIGH))):
                load = pltpu.make_async_copy(
                    self.block(half, by, part), self.near.at[side], self.local.at[half, side]
                )
                load.start()
                loads.append(load)
            for side in (0, 1):
                loads[side].wait()
                self.copies[half, side].wait_recv()
                via = self.via.at[half, side]
                self.add(via, [self.near.at[side]], 2)
                self.ship(
                    half,
                    4 + side,
                    lambda half=half, side=side: self.via.at[half, side],
                    lambda half=half, side=side: self.ring.at[half, 2 + side],
                    1 - 2 * side,
                    0,
                )

    def turn(self):
        for half in (0, 1):
            self.own_load(half).wait()
            for slot in (2, 3, 4, 5):
                self.copies[half, slot].wait_recv()
            ring = self.ring
            self.add(self.own.at[half, self.LOW], [ring.at[half, 1], ring.at[half, 2]], 2)
            self.add(self.own.at[half, self.HIGH], [ring.at[half, 0], ring.at[half, 3]], 2)
            for by in (1, 2, 3):
                self.ship(
                    half,
                    5 + by,
                    lambda half=half, by=by: self.own.at[
                        half, lax.rem(self.spots(half)[1] + by, 4)
                    ],
                    lambda half=half, by=by: self.last.at[half, by - 1],
                    0,
                    by,
                )

    def finish(self, share):
        for half in (0, 1):
            for by in (1, 2, 3):
                self.copies[half, 5 + by].wait_recv()
            total = self.own[half, self.spots(half)[1]].astype(jnp.float32)
            for by in range(3):
                total = total + self.last[half, by].astype(jnp.float32)
            share[half * self.rows : (half + 1) * self.rows, :] = total
        for copy in self.copies.values():
            copy.wait_send()


def data_buffers(rows, columns, dtype):
    return [
        pltpu.VMEM((2, 4, rows, columns), dtype),
        pltpu.VMEM((2, 2, 2, rows, columns), dtype),
        pltpu.VMEM((2, 4, 2, rows, columns), dtype),
        pltpu.VMEM((2, 3, rows, columns), dtype),
    ]


def data_sems():
    dma = pltpu.SemaphoreType.DMA
    return [dma((2, 9)), dma((2, 9)), dma((2, 3))]


def ring_peers():
    me = lax.axis_index("dp")
    z, y = me // 4, lax.rem(me, 4)
    along_y = [{"dp": z * 4 + lax.rem(y + by, 4)} for by in (1, 2, 3)]
    return along_y + [{"dp": lax.rem(z + by, 4) * 4 + y} for by in (1, 2, 3)]


def gather_scratch():
    return [
        pltpu.SemaphoreType.DMA((3,)),
        pltpu.SemaphoreType.DMA((3,)),
        pltpu.SemaphoreType.DMA((4,)),
        pltpu.SemaphoreType.DMA((4,)),
    ]


def dp_peers():
    me = lax.axis_index("dp")
    return [{"dp": lax.rem(me + by, N_DP)} for by in range(1, N_DP)]


def place_matrix(shift):
    row = lax.broadcasted_iota(jnp.int32, (WIDTH, 2 * BLOCK), 0)
    lane = lax.broadcasted_iota(jnp.int32, (WIDTH, 2 * BLOCK), 1)
    return jnp.where(lane == row + shift, 1.0, 0.0).astype(jnp.bfloat16)


def wide_gates(gates, wide, shift):
    row = lax.broadcasted_iota(jnp.int32, (WIDTH, BLOCK), 0)
    low = row + shift < BLOCK
    for gate in range(2):
        matrix = gates[gate].astype(jnp.float32)
        wide[gate, :, 0:BLOCK] = jnp.where(low, matrix, 0.0).astype(jnp.bfloat16)
        wide[gate, :, BLOCK : 2 * BLOCK] = jnp.where(low, 0.0, matrix).astype(jnp.bfloat16)


def one_less_exp(z):
    series = 1.0 + z / 7.0
    for term in (6.0, 5.0, 4.0, 3.0, 2.0):
        series = 1.0 + z / term * series
    return jnp.where(z > -0.35, -z * series, 1.0 - jnp.exp(z))


def tiles(count, size, body, unroll=1):
    def step(index, _):
        body(pl.multiple_of(index * size, size))
        return 0

    lax.fori_loop(0, count, step, 0, unroll=unroll)


def norm_rows(source, target, gain, rows):
    def body(first):
        at = pl.ds(first, 16)
        target[at, :] = rms_norm(source[at, :].astype(jnp.float32), gain).astype(jnp.bfloat16)

    tiles(rows // 16, 16, body, min(4, rows // 16))


def shifted(values, by, fill, reverse):
    count = values.shape[0]
    row = lax.broadcasted_iota(jnp.int32, values.shape, 0)
    if reverse:
        return jnp.where(row < count - by, pltpu.roll(values, count - by, 0), fill)
    return jnp.where(row >= by, pltpu.roll(values, by, 0), fill)


def local_scan(factor_at, term_at, values, prods, reverse):
    def step(index, held):
        prod, value = held
        first = pl.multiple_of((ROWS // 8 - 1 - index if reverse else index) * 8, 8)
        factor, term = factor_at(first), term_at(first)
        for by in (1, 2, 4):
            term = term + factor * shifted(term, by, 0.0, reverse)
            factor = factor * shifted(factor, by, 1.0, reverse)
        value = factor * value + term
        prod = factor * prod
        values[pl.ds(first, 8), :] = value
        prods[pl.ds(first, 8), :] = prod
        last = 0 if reverse else 7
        return (
            jnp.broadcast_to(prod[last : last + 1], prod.shape),
            jnp.broadcast_to(value[last : last + 1], value.shape),
        )

    ones = jnp.ones((8, WIDTH), jnp.float32)
    return lax.fori_loop(0, ROWS // 8, step, (ones, jnp.zeros_like(ones)), unroll=8)


def start_share(slots, send, recv):
    me = lax.axis_index("dp")
    copies = []
    for by in range(1, N_DP):
        copy = remote(
            slots.at[me], slots.at[me], send.at[by], recv.at[by], {"dp": lax.rem(me + by, N_DP)}
        )
        copy.start()
        copies.append(copy)
    return copies


def beside_peers():
    index = lax.axis_index("tensor")
    return {"tensor": lax.rem(index + 1, N_T)}, {"tensor": lax.rem(index + N_T - 1, N_T)}


def far_peer():
    index = lax.axis_index("tensor")
    _, core = place()
    return {"tensor": lax.rem(index + N_T - 1 + 2 * core, N_T)}


def gelu_parts(y):
    c = 0.7978845608028654
    inner = jnp.tanh(c * (y + 0.044715 * y * y * y))
    half = 0.5 * (1.0 + inner)
    slope = half + 0.5 * y * (1.0 - inner * inner) * c * (1.0 + 3 * 0.044715 * y * y)
    return y * half, slope


def forward_kernel(
    tokens, branch_hbm, gates, out_hbm, chan, gains, flags, residual, block, *rest
):
    outs = rest[:9]
    (
        normed_one, ext, window, pre_a, pre_x, carry, state, branch_y, mixed,
        branch_w, out_w, halo, halo_norm, wide, placing, update, values, prods, gelu_y, low, high, slots, partial,
        load_sem, store_sem, halo_send, halo_recv, side_send, side_recv, slot_send, slot_recv, *scratch
    ) = rest[9:]
    me, index = lax.axis_index("dp"), lax.axis_index("tensor")
    shift = lax.rem(index * WIDTH, BLOCK)
    loads = [
        pltpu.make_async_copy(branch_hbm.at[0], branch_w.at[0], load_sem.at[0]),
        pltpu.make_async_copy(branch_hbm.at[1], branch_w.at[1], load_sem.at[1]),
        pltpu.make_async_copy(out_hbm, out_w, load_sem.at[2]),
    ]
    for load in loads:
        load.start()
    ready = announce(dp_peers() + tensor_peers() + [far_peer()])
    stores = []

    def store(number, source, target):
        copy = pltpu.make_async_copy(source, target, store_sem.at[number])
        copy.start()
        stores.append(copy)

    send_halo = remote(
        tokens.at[pl.ds(ROWS - 16, 16)],
        halo,
        halo_send,
        halo_recv,
        {"dp": lax.rem(me + 1, N_DP)},
    )
    wide_gates(gates, wide, shift)
    placing[...] = place_matrix(shift)
    gain = gains[0:1, :]
    norm_rows(tokens, normed_one, gain, ROWS)
    ready()
    send_halo.start()
    store(0, normed_one, outs[0])
    loads[0].wait()

    def branch_tile(first):
        at = pl.ds(first, 128)
        value = times_transposed(normed_one[at, :], branch_w[0])
        ext[pl.ds(first + 16, 128), :] = value.astype(jnp.bfloat16).astype(jnp.float32)

    tiles(4, 128, branch_tile)
    send_halo.wait()
    norm_rows(halo, halo_norm, gain, 16)
    ext[0:16, :] = times_transposed(halo_norm[...], branch_w[0]).astype(jnp.bfloat16).astype(jnp.float32)

    def conv_tile(first):
        near = ext[pl.ds(first + 8, 136), :]
        total = chan[0:1, :] * near[8:]
        for tap in range(1, 4):
            counted = flags[pl.ds(first, 128), tap : tap + 1] > 0.0
            total = total + chan[tap : tap + 1, :] * jnp.where(counted, near[8 - tap : 136 - tap], 0.0)
        window[pl.ds(first, 128), :] = matmul(total.astype(jnp.bfloat16), placing[...]).astype(
            jnp.bfloat16
        )

    tiles(4, 128, conv_tile)
    store(1, ext, outs[1])
    up, down = beside_peers()
    to_up = remote(
        window.at[:, pl.ds(BLOCK, BLOCK)], low, side_send.at[0], side_recv.at[0], up
    )
    to_down = remote(window.at[:, pl.ds(0, BLOCK)], high, side_send.at[1], side_recv.at[1], down)
    to_up.start()
    to_down.start()
    loads[1].wait()

    def gelu_tile(first):
        at = pl.ds(first, 128)
        branch_y[at, :] = times_transposed(normed_one[at, :], branch_w[1])

    tiles(4, 128, gelu_tile)
    store(2, branch_y, outs[6])
    to_up.wait()
    to_down.wait()

    def window_tile(first):
        at = pl.ds(first, 128)
        own_conv = lax.dot_general(
            window[at, :], placing[...], (((1,), (1,)), ((), ())), preferred_element_type=jnp.float32
        )
        from_low = jnp.where(shift != 0, low[at, :].astype(jnp.float32), 0.0)
        from_high = jnp.where(shift != 192, high[at, :].astype(jnp.float32), 0.0)
        whole = window[at, :].astype(jnp.float32) + jnp.concatenate([from_low, from_high], 1)
        whole = whole.astype(jnp.bfloat16)
        window[at, :] = whole
        a = times_transposed(whole, wide[0])
        x = times_transposed(whole, wide[1])
        pre_a[at, :] = a
        pre_x[at, :] = x
        reset = flags[at, 4:5] > 0.0
        log_a = -8.0 * jax.nn.sigmoid(a) * chan[5:6, :]
        carry[at, :] = jnp.where(reset, 0.0, jnp.exp(log_a))
        scale = jnp.where(reset, 1.0, jnp.sqrt(one_less_exp(2.0 * log_a)))
        update[at, :] = own_conv * jax.nn.sigmoid(x) * scale

    tiles(4, 128, window_tile)
    store(3, window, outs[2])
    store(4, pre_a, outs[3])
    store(5, pre_x, outs[4])
    carry[ROWS : ROWS + 8, :] = jnp.ones((8, WIDTH), jnp.float32)
    store(6, carry, outs[5])
    prod, value = local_scan(
        lambda first: carry[pl.ds(first, 8), :],
        lambda first: update[pl.ds(first, 8), :],
        values,
        prods,
        False,
    )
    slots[me, 0:1, :] = prod[0:1]
    slots[me, 1:2, :] = value[0:1]
    copies = start_share(slots, slot_send, slot_recv)

    def activate(first):
        at = pl.ds(first, 64)
        y = branch_y[at, :]
        gelu_y[at, :] = gelu_parts(y)[0]

    tiles(8, 64, activate)
    for copy in copies:
        copy.wait()
    before = jnp.zeros((1, WIDTH), jnp.float32)
    for place_at in range(N_DP - 1):
        longer = slots[place_at, 0:1, :] * before + slots[place_at, 1:2, :]
        before = jnp.where(place_at < me, longer, before)

    state[0:8, :] = jnp.broadcast_to(before, (8, WIDTH))

    def finish(first):
        at = pl.ds(first, 64)
        total = values[at, :] + prods[at, :] * before
        state[pl.ds(first + 8, 64), :] = total
        mixed[at, :] = (total * gelu_y[at, :]).astype(jnp.bfloat16)

    tiles(8, 64, finish)
    store(7, state, outs[7])
    store(8, mixed, outs[8])
    loads[2].wait()

    def produce(by):
        at = pl.ds(pl.multiple_of(chip_row(by, 0), 128), 128)
        partial[at, :] = matmul(mixed[at, :], out_w[...]).astype(jnp.bfloat16)

    summed = TensorSum(chip_row, partial, *scratch)
    summed.start(produce)
    _, core = place()
    total = tokens[pl.ds(chip_row(0, core), OWN), :].astype(jnp.float32) + summed.finish()
    residual[...] = total
    block[...] = rms_norm(total, gains[1:2, :]).astype(jnp.bfloat16)
    for copy in stores:
        copy.wait()


def saved_shapes():
    f32, bf16 = jnp.float32, jnp.bfloat16
    return (
        ((ROWS, D), bf16),
        ((ROWS + 16, WIDTH), f32),
        ((ROWS, 2 * BLOCK), bf16),
        ((ROWS, WIDTH), f32),
        ((ROWS, WIDTH), f32),
        ((ROWS + 8, WIDTH), f32),
        ((ROWS, WIDTH), f32),
        ((ROWS + 8, WIDTH), f32),
        ((ROWS, WIDTH), bf16),
    )


def mixer_forward(tokens, branch_in, gate_blocks, out_proj, chan, gains, flags):
    f32, bf16 = jnp.float32, jnp.bfloat16
    dma = pltpu.SemaphoreType.DMA
    here = pl.BlockSpec(memory_space=pltpu.VMEM)
    there = pl.BlockSpec(memory_space=pl.ANY)
    shapes = saved_shapes()
    inside = shapes[:6] + (shapes[7], shapes[6], shapes[8])
    return pl.pallas_call(
        forward_kernel,
        out_shape=(
            jax.ShapeDtypeStruct((OWN, D), f32),
            jax.ShapeDtypeStruct((OWN, D), bf16),
            *(jax.ShapeDtypeStruct(*shape) for shape in shapes),
        ),
        in_specs=[here, there, here, there, here, here, here],
        out_specs=tuple([here] * 2 + [there] * 9),
        scratch_shapes=[pltpu.VMEM(*shape) for shape in inside]
        + [
            pltpu.VMEM((2, WIDTH, D), bf16),
            pltpu.VMEM((WIDTH, D), bf16),
            pltpu.VMEM((16, D), bf16),
            pltpu.VMEM((16, D), bf16),
            pltpu.VMEM((2, WIDTH, 2 * BLOCK), bf16),
            pltpu.VMEM((WIDTH, 2 * BLOCK), bf16),
            pltpu.VMEM((ROWS, WIDTH), f32),
            pltpu.VMEM((ROWS, WIDTH), f32),
            pltpu.VMEM((ROWS, WIDTH), f32),
            pltpu.VMEM((ROWS, WIDTH), f32),
            pltpu.VMEM((ROWS, BLOCK), bf16),
            pltpu.VMEM((ROWS, BLOCK), bf16),
            pltpu.VMEM((N_DP, 8, WIDTH), f32),
            pltpu.VMEM((ROWS, D), bf16),
            dma((3,)),
            dma((9,)),
            dma,
            dma,
            dma((2,)),
            dma((2,)),
            dma((N_DP,)),
            dma((N_DP,)),
        ]
        + reduce_scratch(),
        compiler_params=params(1),
    )(tokens, branch_in, gate_blocks, out_proj, chan, gains, flags)


def norm_back(value, gain, grad):
    scale = lax.rsqrt(jnp.mean(value * value, axis=-1, keepdims=True) + NORM_EPS)
    unit = value * scale
    scaled = grad * gain
    back = scale * (scaled - unit * jnp.mean(scaled * unit, axis=-1, keepdims=True))
    return back, jnp.sum(grad * unit, axis=0, keepdims=True)


def back_kernel(
    block, residual, gains, chan, flags, dy_hbm, ffn_hbm, down_hbm, tokens, out_hbm, branch_hbm, gates_hbm, *rest
):
    saved, rest = rest[:9], rest[9:]
    tokens_grad, out, gain_sum, channel_sum, blocks_share, *rest = rest
    shares, (down_grad, up_grad, gate_grad, mixer_grad), rest = rest[:4], rest[4:8], rest[8:]
    (
        normed, rounded, grad, grad_gain_two, partial, stage, near, near_blocks,
        low_in, high_in, slots, halo, halo_in, gain_t, gain_dp, chan_dp, blocks_grad,
        load_sem, stage_sem, share_sem, slot_send, slot_recv, side_send, side_recv, halo_send, halo_recv,
        t_send, t_recv, g_send, g_recv, c_send, c_recv, reuse_sem, free_sem, *scratch
    ) = rest
    me, index = lax.axis_index("dp"), lax.axis_index("tensor")
    x, core = place()
    shift = lax.rem(index * WIDTH, BLOCK)
    ready = announce(dp_peers() + tensor_peers() + [far_peer()])

    def take(count):
        taken = scratch[:count]
        del scratch[:count]
        return taken

    sum_scratch = take(7)
    summed = TensorSum(arrival_row, partial, *sum_scratch)
    summed_out = TensorSum(arrival_row, partial, *sum_scratch)
    summed_last = TensorSum(chip_row, partial, *sum_scratch)
    before = TensorGather(arrival_row, normed, *take(4))
    after = TensorGather(chip_row, rounded, *take(4))
    first = take(4)
    down_sum = DataSum(down_grad, *first, near, *take(3), HALF)
    up_sum = DataSum(up_grad, *take(4), near, *take(3), HALF)
    gate_sum = DataSum(gate_grad, *take(4), near, *take(3), HALF)
    mixer_sum = DataSum(mixer_grad, *first, near, *take(3), HALF)
    blocks_sum = DataSum(blocks_grad, *take(4), near_blocks, *take(3), GATE_HALF)

    def weight_grad(target, jobs):
        pending = None
        for z in range(4):
            columns = pl.ds(z * 640, 640)
            parts = [transposed_times(left[:, columns], right[...]) for left, right in jobs]
            whole = parts[0] if len(parts) == 1 else jnp.concatenate(parts, 1)
            if pending is not None:
                pending.wait()
            stage[...] = whole.astype(jnp.bfloat16).reshape(4, 2, HALF, HIDE)
            pending = pltpu.make_async_copy(stage, target.at[z], stage_sem)
            pending.start()
        pending.wait()

    def ffn_part(dy, ffn_w, down_w, hidden, to_gate, to_up, gate_pre, up_pre, grad_hidden):
        loads = []

        def load(source, target):
            copy = pltpu.make_async_copy(source, target, load_sem.at[len(loads)])
            copy.start()
            loads.append(copy)

        for by, spot in ARRIVAL.items():
            load(
                dy_hbm.at[pl.ds(pl.multiple_of(lax.rem(x + by, 4) * 128, 128), 128)],
                dy.at[pl.ds(spot * 128, 128)],
            )
        load(down_hbm, down_w)
        load(ffn_hbm.at[pl.ds(0, HIDE)], ffn_w.at[pl.ds(0, HIDE)])
        load(ffn_hbm.at[pl.ds(HIDE, HIDE)], ffn_w.at[pl.ds(HIDE, HIDE)])
        pieces = ((0, 384), (384, 384), (768, 192))
        ready()
        before.start(block[...])
        for copy in loads[:5]:
            copy.wait()
        for start, size in pieces:
            units = pl.ds(start, size)
            grad_hidden[:, units] = times_transposed(dy[...], down_w[units, :])
        for copy in loads[5:]:
            copy.wait()
        before.arrive(1)
        before.settle(0)
        before.settle(1)
        for group in range(2):
            if group:
                before.arrive(3)
                before.arrive(2)
                before.settle(3)
                before.settle(2)
            rows = pl.ds(group * 256, 256)
            for start, size in pieces:
                units = pl.ds(start, size)
                gate_pre[:, 0:size] = times_transposed(normed[rows, :], ffn_w[units, :])
                up_pre[:, 0:size] = times_transposed(normed[rows, :], ffn_w[pl.ds(HIDE + start, size), :])

                def activate(first, units=units, size=size, group=group):
                    here = pl.ds(first, 32)
                    at = pl.ds(pl.multiple_of(group * 256 + first, 32), 32)
                    value, slope = gelu_parts(gate_pre[here, 0:size])
                    up, back = up_pre[here, 0:size], grad_hidden[at, units]
                    hidden[at, units] = (value * up).astype(jnp.bfloat16)
                    to_up[at, units] = (back * value).astype(jnp.bfloat16)
                    to_gate[at, units] = (back * up * slope).astype(jnp.bfloat16)

                tiles(256 // 32, 32, activate)
        before.finish()

        def produce(by):
            at = pl.ds(arrival_row(by, 0), 128)
            total = matmul(to_gate[at, :], ffn_w[0:HIDE, :]) + matmul(
                to_up[at, :], ffn_w[HIDE : 2 * HIDE, :]
            )
            partial[at, :] = total.astype(jnp.bfloat16)

        weight_grad(down_grad, [(dy, hidden)])
        down_sum.start()
        summed.start(produce)
        weight_grad(up_grad, [(normed, to_up)])
        up_sum.start()
        down_sum.middle()
        norm_grad = summed.finish()
        back, gain_part = norm_back(residual[...], gains[1:2, :], norm_grad)
        back = back + dy[pl.ds(arrival_row(0, core), OWN), :].astype(jnp.float32)
        grad[...] = back
        grad_gain_two[...] = gain_part
        after.start(back.astype(jnp.bfloat16))

        def produce_out(first):
            at = pl.ds(first, 128)
            partial[at, :] = matmul(hidden[at, :], down_w[...]).astype(jnp.bfloat16)

        tiles(4, 128, produce_out)
        weight_grad(gate_grad, [(normed, to_gate)])
        gate_sum.start()

    f32, bf16 = jnp.float32, jnp.bfloat16
    pl.run_scoped(
        ffn_part,
        pltpu.VMEM((ROWS, D), bf16),
        pltpu.VMEM((2 * HIDE, D), bf16),
        pltpu.VMEM((HIDE, D), bf16),
        pltpu.VMEM((ROWS, HIDE), bf16),
        pltpu.VMEM((ROWS, HIDE), bf16),
        pltpu.VMEM((ROWS, HIDE), bf16),
        pltpu.VMEM((256, 384), f32),
        pltpu.VMEM((256, 384), f32),
        pltpu.VMEM((ROWS, HIDE), f32),
    )

    def mixer_part(
        normed_one, ext, window, pre_a, pre_x, carry, branch_y, state, mixed,
        out_w, branch_w, gates, own, wide, to_y, local, sums, prods, to_a, to_gx, window_grad, low, high, conv_grad,
        share_stage,
    ):
        targets = (
            normed_one, ext, window, pre_a, pre_x, carry, branch_y, state, mixed, out_w, branch_w, gates, own,
        )
        sources = (
            *saved,
            out_hbm,
            branch_hbm,
            gates_hbm,
            tokens.at[pl.ds(chip_row(0, core), OWN)],
        )
        def keep_share(number):
            copy = pltpu.make_async_copy(share_stage, shares[number], share_sem)
            copy.start()
            copy.wait()

        loads = []
        for source, target in zip(sources, targets):
            loads.append(pltpu.make_async_copy(source, target, load_sem.at[len(loads)]))
            loads[-1].start()
        for by in (1, 3, 2):
            after.arrive(by)
        for by in (0, 1, 3, 2):
            after.settle(by)
        after.finish()
        for step, by in enumerate(summed_out.ORDER):
            summed_out.give(by)
        for by in (2, 1, 3):
            summed_out.pass_on(by)
        for copy in loads:
            copy.wait()
        wide_gates(gates, wide, shift)

        def mixed_tile(first):
            at = pl.ds(first, 128)
            local[at, :] = times_transposed(rounded[at, :], out_w[...])

        tiles(4, 128, mixed_tile)

        def gelu_tile(first):
            at = pl.ds(first, 64)
            value, slope = gelu_parts(branch_y[at, :])
            mixed_grad = local[at, :]
            to_y[at, :] = (mixed_grad * state[pl.ds(first + 8, 64), :] * slope).astype(jnp.bfloat16)
            local[at, :] = mixed_grad * value

        tiles(8, 64, gelu_tile)
        prod, value = local_scan(
            lambda first: carry[pl.ds(first, 16), :][1:9],
            lambda first: local[pl.ds(first, 8), :],
            sums,
            prods,
            True,
        )
        slots[me, 0:1, :] = carry[0:1, :] * prod[0:1]
        slots[me, 1:2, :] = carry[0:1, :] * value[0:1]
        copies = start_share(slots, slot_send, slot_recv)
        down_sum.turn()

        for copy in copies:
            copy.wait()
        up_sum.middle()
        later = jnp.zeros((1, WIDTH), jnp.float32)
        for place_at in range(N_DP - 1, 0, -1):
            longer = slots[place_at, 0:1, :] * later + slots[place_at, 1:2, :]
            later = jnp.where(place_at > me, longer, later)
        plus, decay_slope = chan[5:6, :], chan[6:7, :]
        zero_row = jnp.zeros((1, WIDTH), jnp.float32)

        def gate_tile(first, decay_grad):
            at = pl.ds(first, 64)
            total = sums[at, :] + prods[at, :] * later
            near = state[pl.ds(first, 72), :]
            conv = lax.dot_general(
                window[at, :], place_matrix(shift), (((1,), (1,)), ((), ())), preferred_element_type=jnp.float32
            )
            reset = flags[at, 4:5] > 0.0
            gate_a, gate_x = jax.nn.sigmoid(pre_a[at, :]), jax.nn.sigmoid(pre_x[at, :])
            log_a = -8.0 * gate_a * plus
            keep = jnp.exp(log_a)
            scale = jnp.sqrt(one_less_exp(2.0 * log_a))
            scale_here = jnp.where(reset, 1.0, scale)
            conv_grad[at, :] = total * gate_x * scale_here
            to_gx[at, :] = (total * conv * scale_here * gate_x * (1.0 - gate_x)).astype(jnp.bfloat16)
            log_grad = total * near[7:71] * keep - total * conv * gate_x * keep * keep / scale
            log_grad = jnp.where(reset, 0.0, log_grad)
            to_a[at, :] = (log_grad * (-8.0 * plus) * gate_a * (1.0 - gate_a)).astype(jnp.bfloat16)
            return decay_grad + jnp.sum(log_grad * (-8.0 * gate_a), axis=0, keepdims=True)

        decay_grad = lax.fori_loop(
            0, 8, lambda i, held: gate_tile(pl.multiple_of(i * 64, 64), held), zero_row
        )
        decay_grad = decay_grad * decay_slope

        def window_tile(first):
            at = pl.ds(first, 128)
            total = matmul(to_a[at, :], wide[0]) + matmul(to_gx[at, :], wide[1])
            window_grad[at, :] = total
            low[at, :] = total[:, 0:BLOCK].astype(jnp.bfloat16)
            high[at, :] = total[:, BLOCK : 2 * BLOCK].astype(jnp.bfloat16)

        tiles(4, 128, window_tile)
        up, down = beside_peers()
        to_up = remote(high, low_in, side_send.at[0], side_recv.at[0], up)
        to_down = remote(low, high_in, side_send.at[1], side_recv.at[1], down)
        to_up.start()
        to_down.start()
        column = lax.broadcasted_iota(jnp.int32, (BLOCK, WIDTH), 1)
        chosen = []
        for right in (to_a, to_gx):
            both = transposed_times(window[...], right[...])
            chosen.append(
                jnp.where(column + shift < BLOCK, both[0:BLOCK], both[BLOCK : 2 * BLOCK])
            )
        blocks_grad[...] = jnp.concatenate(chosen, 1).reshape(4, 4, 2, GATE_HALF, 2 * WIDTH)
        down_sum.finish(share_stage)
        keep_share(0)
        for peer in ring_peers():
            pl.semaphore_signal(reuse_sem, inc=1, device_id=peer, device_id_type=MESH)
        to_up.wait()
        to_down.wait()

        def conv_tile(first):
            at = pl.ds(first, 64)
            from_low = jnp.where(shift != 0, low_in[at, :].astype(jnp.float32), 0.0)
            from_high = jnp.where(shift != 192, high_in[at, :].astype(jnp.float32), 0.0)
            total = window_grad[at, :] + jnp.concatenate([from_low, from_high], 1)
            total = pltpu.roll(total, lax.rem(2 * BLOCK - shift, 2 * BLOCK), 1)
            conv_grad[at, :] = conv_grad[at, :] + total[:, 0:WIDTH]

        tiles(8, 64, conv_tile)
        conv_grad[ROWS : ROWS + 8, :] = jnp.zeros((8, WIDTH), jnp.float32)
        head = conv_grad[0:8, :]
        rows = []
        for row in range(3):
            total = zero_row
            for tap in range(3 - row, 4):
                from_row = row - 3 + tap
                counted = flags[from_row : from_row + 1, tap : tap + 1] > 0.0
                total = total + chan[tap : tap + 1, :] * jnp.where(
                    counted, head[from_row : from_row + 1], 0.0
                )
            rows.append(total)
        halo[0:5, :] = jnp.zeros((5, WIDTH), jnp.float32)
        for row in range(3):
            halo[5 + row : 6 + row, :] = rows[row]
        send_halo = remote(halo, halo_in, halo_send, halo_recv, {"dp": lax.rem(me + N_DP - 1, N_DP)})
        send_halo.start()
        blocks_sum.start()

        def tap_tile(first, held):
            at = pl.ds(first, 64)
            near = conv_grad[pl.ds(first, 72), :]
            marks = flags[pl.ds(first, 72), :]
            behind = ext[pl.ds(first + 8, 72), :]
            total = chan[0:1, :] * near[0:64]
            taps = [held[0] + jnp.sum(near[0:64] * behind[8:72], axis=0, keepdims=True)]
            for tap in range(1, 4):
                counted = marks[tap : tap + 64, tap : tap + 1] > 0.0
                total = total + chan[tap : tap + 1, :] * jnp.where(counted, near[tap : tap + 64], 0.0)
                here = jnp.where(marks[0:64, tap : tap + 1] > 0.0, near[0:64], 0.0)
                taps.append(
                    held[tap] + jnp.sum(here * behind[8 - tap : 72 - tap], axis=0, keepdims=True)
                )
            local[at, :] = total
            return tuple(taps)

        tap_grads = lax.fori_loop(
            0, 8, lambda i, held: tap_tile(pl.multiple_of(i * 64, 64), held), (zero_row,) * 4
        )
        for tap in range(4):
            chan_dp[me, tap : tap + 1, :] = tap_grads[tap]
        chan_dp[me, 4:5, :] = decay_grad
        chan_dp[me, 5:8, :] = jnp.zeros((3, WIDTH), jnp.float32)
        channel_copies = start_share(chan_dp, c_send, c_recv)
        pl.semaphore_wait(reuse_sem, 6)
        gate_sum.middle()
        out[...] = (residual[...] + summed_out.finish()).astype(jnp.bfloat16)
        for peer in tensor_peers():
            pl.semaphore_signal(free_sem, inc=1, device_id=peer, device_id_type=MESH)
        send_halo.wait()
        local[ROWS - 8 : ROWS, :] = local[ROWS - 8 : ROWS, :] + halo_in[...]
        to_x = to_a
        to_x[...] = local[...].astype(jnp.bfloat16)

        def produce(by):
            at = pl.ds(pl.multiple_of(chip_row(by, 0), 128), 128)
            total = matmul(to_x[at, :], branch_w[0]) + matmul(to_y[at, :], branch_w[1])
            partial[at, :] = total.astype(jnp.bfloat16)

        pl.semaphore_wait(free_sem, 4)
        summed_last.start(produce)
        weight_grad(mixer_grad, [(rounded, mixed), (normed_one, to_y), (normed_one, to_x)])
        mixer_sum.start()
        up_sum.turn()
        blocks_sum.middle()
        norm_grad = summed_last.finish()
        before_norm, gain_part = norm_back(own[...].astype(jnp.float32), gains[0:1, :], norm_grad)
        tokens_grad[...] = (grad[...] + before_norm).astype(jnp.bfloat16)
        gain_t[index, 0:1, :] = gain_part
        gain_t[index, 1:2, :] = grad_gain_two[...]
        gain_copies = []
        for by in range(1, N_T):
            copy = remote(
                gain_t.at[index],
                gain_t.at[index],
                t_send.at[by],
                t_recv.at[by],
                {"tensor": lax.rem(index + by, N_T)},
            )
            copy.start()
            gain_copies.append(copy)
        gate_sum.turn()
        mixer_sum.middle()
        for copy in gain_copies:
            copy.wait()
        total = gain_t[0]
        for by in range(1, N_T):
            total = total + gain_t[by]
        gain_dp[me] = total
        gain_copies = start_share(gain_dp, g_send, g_recv)
        up_sum.finish(share_stage)
        keep_share(1)
        blocks_sum.turn()
        gate_sum.finish(share_stage)
        keep_share(2)
        mixer_sum.turn()
        for copy in channel_copies + gain_copies:
            copy.wait()
        total, channels = gain_dp[0], chan_dp[0]
        for by in range(1, N_DP):
            total = total + gain_dp[by]
            channels = channels + chan_dp[by]
        gain_sum[...] = total
        channel_sum[...] = channels
        blocks_sum.finish(blocks_share)
        mixer_sum.finish(share_stage)
        keep_share(3)


    wide_f32 = pltpu.VMEM((ROWS, WIDTH), f32)
    wide_bf16 = pltpu.VMEM((ROWS, WIDTH), bf16)
    pl.run_scoped(
        mixer_part,
        *(pltpu.VMEM(*shape) for shape in saved_shapes()),
        pltpu.VMEM((WIDTH, D), bf16),
        pltpu.VMEM((2, WIDTH, D), bf16),
        pltpu.VMEM((2, WIDTH, BLOCK), bf16),
        pltpu.VMEM((OWN, D), bf16),
        pltpu.VMEM((2, WIDTH, 2 * BLOCK), bf16),
        wide_bf16,
        wide_f32,
        wide_f32,
        wide_f32,
        wide_bf16,
        wide_bf16,
        pltpu.VMEM((ROWS, 2 * BLOCK), f32),
        pltpu.VMEM((ROWS, BLOCK), bf16),
        pltpu.VMEM((ROWS, BLOCK), bf16),
        pltpu.VMEM((ROWS + 8, WIDTH), f32),
        pltpu.VMEM((2 * HALF, HIDE), f32),
    )


def backward(block, residual, gains, chan, flags, dy, ffn_t, down, tokens, out_proj, branch_t, gates_t, saved):
    f32, bf16 = jnp.float32, jnp.bfloat16
    dma = pltpu.SemaphoreType.DMA
    here = pl.BlockSpec(memory_space=pltpu.VMEM)
    there = pl.BlockSpec(memory_space=pl.ANY)
    share = jax.ShapeDtypeStruct((2 * HALF, HIDE), f32)
    shared = jax.ShapeDtypeStruct((4, 4, 2, HALF, HIDE), bf16)
    return pl.pallas_call(
        back_kernel,
        out_shape=(
            jax.ShapeDtypeStruct((OWN, D), bf16),
            jax.ShapeDtypeStruct((OWN, D), bf16),
            jax.ShapeDtypeStruct((2, D), f32),
            jax.ShapeDtypeStruct((8, WIDTH), f32),
            jax.ShapeDtypeStruct((2 * GATE_HALF, 2 * WIDTH), f32),
            *[share] * 4,
            *[shared] * 4,
        ),
        in_specs=[here] * 5 + [there] * 16,
        out_specs=tuple([here] * 5 + [there] * 8),
        scratch_shapes=[
            pltpu.VMEM((ROWS, D), bf16),
            pltpu.VMEM((ROWS, D), bf16),
            pltpu.VMEM((OWN, D), f32),
            pltpu.VMEM((1, D), f32),
            pltpu.VMEM((ROWS, D), bf16),
            pltpu.VMEM((4, 2, HALF, HIDE), bf16),
            pltpu.VMEM((2, 2, HALF, HIDE), bf16),
            pltpu.VMEM((2, 2, GATE_HALF, 2 * WIDTH), f32),
            pltpu.VMEM((ROWS, BLOCK), bf16),
            pltpu.VMEM((ROWS, BLOCK), bf16),
            pltpu.VMEM((N_DP, 8, WIDTH), f32),
            pltpu.VMEM((8, WIDTH), f32),
            pltpu.VMEM((8, WIDTH), f32),
            pltpu.VMEM((N_T, 2, D), f32),
            pltpu.VMEM((N_DP, 2, D), f32),
            pltpu.VMEM((N_DP, 8, WIDTH), f32),
            pltpu.VMEM((4, 4, 2, GATE_HALF, 2 * WIDTH), f32),
            dma((13,)),
            dma,
            dma,
            dma((N_DP,)),
            dma((N_DP,)),
            dma((2,)),
            dma((2,)),
            dma,
            dma,
            dma((N_T,)),
            dma((N_T,)),
            dma((N_DP,)),
            dma((N_DP,)),
            dma((N_DP,)),
            dma((N_DP,)),
            pltpu.SemaphoreType.REGULAR,
            pltpu.SemaphoreType.REGULAR,
        ]
        + reduce_scratch()
        + gather_scratch()
        + gather_scratch()
        + data_buffers(HALF, HIDE, bf16)
        + data_sems()
        + data_buffers(HALF, HIDE, bf16)
        + data_sems()
        + data_buffers(HALF, HIDE, bf16)
        + data_sems()
        + data_sems()
        + data_buffers(GATE_HALF, 2 * WIDTH, f32)
        + data_sems(),
        compiler_params=params(2),
    )(block, residual, gains, chan, flags, dy, ffn_t, down, tokens, out_proj, branch_t, gates_t, *saved)


def rms_norm(values, gain):
    return values * lax.rsqrt(jnp.mean(values * values, axis=-1, keepdims=True) + NORM_EPS) * gain


def matmul(left, right):
    return jnp.dot(left, right, preferred_element_type=jnp.float32)


def times_transposed(left, right):
    return lax.dot_general(
        left, right, (((1,), (1,)), ((), ())), preferred_element_type=jnp.float32
    )


def transposed_times(left, right):
    return lax.dot_general(
        left, right, (((0,), (0,)), ((), ())), preferred_element_type=jnp.float32
    )


def adam_step(weight, grad, first, second, rate, decay):
    first_new = BETA_ONE * first + (1.0 - BETA_ONE) * grad
    second_new = BETA_TWO * second + (1.0 - BETA_TWO) * grad * grad
    first_hat = first_new / (1.0 - BETA_ONE**STEP)
    second_hat = second_new / (1.0 - BETA_TWO**STEP)
    weight_new = weight - rate * (first_hat / (jnp.sqrt(second_hat) + ADAM_EPS) + decay * weight)
    return (first_new, second_new, weight_new)


SHARE = 2 * HALF
SPAN = 384
DECAY = 0.1
BRANCH_RATE, GATE_RATE, OUT_RATE = 3.0 * D**-0.5, 3.0 * BLOCK**-0.5, 3.0 * (L // 8) ** -0.5
FFN_RATE, DOWN_RATE = 3.0 * D**-0.5, 3.0 * (F // 2) ** -0.5


def update_jobs():
    return (
        ("down", None, 0, 0, HIDE, 0, DOWN_RATE),
        ("ffn", 1, 1, 0, HIDE, HIDE, FFN_RATE),
        ("ffn", 0, 2, 0, HIDE, 0, FFN_RATE),
        ("out", None, 3, 0, WIDTH, 0, OUT_RATE),
        ("branch", 1, 3, WIDTH, WIDTH, WIDTH, BRANCH_RATE),
        ("branch", 0, 3, 2 * WIDTH, WIDTH, 0, BRANCH_RATE),
        ("gate", 0, 4, 0, WIDTH, 0, GATE_RATE),
        ("gate", 1, 4, WIDTH, WIDTH, WIDTH, GATE_RATE),
    )


ARRAYS = ("down", "ffn", "out", "branch", "gate")


def update_kernel(*refs):
    shares, weights = refs[:5], dict(zip(ARRAYS, refs[5:10]))
    moments = {name: refs[10 + 2 * i : 12 + 2 * i] for i, name in enumerate(ARRAYS)}
    outs = {name: refs[20 + 3 * i : 23 + 3 * i] for i, name in enumerate(ARRAYS)}
    windows = dict(zip(ARRAYS, refs[35:40]))
    held = refs[40:48]
    in_sem, window_sem, out_sem = refs[48:]
    me = lax.axis_index("dp")
    begin = jnp.minimum(me * SHARE // 128 * 128, D - SPAN)
    copies = {}

    def copy(key, source, target, sem):
        copies[key] = pltpu.make_async_copy(source, target, sem)
        copies[key].start()

    jobs = update_jobs()
    waiting = list(ARRAYS)
    for number, (name, part, *_) in enumerate(jobs):
        if name not in copies:
            source = weights[name]
            if name != "gate":
                source = source.at[:, pl.ds(pl.multiple_of(begin, 128), SPAN)]
            copy(name, source, windows[name], window_sem.at[ARRAYS.index(name)])
        for which in range(2):
            source = moments[name][which]
            source = source if part is None else source.at[part]
            copy((number, which), source, held[number].at[which], in_sem.at[number, which])
    for number, (name, part, share, lane, width, row, rate) in enumerate(jobs):
        if name in waiting:
            waiting.remove(name)
            copies[name].wait()
        count = 16 if name == "gate" else SHARE
        span = BLOCK if name == "gate" else SPAN
        offset = me * count if name == "gate" else me * SHARE - begin
        mine = lax.broadcasted_iota(jnp.int32, (count, span), 0) + offset
        lanes = lax.broadcasted_iota(jnp.int32, (count, span), 1)
        chosen = jnp.where(lanes == mine, 1.0, 0.0).astype(jnp.bfloat16)
        box = held[number]
        box[2] = times_transposed(chosen, windows[name][row : row + width, :])
        for which in range(2):
            copies[number, which].wait()

        def body(first, box=box, share=share, lane=lane, width=width, rate=rate):
            at = pl.ds(first, 16)
            grad = shares[share][at, lane : lane + width]
            new = adam_step(box[2, at, :], grad, box[0, at, :], box[1, at, :], rate, DECAY)
            for which in range(3):
                box[which, at, :] = new[which]

        tiles(count // 16, 16, body, 1 if count == 16 else 5)
        for which in range(3):
            target = outs[name][which]
            target = target if part is None else target.at[part]
            copy((number, which), box.at[which], target, out_sem.at[number, which])
    for number in range(len(jobs)):
        for which in range(3):
            copies[number, which].wait()


def update_weights(shares, weights, moments):
    f32, bf16 = jnp.float32, jnp.bfloat16
    dma = pltpu.SemaphoreType.DMA
    here = pl.BlockSpec(memory_space=pltpu.VMEM)
    there = pl.BlockSpec(memory_space=pl.ANY)
    jobs = update_jobs()
    return pl.pallas_call(
        update_kernel,
        out_shape=tuple(
            jax.ShapeDtypeStruct(moments[2 * i].shape, f32) for i in range(5) for _ in range(3)
        ),
        in_specs=[here] * 5 + [there] * 15,
        out_specs=tuple([there] * 15),
        scratch_shapes=[
            pltpu.VMEM((weight.shape[0], BLOCK if name == "gate" else SPAN), bf16)
            for name, weight in zip(ARRAYS, weights)
        ]
        + [pltpu.VMEM((3, 16 if job[0] == "gate" else SHARE, job[4]), f32) for job in jobs]
        + [dma((len(jobs), 2)), dma((5,)), dma((len(jobs), 3))],
        compiler_params=pltpu.CompilerParams(vmem_limit_bytes=63 * 2**20),
    )(*shares, *weights, *moments)


def shards(
    tokens,
    cotangent,
    segments,
    gains,
    channel_params,
    branch_in,
    gate_blocks,
    out_proj,
    ffn_in,
    ffn_down,
    gains_first,
    gains_second,
    channel_first,
    channel_second,
    branch_first,
    branch_second,
    gate_first,
    gate_second,
    out_first,
    out_second,
    ffn_in_first,
    ffn_in_second,
    down_first,
    down_second,
):
    rows = ROWS
    data_index = lax.axis_index("dp")

    padded_ids = jnp.concatenate([jnp.full((3,), -1, jnp.int32), segments])
    local_ids = lax.dynamic_slice_in_dim(padded_ids, data_index * rows, rows + 3)
    marks = [local_ids[3 - tap : 3 - tap + rows] == local_ids[3:] for tap in range(4)]
    marks.append(local_ids[3:] != local_ids[2 : 2 + rows])
    flags = jnp.pad(jnp.stack(marks, 1).astype(jnp.float32), ((0, 8), (0, 3)))
    decay_param = channel_params[4:5]
    chan = jnp.concatenate(
        [channel_params, jax.nn.softplus(decay_param), jax.nn.sigmoid(decay_param), decay_param], 0
    )
    branch_t = branch_in.swapaxes(1, 2)
    gates_t = gate_blocks.swapaxes(1, 2)
    ffn_t = ffn_in.swapaxes(1, 2).reshape(2 * HIDE, D)
    residual_own, block, *saved = mixer_forward(
        tokens, branch_t, gates_t, out_proj, chan, gains, flags
    )
    tokens_grad, block_out, gain_grad, channel_grad, blocks_share, down_share, up_share, gate_share, mixer_share, *_ = (
        backward(
            block,
            residual_own,
            gains,
            chan,
            flags,
            cotangent,
            ffn_t,
            ffn_down,
            tokens,
            out_proj,
            branch_t,
            gates_t,
            saved,
        )
    )
    channel_rate = jnp.array([1.0, 1.0, 1.0, 1.0, 3.0], jnp.float32)[:, None]
    gains_out = adam_step(gains, gain_grad, gains_first, gains_second, 1.0, 0.0)
    channel_out = adam_step(
        channel_params, channel_grad[:5], channel_first, channel_second, channel_rate, 0.0
    )
    new = update_weights(
        (down_share, up_share, gate_share, mixer_share, blocks_share),
        (
            ffn_down,
            ffn_t,
            out_proj,
            branch_t.reshape(2 * WIDTH, D),
            gates_t.reshape(2 * WIDTH, BLOCK),
        ),
        (
            down_first.T,
            down_second.T,
            ffn_in_first,
            ffn_in_second,
            out_first.T,
            out_second.T,
            branch_first,
            branch_second,
            gate_first,
            gate_second,
        ),
    )
    return (
        block_out,
        tokens_grad,
        *gains_out,
        *channel_out,
        *new[9:12],
        *new[12:15],
        *(value.T for value in new[6:9]),
        *new[3:6],
        *(value.T for value in new[0:3]),
    )


def solution(mesh):
    weights = [
        P(None, None, "tensor"),
        P(None, None, "tensor"),
        P("tensor", None),
        P(None, None, "tensor"),
        P("tensor", None),
    ]
    owned = [
        P(None, "dp", "tensor"),
        P(None, "dp", "tensor"),
        P("tensor", "dp"),
        P(None, "dp", "tensor"),
        P("tensor", "dp"),
    ]
    moments = [P(), P(None, "tensor")] + owned
    placed = [P("dp", None), P("dp", None), P(), P(), P(None, "tensor")] + weights
    for spec in moments:
        placed += [spec, spec]
    outs = [P(("dp", "tensor"), None)] * 2
    for spec in moments:
        outs += [spec, spec, spec]
    return jax.shard_map(
        shards, mesh=mesh, in_specs=tuple(placed), out_specs=tuple(outs), check_vma=False
    )
```

```python
import functools

import jax
import jax.numpy as jnp
from jax import lax
from jax.experimental import pallas as pl
from jax.experimental.pallas import tpu as pltpu
from jax.sharding import PartitionSpec as P

D = 2560
L = 2560
BLOCK = 256
F = 7680
STEP = 10
N_DP = 16
N_T = 8
ROWS = 512
OWN = ROWS // N_T
WIDTH = L // N_T
HIDE = F // N_T
HALF = 80
GATE_HALF = 8
MESH = pl.DeviceIdType.MESH

NORM_EPS = 1e-06
ADAM_EPS = 1e-08
BETA_ONE = 0.9
BETA_TWO = 0.95


def params(cid):
    return pltpu.CompilerParams(
        collective_id=cid, has_side_effects=True, vmem_limit_bytes=63 * 2**20
    )


def vmem(count):
    return [pl.BlockSpec(memory_space=pltpu.VMEM)] * count


def announce(peers):
    barrier = pltpu.get_barrier_semaphore()
    for peer in peers:
        pl.semaphore_signal(barrier, inc=1, device_id=peer, device_id_type=MESH)
    return lambda: pl.semaphore_wait(barrier, len(peers))


def remote(source, target, send_sem, recv_sem, peer):
    return pltpu.make_async_remote_copy(
        src_ref=source,
        dst_ref=target,
        send_sem=send_sem,
        recv_sem=recv_sem,
        device_id=peer,
        device_id_type=MESH,
    )


class Later:
    def __init__(self, make):
        self.make = make

    def start(self):
        self.make().start()

    def wait(self):
        self.make().wait()

    def wait_send(self):
        self.make().wait_send()

    def wait_recv(self):
        self.make().wait_recv()


def place():
    index = lax.axis_index("tensor")
    return index // 2, lax.rem(index, 2)


def at_x(x, core, by):
    return {"tensor": lax.rem(x + by, 4) * 2 + core}


def tensor_peers():
    x, core = place()
    return [{"tensor": x * 2 + 1 - core}] + [at_x(x, core, by) for by in (1, 2, 3)]


def chip_row(by, which):
    x, _ = place()
    return pl.multiple_of((lax.rem(x + by, 4) * 2 + which) * OWN, OWN)


ARRIVAL = {0: 0, 1: 1, 3: 2, 2: 3}


def arrival_row(by, which):
    return pl.multiple_of((ARRIVAL[by % 4] * 2 + which) * OWN, OWN)


class TensorSum:
    ORDER = (2, 1, 3, 0)

    def __init__(self, row, partial, pair, held, landed, pair_send, pair_recv, x_send, x_recv):
        self.row = row
        self.partial, self.pair, self.held, self.landed = partial, pair, held, landed
        self.sems = pair_send, pair_recv, x_send, x_recv
        self.pair_copies, self.x_copies = {}, {}

    def give(self, by):
        def make():
            x, core = place()
            return remote(
                self.partial.at[pl.ds(self.row(by, 1 - core), OWN)],
                self.pair.at[by],
                self.sems[0].at[by],
                self.sems[1].at[by],
                {"tensor": x * 2 + 1 - core},
            )

        self.pair_copies[by] = Later(make)
        self.pair_copies[by].start()

    def pass_on(self, by):
        _, core = place()
        self.pair_copies[by].wait_recv()
        mine = self.partial[pl.ds(self.row(by, core), OWN), :].astype(jnp.float32)
        self.held[by - 1] = (mine + self.pair[by].astype(jnp.float32)).astype(jnp.bfloat16)

        def make():
            x, core = place()
            return remote(
                self.held.at[by - 1],
                self.landed.at[by - 1],
                self.sems[2].at[by - 1],
                self.sems[3].at[by - 1],
                at_x(x, core, by),
            )

        self.x_copies[by] = Later(make)
        self.x_copies[by].start()

    def start(self, produce):
        for step, by in enumerate(self.ORDER):
            produce(by)
            self.give(by)
            if step:
                self.pass_on(self.ORDER[step - 1])

    def finish(self):
        _, core = place()
        self.pair_copies[0].wait_recv()
        total = self.partial[pl.ds(self.row(0, core), OWN), :].astype(jnp.float32)
        total = total + self.pair[0].astype(jnp.float32)
        for by in (1, 3, 2):
            self.x_copies[by].wait_recv()
            total = total + self.landed[by - 1].astype(jnp.float32)
        for by in self.ORDER:
            self.pair_copies[by].wait_send()
        for by in (2, 1, 3):
            self.x_copies[by].wait_send()
        return total


def reduce_scratch():
    return [
        pltpu.VMEM((4, OWN, D), jnp.bfloat16),
        pltpu.VMEM((3, OWN, D), jnp.bfloat16),
        pltpu.VMEM((3, OWN, D), jnp.bfloat16),
        pltpu.SemaphoreType.DMA((4,)),
        pltpu.SemaphoreType.DMA((4,)),
        pltpu.SemaphoreType.DMA((3,)),
        pltpu.SemaphoreType.DMA((3,)),
    ]


class TensorGather:
    def __init__(self, row, whole, x_send, x_recv, pair_send, pair_recv):
        self.row, self.whole, self.sems = row, whole, (x_send, x_recv, pair_send, pair_recv)

    def at(self, by):
        _, core = place()
        return self.whole.at[pl.ds(self.row(by, core), OWN)]

    def start(self, block):
        _, core = place()
        self.whole[pl.ds(self.row(0, core), OWN), :] = block
        self.sends, self.pairs = [], {}
        for by in (1, 3, 2):

            def make(by=by):
                x, core = place()
                mine = self.at(0)
                target = mine if self.row is chip_row else self.at(4 - by)
                return remote(
                    mine,
                    target,
                    self.sems[0].at[by - 1],
                    self.sems[1].at[by - 1],
                    at_x(x, core, by),
                )

            self.sends.append(Later(make))
            self.sends[-1].start()
        self.hand(0)

    def hand(self, by):
        def make():
            x, core = place()
            block = self.at(by)
            return remote(
                block,
                block,
                self.sems[2].at[by],
                self.sems[3].at[by],
                {"tensor": x * 2 + 1 - core},
            )

        self.pairs[by] = Later(make)
        self.pairs[by].start()

    def arrive(self, by):
        x, core = place()
        sender = 4 - by
        block = self.at(by)
        remote(
            block,
            block,
            self.sems[0].at[sender - 1],
            self.sems[1].at[sender - 1],
            at_x(x, core, sender),
        ).wait_recv()
        self.hand(by)

    def settle(self, by):
        self.pairs[by].wait_recv()

    def finish(self):
        for copy in self.sends:
            copy.wait_send()
        for copy in self.pairs.values():
            copy.wait_send()


class DataSum:
    LOW, HIGH = pl.ds(0, 2), pl.ds(2, 2)

    def __init__(self, grad, own, via, ring, last, near, send, recv, local, rows):
        self.grad, self.own, self.near, self.via = grad, own, near, via
        self.ring, self.last, self.rows = ring, last, rows
        self.send, self.recv, self.local = send, recv, local
        self.copies = {}

    def spots(self, half):
        me = lax.axis_index("dp")
        z, y = me // 4, lax.rem(me, 4)
        return (y, z) if half == 0 else (z, y)

    def peer(self, half, first_by, second_by):
        first, second = self.spots(half)
        a, b = lax.rem(first + first_by + 4, 4), lax.rem(second + second_by + 4, 4)
        return {"dp": b * 4 + a if half == 0 else a * 4 + b}

    def block(self, half, by, part):
        a = lax.rem(self.spots(half)[0] + by + 4, 4)
        return self.grad.at[part, a, 0] if half == 0 else self.grad.at[a, part, 1]

    def ship(self, half, slot, source, target, first_by, second_by):
        def make():
            return remote(
                source(),
                target(),
                self.send.at[half, slot],
                self.recv.at[half, slot],
                self.peer(half, first_by, second_by),
            )

        self.copies[half, slot] = Later(make)
        self.copies[half, slot].start()

    def own_load(self, half):
        return pltpu.make_async_copy(
            self.block(half, 0, pl.ds(0, 4)), self.own.at[half], self.local.at[half, 2]
        )

    def start(self):
        for half in (0, 1):
            self.ship(
                half, 0, lambda half=half: self.block(half, 2, self.LOW), lambda half=half: self.via.at[half, 0], 1, 0
            )
            self.ship(
                half, 1, lambda half=half: self.block(half, 2, self.HIGH), lambda half=half: self.via.at[half, 1], -1, 0
            )
            self.own_load(half).start()
        for half in (0, 1):
            self.ship(
                half, 2, lambda half=half: self.block(half, 1, self.HIGH), lambda half=half: self.ring.at[half, 0], 1, 0
            )
            self.ship(
                half, 3, lambda half=half: self.block(half, -1, self.LOW), lambda half=half: self.ring.at[half, 1], -1, 0
            )

    def add(self, target, sources, blocks):
        for block in range(blocks):
            if len(sources) == 1:
                target[block] = target[block] + sources[0][block]
                continue
            total = target[block].astype(jnp.float32)
            for source in sources:
                total = total + source[block].astype(jnp.float32)
            target[block] = total.astype(target.dtype)

    def middle(self):
        for half in (0, 1):
            loads = []
            for side, (by, part) in enumerate(((1, self.LOW), (-1, self.HIGH))):
                load = pltpu.make_async_copy(
                    self.block(half, by, part), self.near.at[side], self.local.at[half, side]
                )
                load.start()
                loads.append(load)
            for side in (0, 1):
                loads[side].wait()
                self.copies[half, side].wait_recv()
                via = self.via.at[half, side]
                self.add(via, [self.near.at[side]], 2)
                self.ship(
                    half,
                    4 + side,
                    lambda half=half, side=side: self.via.at[half, side],
                    lambda half=half, side=side: self.ring.at[half, 2 + side],
                    1 - 2 * side,
                    0,
                )

    def turn(self):
        for half in (0, 1):
            self.own_load(half).wait()
            for slot in (2, 3, 4, 5):
                self.copies[half, slot].wait_recv()
            ring = self.ring
            self.add(self.own.at[half, self.LOW], [ring.at[half, 1], ring.at[half, 2]], 2)
            self.add(self.own.at[half, self.HIGH], [ring.at[half, 0], ring.at[half, 3]], 2)
            for by in (1, 2, 3):
                self.ship(
                    half,
                    5 + by,
                    lambda half=half, by=by: self.own.at[
                        half, lax.rem(self.spots(half)[1] + by, 4)
                    ],
                    lambda half=half, by=by: self.last.at[half, by - 1],
                    0,
                    by,
                )

    def finish(self, share):
        for half in (0, 1):
            for by in (1, 2, 3):
                self.copies[half, 5 + by].wait_recv()
            total = self.own[half, self.spots(half)[1]].astype(jnp.float32)
            for by in range(3):
                total = total + self.last[half, by].astype(jnp.float32)
            share[half * self.rows : (half + 1) * self.rows, :] = total
        for copy in self.copies.values():
            copy.wait_send()


def data_buffers(rows, columns, dtype):
    return [
        pltpu.VMEM((2, 4, rows, columns), dtype),
        pltpu.VMEM((2, 2, 2, rows, columns), dtype),
        pltpu.VMEM((2, 4, 2, rows, columns), dtype),
        pltpu.VMEM((2, 3, rows, columns), dtype),
    ]


def data_sems():
    dma = pltpu.SemaphoreType.DMA
    return [dma((2, 9)), dma((2, 9)), dma((2, 3))]


def ring_peers():
    me = lax.axis_index("dp")
    z, y = me // 4, lax.rem(me, 4)
    along_y = [{"dp": z * 4 + lax.rem(y + by, 4)} for by in (1, 2, 3)]
    return along_y + [{"dp": lax.rem(z + by, 4) * 4 + y} for by in (1, 2, 3)]


def gather_scratch():
    return [
        pltpu.SemaphoreType.DMA((3,)),
        pltpu.SemaphoreType.DMA((3,)),
        pltpu.SemaphoreType.DMA((4,)),
        pltpu.SemaphoreType.DMA((4,)),
    ]


def dp_peers():
    me = lax.axis_index("dp")
    return [{"dp": lax.rem(me + by, N_DP)} for by in range(1, N_DP)]


def place_matrix(shift):
    row = lax.broadcasted_iota(jnp.int32, (WIDTH, 2 * BLOCK), 0)
    lane = lax.broadcasted_iota(jnp.int32, (WIDTH, 2 * BLOCK), 1)
    return jnp.where(lane == row + shift, 1.0, 0.0).astype(jnp.bfloat16)


def wide_gates(gates, wide, shift):
    row = lax.broadcasted_iota(jnp.int32, (WIDTH, BLOCK), 0)
    low = row + shift < BLOCK
    for gate in range(2):
        matrix = gates[gate].astype(jnp.float32)
        wide[gate, :, 0:BLOCK] = jnp.where(low, matrix, 0.0).astype(jnp.bfloat16)
        wide[gate, :, BLOCK : 2 * BLOCK] = jnp.where(low, 0.0, matrix).astype(jnp.bfloat16)


def one_less_exp(z):
    series = 1.0 + z / 7.0
    for term in (6.0, 5.0, 4.0, 3.0, 2.0):
        series = 1.0 + z / term * series
    return jnp.where(z > -0.35, -z * series, 1.0 - jnp.exp(z))


def tiles(count, size, body, unroll=1):
    def step(index, _):
        body(pl.multiple_of(index * size, size))
        return 0

    lax.fori_loop(0, count, step, 0, unroll=unroll)


def norm_rows(source, target, gain, rows):
    def body(first):
        at = pl.ds(first, 16)
        target[at, :] = rms_norm(source[at, :].astype(jnp.float32), gain).astype(jnp.bfloat16)

    tiles(rows // 16, 16, body, min(4, rows // 16))


def shifted(values, by, fill, reverse):
    count = values.shape[0]
    row = lax.broadcasted_iota(jnp.int32, values.shape, 0)
    if reverse:
        return jnp.where(row < count - by, pltpu.roll(values, count - by, 0), fill)
    return jnp.where(row >= by, pltpu.roll(values, by, 0), fill)


def local_scan(factor_at, term_at, values, prods, reverse):
    def step(index, held):
        prod, value = held
        first = pl.multiple_of((ROWS // 8 - 1 - index if reverse else index) * 8, 8)
        factor, term = factor_at(first), term_at(first)
        for by in (1, 2, 4):
            term = term + factor * shifted(term, by, 0.0, reverse)
            factor = factor * shifted(factor, by, 1.0, reverse)
        value = factor * value + term
        prod = factor * prod
        values[pl.ds(first, 8), :] = value
        prods[pl.ds(first, 8), :] = prod
        last = 0 if reverse else 7
        return (
            jnp.broadcast_to(prod[last : last + 1], prod.shape),
            jnp.broadcast_to(value[last : last + 1], value.shape),
        )

    ones = jnp.ones((8, WIDTH), jnp.float32)
    return lax.fori_loop(0, ROWS // 8, step, (ones, jnp.zeros_like(ones)), unroll=8)


def start_share(slots, send, recv):
    me = lax.axis_index("dp")
    copies = []
    for by in range(1, N_DP):
        copy = remote(
            slots.at[me], slots.at[me], send.at[by], recv.at[by], {"dp": lax.rem(me + by, N_DP)}
        )
        copy.start()
        copies.append(copy)
    return copies


def beside_peers():
    index = lax.axis_index("tensor")
    return {"tensor": lax.rem(index + 1, N_T)}, {"tensor": lax.rem(index + N_T - 1, N_T)}


def far_peer():
    index = lax.axis_index("tensor")
    _, core = place()
    return {"tensor": lax.rem(index + N_T - 1 + 2 * core, N_T)}


def gelu_parts(y):
    c = 0.7978845608028654
    inner = jnp.tanh(c * (y + 0.044715 * y * y * y))
    half = 0.5 * (1.0 + inner)
    slope = half + 0.5 * y * (1.0 - inner * inner) * c * (1.0 + 3 * 0.044715 * y * y)
    return y * half, slope


def forward_kernel(
    tokens, branch_hbm, gates, out_hbm, chan, gains, flags, residual, block, *rest
):
    outs = rest[:9]
    (
        normed_one, ext, window, pre_a, pre_x, carry, state, branch_y, mixed,
        branch_w, out_w, halo, halo_norm, wide, placing, update, values, prods, gelu_y, low, high, slots, partial,
        load_sem, store_sem, halo_send, halo_recv, side_send, side_recv, slot_send, slot_recv, *scratch
    ) = rest[9:]
    me, index = lax.axis_index("dp"), lax.axis_index("tensor")
    shift = lax.rem(index * WIDTH, BLOCK)
    loads = [
        pltpu.make_async_copy(branch_hbm.at[0], branch_w.at[0], load_sem.at[0]),
        pltpu.make_async_copy(branch_hbm.at[1], branch_w.at[1], load_sem.at[1]),
        pltpu.make_async_copy(out_hbm, out_w, load_sem.at[2]),
    ]
    for load in loads:
        load.start()
    ready = announce(dp_peers() + tensor_peers() + [far_peer()])
    stores = []

    def store(number, source, target):
        copy = pltpu.make_async_copy(source, target, store_sem.at[number])
        copy.start()
        stores.append(copy)

    send_halo = remote(
        tokens.at[pl.ds(ROWS - 16, 16)],
        halo,
        halo_send,
        halo_recv,
        {"dp": lax.rem(me + 1, N_DP)},
    )
    wide_gates(gates, wide, shift)
    placing[...] = place_matrix(shift)
    gain = gains[0:1, :]
    norm_rows(tokens, normed_one, gain, ROWS)
    ready()
    send_halo.start()
    store(0, normed_one, outs[0])
    loads[0].wait()

    def branch_tile(first):
        at = pl.ds(first, 128)
        value = times_transposed(normed_one[at, :], branch_w[0])
        ext[pl.ds(first + 16, 128), :] = value.astype(jnp.bfloat16).astype(jnp.float32)

    tiles(4, 128, branch_tile)
    send_halo.wait()
    norm_rows(halo, halo_norm, gain, 16)
    ext[0:16, :] = times_transposed(halo_norm[...], branch_w[0]).astype(jnp.bfloat16).astype(jnp.float32)

    def conv_tile(first):
        near = ext[pl.ds(first + 8, 136), :]
        total = chan[0:1, :] * near[8:]
        for tap in range(1, 4):
            counted = flags[pl.ds(first, 128), tap : tap + 1] > 0.0
            total = total + chan[tap : tap + 1, :] * jnp.where(counted, near[8 - tap : 136 - tap], 0.0)
        window[pl.ds(first, 128), :] = matmul(total.astype(jnp.bfloat16), placing[...]).astype(
            jnp.bfloat16
        )

    tiles(4, 128, conv_tile)
    store(1, ext, outs[1])
    up, down = beside_peers()
    to_up = remote(
        window.at[:, pl.ds(BLOCK, BLOCK)], low, side_send.at[0], side_recv.at[0], up
    )
    to_down = remote(window.at[:, pl.ds(0, BLOCK)], high, side_send.at[1], side_recv.at[1], down)
    to_up.start()
    to_down.start()
    loads[1].wait()

    def gelu_tile(first):
        at = pl.ds(first, 128)
        branch_y[at, :] = times_transposed(normed_one[at, :], branch_w[1])

    tiles(4, 128, gelu_tile)
    store(2, branch_y, outs[6])
    to_up.wait()
    to_down.wait()

    def window_tile(first):
        at = pl.ds(first, 128)
        own_conv = lax.dot_general(
            window[at, :], placing[...], (((1,), (1,)), ((), ())), preferred_element_type=jnp.float32
        )
        from_low = jnp.where(shift != 0, low[at, :].astype(jnp.float32), 0.0)
        from_high = jnp.where(shift != 192, high[at, :].astype(jnp.float32), 0.0)
        whole = window[at, :].astype(jnp.float32) + jnp.concatenate([from_low, from_high], 1)
        whole = whole.astype(jnp.bfloat16)
        window[at, :] = whole
        a = times_transposed(whole, wide[0])
        x = times_transposed(whole, wide[1])
        pre_a[at, :] = a
        pre_x[at, :] = x
        reset = flags[at, 4:5] > 0.0
        log_a = -8.0 * jax.nn.sigmoid(a) * chan[5:6, :]
        carry[at, :] = jnp.where(reset, 0.0, jnp.exp(log_a))
        scale = jnp.where(reset, 1.0, jnp.sqrt(one_less_exp(2.0 * log_a)))
        update[at, :] = own_conv * jax.nn.sigmoid(x) * scale

    tiles(4, 128, window_tile)
    store(3, window, outs[2])
    store(4, pre_a, outs[3])
    store(5, pre_x, outs[4])
    carry[ROWS : ROWS + 8, :] = jnp.ones((8, WIDTH), jnp.float32)
    store(6, carry, outs[5])
    prod, value = local_scan(
        lambda first: carry[pl.ds(first, 8), :],
        lambda first: update[pl.ds(first, 8), :],
        values,
        prods,
        False,
    )
    slots[me, 0:1, :] = prod[0:1]
    slots[me, 1:2, :] = value[0:1]
    copies = start_share(slots, slot_send, slot_recv)

    def activate(first):
        at = pl.ds(first, 64)
        y = branch_y[at, :]
        gelu_y[at, :] = gelu_parts(y)[0]

    tiles(8, 64, activate)
    for copy in copies:
        copy.wait()
    before = jnp.zeros((1, WIDTH), jnp.float32)
    for place_at in range(N_DP - 1):
        longer = slots[place_at, 0:1, :] * before + slots[place_at, 1:2, :]
        before = jnp.where(place_at < me, longer, before)

    state[0:8, :] = jnp.broadcast_to(before, (8, WIDTH))

    def finish(first):
        at = pl.ds(first, 64)
        total = values[at, :] + prods[at, :] * before
        state[pl.ds(first + 8, 64), :] = total
        mixed[at, :] = (total * gelu_y[at, :]).astype(jnp.bfloat16)

    tiles(8, 64, finish)
    store(7, state, outs[7])
    store(8, mixed, outs[8])
    loads[2].wait()

    def produce(by):
        at = pl.ds(pl.multiple_of(chip_row(by, 0), 128), 128)
        partial[at, :] = matmul(mixed[at, :], out_w[...]).astype(jnp.bfloat16)

    summed = TensorSum(chip_row, partial, *scratch)
    summed.start(produce)
    _, core = place()
    total = tokens[pl.ds(chip_row(0, core), OWN), :].astype(jnp.float32) + summed.finish()
    residual[...] = total
    block[...] = rms_norm(total, gains[1:2, :]).astype(jnp.bfloat16)
    for copy in stores:
        copy.wait()


def saved_shapes():
    f32, bf16 = jnp.float32, jnp.bfloat16
    return (
        ((ROWS, D), bf16),
        ((ROWS + 16, WIDTH), f32),
        ((ROWS, 2 * BLOCK), bf16),
        ((ROWS, WIDTH), f32),
        ((ROWS, WIDTH), f32),
        ((ROWS + 8, WIDTH), f32),
        ((ROWS, WIDTH), f32),
        ((ROWS + 8, WIDTH), f32),
        ((ROWS, WIDTH), bf16),
    )


def mixer_forward(tokens, branch_in, gate_blocks, out_proj, chan, gains, flags):
    f32, bf16 = jnp.float32, jnp.bfloat16
    dma = pltpu.SemaphoreType.DMA
    here = pl.BlockSpec(memory_space=pltpu.VMEM)
    there = pl.BlockSpec(memory_space=pl.ANY)
    shapes = saved_shapes()
    inside = shapes[:6] + (shapes[7], shapes[6], shapes[8])
    return pl.pallas_call(
        forward_kernel,
        out_shape=(
            jax.ShapeDtypeStruct((OWN, D), f32),
            jax.ShapeDtypeStruct((OWN, D), bf16),
            *(jax.ShapeDtypeStruct(*shape) for shape in shapes),
        ),
        in_specs=[here, there, here, there, here, here, here],
        out_specs=tuple([here] * 2 + [there] * 9),
        scratch_shapes=[pltpu.VMEM(*shape) for shape in inside]
        + [
            pltpu.VMEM((2, WIDTH, D), bf16),
            pltpu.VMEM((WIDTH, D), bf16),
            pltpu.VMEM((16, D), bf16),
            pltpu.VMEM((16, D), bf16),
            pltpu.VMEM((2, WIDTH, 2 * BLOCK), bf16),
            pltpu.VMEM((WIDTH, 2 * BLOCK), bf16),
            pltpu.VMEM((ROWS, WIDTH), f32),
            pltpu.VMEM((ROWS, WIDTH), f32),
            pltpu.VMEM((ROWS, WIDTH), f32),
            pltpu.VMEM((ROWS, WIDTH), f32),
            pltpu.VMEM((ROWS, BLOCK), bf16),
            pltpu.VMEM((ROWS, BLOCK), bf16),
            pltpu.VMEM((N_DP, 8, WIDTH), f32),
            pltpu.VMEM((ROWS, D), bf16),
            dma((3,)),
            dma((9,)),
            dma,
            dma,
            dma((2,)),
            dma((2,)),
            dma((N_DP,)),
            dma((N_DP,)),
        ]
        + reduce_scratch(),
        compiler_params=params(1),
    )(tokens, branch_in, gate_blocks, out_proj, chan, gains, flags)


def norm_back(value, gain, grad):
    scale = lax.rsqrt(jnp.mean(value * value, axis=-1, keepdims=True) + NORM_EPS)
    unit = value * scale
    scaled = grad * gain
    back = scale * (scaled - unit * jnp.mean(scaled * unit, axis=-1, keepdims=True))
    return back, jnp.sum(grad * unit, axis=0, keepdims=True)


def back_kernel(
    block, residual, gains, chan, flags, dy_hbm, ffn_hbm, down_hbm, tokens, out_hbm, branch_hbm, gates_hbm, *rest
):
    saved, rest = rest[:9], rest[9:]
    tokens_grad, out, gain_sum, channel_sum, blocks_share, *rest = rest
    shares, (down_grad, up_grad, gate_grad, mixer_grad), rest = rest[:4], rest[4:8], rest[8:]
    (
        normed, rounded, grad, grad_gain_two, partial, stage, near, near_blocks,
        low_in, high_in, slots, halo, halo_in, gain_t, gain_dp, chan_dp, blocks_grad,
        load_sem, stage_sem, share_sem, slot_send, slot_recv, side_send, side_recv, halo_send, halo_recv,
        t_send, t_recv, g_send, g_recv, c_send, c_recv, reuse_sem, free_sem, *scratch
    ) = rest
    me, index = lax.axis_index("dp"), lax.axis_index("tensor")
    x, core = place()
    shift = lax.rem(index * WIDTH, BLOCK)
    ready = announce(dp_peers() + tensor_peers() + [far_peer()])

    def take(count):
        taken = scratch[:count]
        del scratch[:count]
        return taken

    sum_scratch = take(7)
    summed = TensorSum(arrival_row, partial, *sum_scratch)
    summed_out = TensorSum(arrival_row, partial, *sum_scratch)
    summed_last = TensorSum(chip_row, partial, *sum_scratch)
    before = TensorGather(arrival_row, normed, *take(4))
    after = TensorGather(chip_row, rounded, *take(4))
    first = take(4)
    down_sum = DataSum(down_grad, *first, near, *take(3), HALF)
    up_sum = DataSum(up_grad, *take(4), near, *take(3), HALF)
    gate_sum = DataSum(gate_grad, *take(4), near, *take(3), HALF)
    mixer_sum = DataSum(mixer_grad, *first, near, *take(3), HALF)
    blocks_sum = DataSum(blocks_grad, *take(4), near_blocks, *take(3), GATE_HALF)

    def weight_grad(target, jobs):
        pending = None
        for z in range(4):
            columns = pl.ds(z * 640, 640)
            parts = [transposed_times(left[:, columns], right[...]) for left, right in jobs]
            whole = parts[0] if len(parts) == 1 else jnp.concatenate(parts, 1)
            if pending is not None:
                pending.wait()
            stage[...] = whole.astype(jnp.bfloat16).reshape(4, 2, HALF, HIDE)
            pending = pltpu.make_async_copy(stage, target.at[z], stage_sem)
            pending.start()
        pending.wait()

    def ffn_part(dy, ffn_w, down_w, hidden, to_gate, to_up, gate_pre, up_pre, grad_hidden):
        loads = []

        def load(source, target):
            copy = pltpu.make_async_copy(source, target, load_sem.at[len(loads)])
            copy.start()
            loads.append(copy)

        for by, spot in ARRIVAL.items():
            load(
                dy_hbm.at[pl.ds(pl.multiple_of(lax.rem(x + by, 4) * 128, 128), 128)],
                dy.at[pl.ds(spot * 128, 128)],
            )
        load(down_hbm, down_w)
        load(ffn_hbm.at[pl.ds(0, HIDE)], ffn_w.at[pl.ds(0, HIDE)])
        load(ffn_hbm.at[pl.ds(HIDE, HIDE)], ffn_w.at[pl.ds(HIDE, HIDE)])
        pieces = ((0, 384), (384, 384), (768, 192))
        ready()
        before.start(block[...])
        for copy in loads[:5]:
            copy.wait()
        for start, size in pieces:
            units = pl.ds(start, size)
            grad_hidden[:, units] = times_transposed(dy[...], down_w[units, :])
        for copy in loads[5:]:
            copy.wait()
        before.arrive(1)
        before.settle(0)
        before.settle(1)
        for group in range(2):
            if group:
                before.arrive(3)
                before.arrive(2)
                before.settle(3)
                before.settle(2)
            rows = pl.ds(group * 256, 256)
            for start, size in pieces:
                units = pl.ds(start, size)
                gate_pre[:, 0:size] = times_transposed(normed[rows, :], ffn_w[units, :])
                up_pre[:, 0:size] = times_transposed(normed[rows, :], ffn_w[pl.ds(HIDE + start, size), :])

                def activate(first, units=units, size=size, group=group):
                    here = pl.ds(first, 32)
                    at = pl.ds(pl.multiple_of(group * 256 + first, 32), 32)
                    value, slope = gelu_parts(gate_pre[here, 0:size])
                    up, back = up_pre[here, 0:size], grad_hidden[at, units]
                    hidden[at, units] = (value * up).astype(jnp.bfloat16)
                    to_up[at, units] = (back * value).astype(jnp.bfloat16)
                    to_gate[at, units] = (back * up * slope).astype(jnp.bfloat16)

                tiles(256 // 32, 32, activate)
        before.finish()

        def produce(by):
            at = pl.ds(arrival_row(by, 0), 128)
            total = matmul(to_gate[at, :], ffn_w[0:HIDE, :]) + matmul(
                to_up[at, :], ffn_w[HIDE : 2 * HIDE, :]
            )
            partial[at, :] = total.astype(jnp.bfloat16)

        weight_grad(down_grad, [(dy, hidden)])
        down_sum.start()
        summed.start(produce)
        weight_grad(up_grad, [(normed, to_up)])
        up_sum.start()
        down_sum.middle()
        norm_grad = summed.finish()
        back, gain_part = norm_back(residual[...], gains[1:2, :], norm_grad)
        back = back + dy[pl.ds(arrival_row(0, core), OWN), :].astype(jnp.float32)
        grad[...] = back
        grad_gain_two[...] = gain_part
        after.start(back.astype(jnp.bfloat16))

        def produce_out(first):
            at = pl.ds(first, 128)
            partial[at, :] = matmul(hidden[at, :], down_w[...]).astype(jnp.bfloat16)

        tiles(4, 128, produce_out)
        weight_grad(gate_grad, [(normed, to_gate)])
        gate_sum.start()

    f32, bf16 = jnp.float32, jnp.bfloat16
    pl.run_scoped(
        ffn_part,
        pltpu.VMEM((ROWS, D), bf16),
        pltpu.VMEM((2 * HIDE, D), bf16),
        pltpu.VMEM((HIDE, D), bf16),
        pltpu.VMEM((ROWS, HIDE), bf16),
        pltpu.VMEM((ROWS, HIDE), bf16),
        pltpu.VMEM((ROWS, HIDE), bf16),
        pltpu.VMEM((256, 384), f32),
        pltpu.VMEM((256, 384), f32),
        pltpu.VMEM((ROWS, HIDE), f32),
    )

    def mixer_part(
        normed_one, ext, window, pre_a, pre_x, carry, branch_y, state, mixed,
        out_w, branch_w, gates, own, wide, to_y, local, sums, prods, to_a, to_gx, window_grad, low, high, conv_grad,
        share_stage,
    ):
        targets = (
            normed_one, ext, window, pre_a, pre_x, carry, branch_y, state, mixed, out_w, branch_w, gates, own,
        )
        sources = (
            *saved,
            out_hbm,
            branch_hbm,
            gates_hbm,
            tokens.at[pl.ds(chip_row(0, core), OWN)],
        )
        def keep_share(number):
            copy = pltpu.make_async_copy(share_stage, shares[number], share_sem)
            copy.start()
            copy.wait()

        loads = []
        for source, target in zip(sources, targets):
            loads.append(pltpu.make_async_copy(source, target, load_sem.at[len(loads)]))
            loads[-1].start()
        for by in (1, 3, 2):
            after.arrive(by)
        for by in (0, 1, 3, 2):
            after.settle(by)
        after.finish()
        for step, by in enumerate(summed_out.ORDER):
            summed_out.give(by)
        for by in (2, 1, 3):
            summed_out.pass_on(by)
        for copy in loads:
            copy.wait()
        wide_gates(gates, wide, shift)

        def mixed_tile(first):
            at = pl.ds(first, 128)
            local[at, :] = times_transposed(rounded[at, :], out_w[...])

        tiles(4, 128, mixed_tile)

        def gelu_tile(first):
            at = pl.ds(first, 64)
            value, slope = gelu_parts(branch_y[at, :])
            mixed_grad = local[at, :]
            to_y[at, :] = (mixed_grad * state[pl.ds(first + 8, 64), :] * slope).astype(jnp.bfloat16)
            local[at, :] = mixed_grad * value

        tiles(8, 64, gelu_tile)
        prod, value = local_scan(
            lambda first: carry[pl.ds(first, 16), :][1:9],
            lambda first: local[pl.ds(first, 8), :],
            sums,
            prods,
            True,
        )
        slots[me, 0:1, :] = carry[0:1, :] * prod[0:1]
        slots[me, 1:2, :] = carry[0:1, :] * value[0:1]
        copies = start_share(slots, slot_send, slot_recv)
        down_sum.turn()

        for copy in copies:
            copy.wait()
        up_sum.middle()
        later = jnp.zeros((1, WIDTH), jnp.float32)
        for place_at in range(N_DP - 1, 0, -1):
            longer = slots[place_at, 0:1, :] * later + slots[place_at, 1:2, :]
            later = jnp.where(place_at > me, longer, later)
        plus, decay_slope = chan[5:6, :], chan[6:7, :]
        zero_row = jnp.zeros((1, WIDTH), jnp.float32)

        def gate_tile(first, decay_grad):
            at = pl.ds(first, 64)
            total = sums[at, :] + prods[at, :] * later
            near = state[pl.ds(first, 72), :]
            conv = lax.dot_general(
                window[at, :], place_matrix(shift), (((1,), (1,)), ((), ())), preferred_element_type=jnp.float32
            )
            reset = flags[at, 4:5] > 0.0
            gate_a, gate_x = jax.nn.sigmoid(pre_a[at, :]), jax.nn.sigmoid(pre_x[at, :])
            log_a = -8.0 * gate_a * plus
            keep = jnp.exp(log_a)
            scale = jnp.sqrt(one_less_exp(2.0 * log_a))
            scale_here = jnp.where(reset, 1.0, scale)
            conv_grad[at, :] = total * gate_x * scale_here
            to_gx[at, :] = (total * conv * scale_here * gate_x * (1.0 - gate_x)).astype(jnp.bfloat16)
            log_grad = total * near[7:71] * keep - total * conv * gate_x * keep * keep / scale
            log_grad = jnp.where(reset, 0.0, log_grad)
            to_a[at, :] = (log_grad * (-8.0 * plus) * gate_a * (1.0 - gate_a)).astype(jnp.bfloat16)
            return decay_grad + jnp.sum(log_grad * (-8.0 * gate_a), axis=0, keepdims=True)

        decay_grad = lax.fori_loop(
            0, 8, lambda i, held: gate_tile(pl.multiple_of(i * 64, 64), held), zero_row
        )
        decay_grad = decay_grad * decay_slope

        def window_tile(first):
            at = pl.ds(first, 128)
            total = matmul(to_a[at, :], wide[0]) + matmul(to_gx[at, :], wide[1])
            window_grad[at, :] = total
            low[at, :] = total[:, 0:BLOCK].astype(jnp.bfloat16)
            high[at, :] = total[:, BLOCK : 2 * BLOCK].astype(jnp.bfloat16)

        tiles(4, 128, window_tile)
        up, down = beside_peers()
        to_up = remote(high, low_in, side_send.at[0], side_recv.at[0], up)
        to_down = remote(low, high_in, side_send.at[1], side_recv.at[1], down)
        to_up.start()
        to_down.start()
        column = lax.broadcasted_iota(jnp.int32, (BLOCK, WIDTH), 1)
        chosen = []
        for right in (to_a, to_gx):
            both = transposed_times(window[...], right[...])
            chosen.append(
                jnp.where(column + shift < BLOCK, both[0:BLOCK], both[BLOCK : 2 * BLOCK])
            )
        blocks_grad[...] = jnp.concatenate(chosen, 1).reshape(4, 4, 2, GATE_HALF, 2 * WIDTH)
        down_sum.finish(share_stage)
        keep_share(0)
        for peer in ring_peers():
            pl.semaphore_signal(reuse_sem, inc=1, device_id=peer, device_id_type=MESH)
        to_up.wait()
        to_down.wait()

        def conv_tile(first):
            at = pl.ds(first, 64)
            from_low = jnp.where(shift != 0, low_in[at, :].astype(jnp.float32), 0.0)
            from_high = jnp.where(shift != 192, high_in[at, :].astype(jnp.float32), 0.0)
            total = window_grad[at, :] + jnp.concatenate([from_low, from_high], 1)
            total = pltpu.roll(total, lax.rem(2 * BLOCK - shift, 2 * BLOCK), 1)
            conv_grad[at, :] = conv_grad[at, :] + total[:, 0:WIDTH]

        tiles(8, 64, conv_tile)
        conv_grad[ROWS : ROWS + 8, :] = jnp.zeros((8, WIDTH), jnp.float32)
        head = conv_grad[0:8, :]
        rows = []
        for row in range(3):
            total = zero_row
            for tap in range(3 - row, 4):
                from_row = row - 3 + tap
                counted = flags[from_row : from_row + 1, tap : tap + 1] > 0.0
                total = total + chan[tap : tap + 1, :] * jnp.where(
                    counted, head[from_row : from_row + 1], 0.0
                )
            rows.append(total)
        halo[0:5, :] = jnp.zeros((5, WIDTH), jnp.float32)
        for row in range(3):
            halo[5 + row : 6 + row, :] = rows[row]
        send_halo = remote(halo, halo_in, halo_send, halo_recv, {"dp": lax.rem(me + N_DP - 1, N_DP)})
        send_halo.start()
        blocks_sum.start()

        def tap_tile(first, held):
            at = pl.ds(first, 64)
            near = conv_grad[pl.ds(first, 72), :]
            marks = flags[pl.ds(first, 72), :]
            behind = ext[pl.ds(first + 8, 72), :]
            total = chan[0:1, :] * near[0:64]
            taps = [held[0] + jnp.sum(near[0:64] * behind[8:72], axis=0, keepdims=True)]
            for tap in range(1, 4):
                counted = marks[tap : tap + 64, tap : tap + 1] > 0.0
                total = total + chan[tap : tap + 1, :] * jnp.where(counted, near[tap : tap + 64], 0.0)
                here = jnp.where(marks[0:64, tap : tap + 1] > 0.0, near[0:64], 0.0)
                taps.append(
                    held[tap] + jnp.sum(here * behind[8 - tap : 72 - tap], axis=0, keepdims=True)
                )
            local[at, :] = total
            return tuple(taps)

        tap_grads = lax.fori_loop(
            0, 8, lambda i, held: tap_tile(pl.multiple_of(i * 64, 64), held), (zero_row,) * 4
        )
        for tap in range(4):
            chan_dp[me, tap : tap + 1, :] = tap_grads[tap]
        chan_dp[me, 4:5, :] = decay_grad
        chan_dp[me, 5:8, :] = jnp.zeros((3, WIDTH), jnp.float32)
        channel_copies = start_share(chan_dp, c_send, c_recv)
        gate_sum.middle()
        send_halo.wait()
        local[ROWS - 8 : ROWS, :] = local[ROWS - 8 : ROWS, :] + halo_in[...]
        to_x = to_a
        to_x[...] = local[...].astype(jnp.bfloat16)

        def produce(by):
            at = pl.ds(pl.multiple_of(chip_row(by, 0), 128), 128)
            total = matmul(to_x[at, :], branch_w[0]) + matmul(to_y[at, :], branch_w[1])
            partial[at, :] = total.astype(jnp.bfloat16)

        branches = jnp.concatenate(
            [to_y[...].astype(jnp.float32), to_x[...].astype(jnp.float32)], 1
        ).astype(jnp.bfloat16)
        weight_grad(mixer_grad, [(normed_one, branches), (rounded, mixed)])
        pl.semaphore_wait(reuse_sem, 6)
        mixer_sum.start()
        up_sum.turn()
        out[...] = (residual[...] + summed_out.finish()).astype(jnp.bfloat16)
        for peer in tensor_peers():
            pl.semaphore_signal(free_sem, inc=1, device_id=peer, device_id_type=MESH)
        blocks_sum.middle()
        pl.semaphore_wait(free_sem, 4)
        summed_last.start(produce)
        mixer_sum.middle()
        norm_grad = summed_last.finish()
        before_norm, gain_part = norm_back(own[...].astype(jnp.float32), gains[0:1, :], norm_grad)
        tokens_grad[...] = (grad[...] + before_norm).astype(jnp.bfloat16)
        gain_t[index, 0:1, :] = gain_part
        gain_t[index, 1:2, :] = grad_gain_two[...]
        gain_copies = []
        for by in range(1, N_T):
            copy = remote(
                gain_t.at[index],
                gain_t.at[index],
                t_send.at[by],
                t_recv.at[by],
                {"tensor": lax.rem(index + by, N_T)},
            )
            copy.start()
            gain_copies.append(copy)
        gate_sum.turn()
        for copy in gain_copies:
            copy.wait()
        total = gain_t[0]
        for by in range(1, N_T):
            total = total + gain_t[by]
        gain_dp[me] = total
        gain_copies = start_share(gain_dp, g_send, g_recv)
        up_sum.finish(share_stage)
        keep_share(1)
        blocks_sum.turn()
        gate_sum.finish(share_stage)
        keep_share(2)
        mixer_sum.turn()
        for copy in channel_copies + gain_copies:
            copy.wait()
        total, channels = gain_dp[0], chan_dp[0]
        for by in range(1, N_DP):
            total = total + gain_dp[by]
            channels = channels + chan_dp[by]
        gain_sum[...] = total
        channel_sum[...] = channels
        blocks_sum.finish(blocks_share)
        mixer_sum.finish(share_stage)
        keep_share(3)


    wide_f32 = pltpu.VMEM((ROWS, WIDTH), f32)
    wide_bf16 = pltpu.VMEM((ROWS, WIDTH), bf16)
    pl.run_scoped(
        mixer_part,
        *(pltpu.VMEM(*shape) for shape in saved_shapes()),
        pltpu.VMEM((WIDTH, D), bf16),
        pltpu.VMEM((2, WIDTH, D), bf16),
        pltpu.VMEM((2, WIDTH, BLOCK), bf16),
        pltpu.VMEM((OWN, D), bf16),
        pltpu.VMEM((2, WIDTH, 2 * BLOCK), bf16),
        wide_bf16,
        wide_f32,
        wide_f32,
        wide_f32,
        wide_bf16,
        wide_bf16,
        pltpu.VMEM((ROWS, 2 * BLOCK), f32),
        pltpu.VMEM((ROWS, BLOCK), bf16),
        pltpu.VMEM((ROWS, BLOCK), bf16),
        pltpu.VMEM((ROWS + 8, WIDTH), f32),
        pltpu.VMEM((2 * HALF, HIDE), f32),
    )


def backward(block, residual, gains, chan, flags, dy, ffn_t, down, tokens, out_proj, branch_t, gates_t, saved):
    f32, bf16 = jnp.float32, jnp.bfloat16
    dma = pltpu.SemaphoreType.DMA
    here = pl.BlockSpec(memory_space=pltpu.VMEM)
    there = pl.BlockSpec(memory_space=pl.ANY)
    share = jax.ShapeDtypeStruct((2 * HALF, HIDE), f32)
    shared = jax.ShapeDtypeStruct((4, 4, 2, HALF, HIDE), bf16)
    return pl.pallas_call(
        back_kernel,
        out_shape=(
            jax.ShapeDtypeStruct((OWN, D), bf16),
            jax.ShapeDtypeStruct((OWN, D), bf16),
            jax.ShapeDtypeStruct((2, D), f32),
            jax.ShapeDtypeStruct((8, WIDTH), f32),
            jax.ShapeDtypeStruct((2 * GATE_HALF, 2 * WIDTH), f32),
            *[share] * 4,
            *[shared] * 4,
        ),
        in_specs=[here] * 5 + [there] * 16,
        out_specs=tuple([here] * 5 + [there] * 8),
        scratch_shapes=[
            pltpu.VMEM((ROWS, D), bf16),
            pltpu.VMEM((ROWS, D), bf16),
            pltpu.VMEM((OWN, D), f32),
            pltpu.VMEM((1, D), f32),
            pltpu.VMEM((ROWS, D), bf16),
            pltpu.VMEM((4, 2, HALF, HIDE), bf16),
            pltpu.VMEM((2, 2, HALF, HIDE), bf16),
            pltpu.VMEM((2, 2, GATE_HALF, 2 * WIDTH), f32),
            pltpu.VMEM((ROWS, BLOCK), bf16),
            pltpu.VMEM((ROWS, BLOCK), bf16),
            pltpu.VMEM((N_DP, 8, WIDTH), f32),
            pltpu.VMEM((8, WIDTH), f32),
            pltpu.VMEM((8, WIDTH), f32),
            pltpu.VMEM((N_T, 2, D), f32),
            pltpu.VMEM((N_DP, 2, D), f32),
            pltpu.VMEM((N_DP, 8, WIDTH), f32),
            pltpu.VMEM((4, 4, 2, GATE_HALF, 2 * WIDTH), f32),
            dma((13,)),
            dma,
            dma,
            dma((N_DP,)),
            dma((N_DP,)),
            dma((2,)),
            dma((2,)),
            dma,
            dma,
            dma((N_T,)),
            dma((N_T,)),
            dma((N_DP,)),
            dma((N_DP,)),
            dma((N_DP,)),
            dma((N_DP,)),
            pltpu.SemaphoreType.REGULAR,
            pltpu.SemaphoreType.REGULAR,
        ]
        + reduce_scratch()
        + gather_scratch()
        + gather_scratch()
        + data_buffers(HALF, HIDE, bf16)
        + data_sems()
        + data_buffers(HALF, HIDE, bf16)
        + data_sems()
        + data_buffers(HALF, HIDE, bf16)
        + data_sems()
        + data_sems()
        + data_buffers(GATE_HALF, 2 * WIDTH, f32)
        + data_sems(),
        compiler_params=params(2),
    )(block, residual, gains, chan, flags, dy, ffn_t, down, tokens, out_proj, branch_t, gates_t, *saved)


def rms_norm(values, gain):
    return values * lax.rsqrt(jnp.mean(values * values, axis=-1, keepdims=True) + NORM_EPS) * gain


def matmul(left, right):
    return jnp.dot(left, right, preferred_element_type=jnp.float32)


def times_transposed(left, right):
    return lax.dot_general(
        left, right, (((1,), (1,)), ((), ())), preferred_element_type=jnp.float32
    )


def transposed_times(left, right):
    return lax.dot_general(
        left, right, (((0,), (0,)), ((), ())), preferred_element_type=jnp.float32
    )


def adam_step(weight, grad, first, second, rate, decay):
    first_new = BETA_ONE * first + (1.0 - BETA_ONE) * grad
    second_new = BETA_TWO * second + (1.0 - BETA_TWO) * grad * grad
    first_hat = first_new / (1.0 - BETA_ONE**STEP)
    second_hat = second_new / (1.0 - BETA_TWO**STEP)
    weight_new = weight - rate * (first_hat / (jnp.sqrt(second_hat) + ADAM_EPS) + decay * weight)
    return (first_new, second_new, weight_new)


SHARE = 2 * HALF
SPAN = 384
DECAY = 0.1
BRANCH_RATE, GATE_RATE, OUT_RATE = 3.0 * D**-0.5, 3.0 * BLOCK**-0.5, 3.0 * (L // 8) ** -0.5
FFN_RATE, DOWN_RATE = 3.0 * D**-0.5, 3.0 * (F // 2) ** -0.5


def update_jobs():
    return (
        ("down", None, 0, 0, HIDE, 0, DOWN_RATE),
        ("ffn", 1, 1, 0, HIDE, HIDE, FFN_RATE),
        ("ffn", 0, 2, 0, HIDE, 0, FFN_RATE),
        ("out", None, 3, 2 * WIDTH, WIDTH, 0, OUT_RATE),
        ("branch", 1, 3, 0, WIDTH, WIDTH, BRANCH_RATE),
        ("branch", 0, 3, WIDTH, WIDTH, 0, BRANCH_RATE),
        ("gate", 0, 4, 0, WIDTH, 0, GATE_RATE),
        ("gate", 1, 4, WIDTH, WIDTH, WIDTH, GATE_RATE),
    )


ARRAYS = ("down", "ffn", "out", "branch", "gate")


def update_kernel(*refs):
    shares, weights = refs[:5], dict(zip(ARRAYS, refs[5:10]))
    moments = {name: refs[10 + 2 * i : 12 + 2 * i] for i, name in enumerate(ARRAYS)}
    small, small_outs = refs[20:28], refs[43:49]
    outs = {name: refs[28 + 3 * i : 31 + 3 * i] for i, name in enumerate(ARRAYS)}
    windows = dict(zip(ARRAYS, refs[49:54]))
    held = refs[54:62]
    in_sem, window_sem, out_sem = refs[62:]
    me = lax.axis_index("dp")
    begin = jnp.minimum(me * SHARE // 128 * 128, D - SPAN)
    copies = {}

    def copy(key, source, target, sem):
        copies[key] = pltpu.make_async_copy(source, target, sem)
        copies[key].start()

    jobs = update_jobs()
    waiting = list(ARRAYS)
    for number, (name, part, *_) in enumerate(jobs):
        if name not in copies:
            source = weights[name]
            if name != "gate":
                source = source.at[:, pl.ds(pl.multiple_of(begin, 128), SPAN)]
            copy(name, source, windows[name], window_sem.at[ARRAYS.index(name)])
        for which in range(2):
            source = moments[name][which]
            source = source if part is None else source.at[part]
            copy((number, which), source, held[number].at[which], in_sem.at[number, which])
    value, grad, mean, square = (ref[...] for ref in small[:4])
    for ref, new in zip(small_outs[:3], adam_step(value, grad, mean, square, 1.0, 0.0)):
        ref[...] = new
    value, grad, mean, square = (ref[...] for ref in small[4:])
    row = lax.broadcasted_iota(jnp.int32, value.shape, 0)
    rates = jnp.where(row == 4, 3.0, 1.0)
    for ref, new in zip(small_outs[3:], adam_step(value, grad[:5], mean, square, rates, 0.0)):
        ref[...] = new
    for number, (name, part, share, lane, width, row, rate) in enumerate(jobs):
        if name in waiting:
            waiting.remove(name)
            copies[name].wait()
        count = 16 if name == "gate" else SHARE
        span = BLOCK if name == "gate" else SPAN
        offset = me * count if name == "gate" else me * SHARE - begin
        mine = lax.broadcasted_iota(jnp.int32, (count, span), 0) + offset
        lanes = lax.broadcasted_iota(jnp.int32, (count, span), 1)
        chosen = jnp.where(lanes == mine, 1.0, 0.0).astype(jnp.bfloat16)
        box = held[number]
        box[2] = times_transposed(chosen, windows[name][row : row + width, :])
        for which in range(2):
            copies[number, which].wait()

        def body(first, box=box, share=share, lane=lane, width=width, rate=rate):
            at = pl.ds(first, 16)
            grad = shares[share][at, lane : lane + width]
            new = adam_step(box[2, at, :], grad, box[0, at, :], box[1, at, :], rate, DECAY)
            for which in range(3):
                box[which, at, :] = new[which]

        tiles(count // 16, 16, body, 1 if count == 16 else 5)
        for which in range(3):
            target = outs[name][which]
            target = target if part is None else target.at[part]
            copy((number, which), box.at[which], target, out_sem.at[number, which])
    for number in range(len(jobs)):
        for which in range(3):
            copies[number, which].wait()


def update_weights(shares, weights, moments, small):
    f32, bf16 = jnp.float32, jnp.bfloat16
    dma = pltpu.SemaphoreType.DMA
    here = pl.BlockSpec(memory_space=pltpu.VMEM)
    there = pl.BlockSpec(memory_space=pl.ANY)
    jobs = update_jobs()
    return pl.pallas_call(
        update_kernel,
        out_shape=tuple(
            jax.ShapeDtypeStruct(value.shape, f32)
            for value in (*moments[::2], small[0], small[4])
            for _ in range(3)
        ),
        in_specs=[here] * 5 + [there] * 15 + [here] * 8,
        out_specs=tuple([there] * 15 + [here] * 6),
        scratch_shapes=[
            pltpu.VMEM((weight.shape[0], BLOCK if name == "gate" else SPAN), bf16)
            for name, weight in zip(ARRAYS, weights)
        ]
        + [pltpu.VMEM((3, 16 if job[0] == "gate" else SHARE, job[4]), f32) for job in jobs]
        + [dma((len(jobs), 2)), dma((5,)), dma((len(jobs), 3))],
        compiler_params=pltpu.CompilerParams(vmem_limit_bytes=63 * 2**20),
    )(*shares, *weights, *moments, *small)


def shards(
    tokens,
    cotangent,
    segments,
    gains,
    channel_params,
    branch_in,
    gate_blocks,
    out_proj,
    ffn_in,
    ffn_down,
    gains_first,
    gains_second,
    channel_first,
    channel_second,
    branch_first,
    branch_second,
    gate_first,
    gate_second,
    out_first,
    out_second,
    ffn_in_first,
    ffn_in_second,
    down_first,
    down_second,
):
    rows = ROWS
    data_index = lax.axis_index("dp")

    padded_ids = jnp.concatenate([jnp.full((3,), -1, jnp.int32), segments])
    local_ids = lax.dynamic_slice_in_dim(padded_ids, data_index * rows, rows + 3)
    marks = [local_ids[3 - tap : 3 - tap + rows] == local_ids[3:] for tap in range(4)]
    marks.append(local_ids[3:] != local_ids[2 : 2 + rows])
    flags = jnp.pad(jnp.stack(marks, 1).astype(jnp.float32), ((0, 8), (0, 3)))
    decay_param = channel_params[4:5]
    chan = jnp.concatenate(
        [channel_params, jax.nn.softplus(decay_param), jax.nn.sigmoid(decay_param), decay_param], 0
    )
    branch_t = branch_in.swapaxes(1, 2)
    gates_t = gate_blocks.swapaxes(1, 2)
    ffn_t = ffn_in.swapaxes(1, 2).reshape(2 * HIDE, D)
    residual_own, block, *saved = mixer_forward(
        tokens, branch_t, gates_t, out_proj, chan, gains, flags
    )
    tokens_grad, block_out, gain_grad, channel_grad, blocks_share, down_share, up_share, gate_share, mixer_share, *_ = (
        backward(
            block,
            residual_own,
            gains,
            chan,
            flags,
            cotangent,
            ffn_t,
            ffn_down,
            tokens,
            out_proj,
            branch_t,
            gates_t,
            saved,
        )
    )
    new = update_weights(
        (down_share, up_share, gate_share, mixer_share, blocks_share),
        (
            ffn_down,
            ffn_t,
            out_proj,
            branch_t.reshape(2 * WIDTH, D),
            gates_t.reshape(2 * WIDTH, BLOCK),
        ),
        (
            down_first.T,
            down_second.T,
            ffn_in_first,
            ffn_in_second,
            out_first.T,
            out_second.T,
            branch_first,
            branch_second,
            gate_first,
            gate_second,
        ),
        (
            gains,
            gain_grad,
            gains_first,
            gains_second,
            channel_params,
            channel_grad,
            channel_first,
            channel_second,
        ),
    )
    return (
        block_out,
        tokens_grad,
        *new[15:21],
        *new[9:12],
        *new[12:15],
        *(value.T for value in new[6:9]),
        *new[3:6],
        *(value.T for value in new[0:3]),
    )


def solution(mesh):
    weights = [
        P(None, None, "tensor"),
        P(None, None, "tensor"),
        P("tensor", None),
        P(None, None, "tensor"),
        P("tensor", None),
    ]
    owned = [
        P(None, "dp", "tensor"),
        P(None, "dp", "tensor"),
        P("tensor", "dp"),
        P(None, "dp", "tensor"),
        P("tensor", "dp"),
    ]
    moments = [P(), P(None, "tensor")] + owned
    placed = [P("dp", None), P("dp", None), P(), P(), P(None, "tensor")] + weights
    for spec in moments:
        placed += [spec, spec]
    outs = [P(("dp", "tensor"), None)] * 2
    for spec in moments:
        outs += [spec, spec, spec]
    return jax.shard_map(
        shards, mesh=mesh, in_specs=tuple(placed), out_specs=tuple(outs), check_vma=False
    )
```

```python
import functools

import jax
import jax.numpy as jnp
from jax import lax
from jax.experimental import pallas as pl
from jax.experimental.pallas import tpu as pltpu
from jax.sharding import PartitionSpec as P

D = 2560
L = 2560
BLOCK = 256
F = 7680
STEP = 10
N_DP = 16
N_T = 8
ROWS = 512
OWN = ROWS // N_T
WIDTH = L // N_T
HIDE = F // N_T
HALF = 80
GATE_HALF = 8
MESH = pl.DeviceIdType.MESH

NORM_EPS = 1e-06
ADAM_EPS = 1e-08
BETA_ONE = 0.9
BETA_TWO = 0.95


def params(cid):
    return pltpu.CompilerParams(
        collective_id=cid, has_side_effects=True, vmem_limit_bytes=63 * 2**20
    )


def vmem(count):
    return [pl.BlockSpec(memory_space=pltpu.VMEM)] * count


def announce(peers):
    barrier = pltpu.get_barrier_semaphore()
    for peer in peers:
        pl.semaphore_signal(barrier, inc=1, device_id=peer, device_id_type=MESH)
    return lambda: pl.semaphore_wait(barrier, len(peers))


def remote(source, target, send_sem, recv_sem, peer):
    return pltpu.make_async_remote_copy(
        src_ref=source,
        dst_ref=target,
        send_sem=send_sem,
        recv_sem=recv_sem,
        device_id=peer,
        device_id_type=MESH,
    )


class Later:
    def __init__(self, make):
        self.make = make

    def start(self):
        self.make().start()

    def wait(self):
        self.make().wait()

    def wait_send(self):
        self.make().wait_send()

    def wait_recv(self):
        self.make().wait_recv()


def place():
    index = lax.axis_index("tensor")
    return index // 2, lax.rem(index, 2)


def at_x(x, core, by):
    return {"tensor": lax.rem(x + by, 4) * 2 + core}


def tensor_peers():
    x, core = place()
    return [{"tensor": x * 2 + 1 - core}] + [at_x(x, core, by) for by in (1, 2, 3)]


def chip_row(by, which):
    x, _ = place()
    return pl.multiple_of((lax.rem(x + by, 4) * 2 + which) * OWN, OWN)


ARRIVAL = {0: 0, 1: 1, 3: 2, 2: 3}


def arrival_row(by, which):
    return pl.multiple_of((ARRIVAL[by % 4] * 2 + which) * OWN, OWN)


class TensorSum:
    ORDER = (2, 1, 3, 0)

    def __init__(self, row, partial, pair, held, landed, pair_send, pair_recv, x_send, x_recv):
        self.row = row
        self.partial, self.pair, self.held, self.landed = partial, pair, held, landed
        self.sems = pair_send, pair_recv, x_send, x_recv
        self.pair_copies, self.x_copies = {}, {}

    def give(self, by):
        def make():
            x, core = place()
            return remote(
                self.partial.at[pl.ds(self.row(by, 1 - core), OWN)],
                self.pair.at[by],
                self.sems[0].at[by],
                self.sems[1].at[by],
                {"tensor": x * 2 + 1 - core},
            )

        self.pair_copies[by] = Later(make)
        self.pair_copies[by].start()

    def pass_on(self, by):
        _, core = place()
        self.pair_copies[by].wait_recv()
        mine = self.partial[pl.ds(self.row(by, core), OWN), :].astype(jnp.float32)
        self.held[by - 1] = (mine + self.pair[by].astype(jnp.float32)).astype(jnp.bfloat16)

        def make():
            x, core = place()
            return remote(
                self.held.at[by - 1],
                self.landed.at[by - 1],
                self.sems[2].at[by - 1],
                self.sems[3].at[by - 1],
                at_x(x, core, by),
            )

        self.x_copies[by] = Later(make)
        self.x_copies[by].start()

    def start(self, produce):
        for step, by in enumerate(self.ORDER):
            produce(by)
            self.give(by)
            if step:
                self.pass_on(self.ORDER[step - 1])

    def finish(self):
        _, core = place()
        self.pair_copies[0].wait_recv()
        total = self.partial[pl.ds(self.row(0, core), OWN), :].astype(jnp.float32)
        total = total + self.pair[0].astype(jnp.float32)
        for by in (1, 3, 2):
            self.x_copies[by].wait_recv()
            total = total + self.landed[by - 1].astype(jnp.float32)
        for by in self.ORDER:
            self.pair_copies[by].wait_send()
        for by in (2, 1, 3):
            self.x_copies[by].wait_send()
        return total


def reduce_scratch():
    return [
        pltpu.VMEM((4, OWN, D), jnp.bfloat16),
        pltpu.VMEM((3, OWN, D), jnp.bfloat16),
        pltpu.VMEM((3, OWN, D), jnp.bfloat16),
        pltpu.SemaphoreType.DMA((4,)),
        pltpu.SemaphoreType.DMA((4,)),
        pltpu.SemaphoreType.DMA((3,)),
        pltpu.SemaphoreType.DMA((3,)),
    ]


class TensorGather:
    def __init__(self, row, whole, x_send, x_recv, pair_send, pair_recv):
        self.row, self.whole, self.sems = row, whole, (x_send, x_recv, pair_send, pair_recv)

    def at(self, by):
        _, core = place()
        return self.whole.at[pl.ds(self.row(by, core), OWN)]

    def start(self, block):
        _, core = place()
        self.whole[pl.ds(self.row(0, core), OWN), :] = block
        self.sends, self.pairs = [], {}
        for by in (1, 3, 2):

            def make(by=by):
                x, core = place()
                mine = self.at(0)
                target = mine if self.row is chip_row else self.at(4 - by)
                return remote(
                    mine,
                    target,
                    self.sems[0].at[by - 1],
                    self.sems[1].at[by - 1],
                    at_x(x, core, by),
                )

            self.sends.append(Later(make))
            self.sends[-1].start()
        self.hand(0)

    def hand(self, by):
        def make():
            x, core = place()
            block = self.at(by)
            return remote(
                block,
                block,
                self.sems[2].at[by],
                self.sems[3].at[by],
                {"tensor": x * 2 + 1 - core},
            )

        self.pairs[by] = Later(make)
        self.pairs[by].start()

    def arrive(self, by):
        x, core = place()
        sender = 4 - by
        block = self.at(by)
        remote(
            block,
            block,
            self.sems[0].at[sender - 1],
            self.sems[1].at[sender - 1],
            at_x(x, core, sender),
        ).wait_recv()
        self.hand(by)

    def settle(self, by):
        self.pairs[by].wait_recv()

    def finish(self):
        for copy in self.sends:
            copy.wait_send()
        for copy in self.pairs.values():
            copy.wait_send()


class DataSum:
    LOW, HIGH = pl.ds(0, 2), pl.ds(2, 2)

    def __init__(self, grad, own, via, ring, last, near, send, recv, local, rows):
        self.grad, self.own, self.near, self.via = grad, own, near, via
        self.ring, self.last, self.rows = ring, last, rows
        self.send, self.recv, self.local = send, recv, local
        self.copies = {}

    def spots(self, half):
        me = lax.axis_index("dp")
        z, y = me // 4, lax.rem(me, 4)
        return (y, z) if half == 0 else (z, y)

    def peer(self, half, first_by, second_by):
        first, second = self.spots(half)
        a, b = lax.rem(first + first_by + 4, 4), lax.rem(second + second_by + 4, 4)
        return {"dp": b * 4 + a if half == 0 else a * 4 + b}

    def block(self, half, by, part):
        a = lax.rem(self.spots(half)[0] + by + 4, 4)
        return self.grad.at[part, a, 0] if half == 0 else self.grad.at[a, part, 1]

    def ship(self, half, slot, source, target, first_by, second_by):
        def make():
            return remote(
                source(),
                target(),
                self.send.at[half, slot],
                self.recv.at[half, slot],
                self.peer(half, first_by, second_by),
            )

        self.copies[half, slot] = Later(make)
        self.copies[half, slot].start()

    def own_load(self, half):
        return pltpu.make_async_copy(
            self.block(half, 0, pl.ds(0, 4)), self.own.at[half], self.local.at[half, 2]
        )

    def start(self):
        for half in (0, 1):
            self.ship(
                half, 0, lambda half=half: self.block(half, 2, self.LOW), lambda half=half: self.via.at[half, 0], 1, 0
            )
            self.ship(
                half, 1, lambda half=half: self.block(half, 2, self.HIGH), lambda half=half: self.via.at[half, 1], -1, 0
            )
            self.own_load(half).start()
        for half in (0, 1):
            self.ship(
                half, 2, lambda half=half: self.block(half, 1, self.HIGH), lambda half=half: self.ring.at[half, 0], 1, 0
            )
            self.ship(
                half, 3, lambda half=half: self.block(half, -1, self.LOW), lambda half=half: self.ring.at[half, 1], -1, 0
            )

    def add(self, target, sources, blocks):
        for block in range(blocks):
            if len(sources) == 1:
                target[block] = target[block] + sources[0][block]
                continue
            total = target[block].astype(jnp.float32)
            for source in sources:
                total = total + source[block].astype(jnp.float32)
            target[block] = total.astype(target.dtype)

    def middle(self):
        for half in (0, 1):
            loads = []
            for side, (by, part) in enumerate(((1, self.LOW), (-1, self.HIGH))):
                load = pltpu.make_async_copy(
                    self.block(half, by, part), self.near.at[side], self.local.at[half, side]
                )
                load.start()
                loads.append(load)
            for side in (0, 1):
                loads[side].wait()
                self.copies[half, side].wait_recv()
                via = self.via.at[half, side]
                self.add(via, [self.near.at[side]], 2)
                self.ship(
                    half,
                    4 + side,
                    lambda half=half, side=side: self.via.at[half, side],
                    lambda half=half, side=side: self.ring.at[half, 2 + side],
                    1 - 2 * side,
                    0,
                )

    def turn(self):
        for half in (0, 1):
            self.own_load(half).wait()
            for slot in (2, 3, 4, 5):
                self.copies[half, slot].wait_recv()
            ring = self.ring
            self.add(self.own.at[half, self.LOW], [ring.at[half, 1], ring.at[half, 2]], 2)
            self.add(self.own.at[half, self.HIGH], [ring.at[half, 0], ring.at[half, 3]], 2)
            for by in (1, 2, 3):
                self.ship(
                    half,
                    5 + by,
                    lambda half=half, by=by: self.own.at[
                        half, lax.rem(self.spots(half)[1] + by, 4)
                    ],
                    lambda half=half, by=by: self.last.at[half, by - 1],
                    0,
                    by,
                )

    def finish(self, share):
        for half in (0, 1):
            for by in (1, 2, 3):
                self.copies[half, 5 + by].wait_recv()
            total = self.own[half, self.spots(half)[1]].astype(jnp.float32)
            for by in range(3):
                total = total + self.last[half, by].astype(jnp.float32)
            share[half * self.rows : (half + 1) * self.rows, :] = total
        for copy in self.copies.values():
            copy.wait_send()


def data_buffers(rows, columns, dtype):
    return [
        pltpu.VMEM((2, 4, rows, columns), dtype),
        pltpu.VMEM((2, 2, 2, rows, columns), dtype),
        pltpu.VMEM((2, 4, 2, rows, columns), dtype),
        pltpu.VMEM((2, 3, rows, columns), dtype),
    ]


def data_sems():
    dma = pltpu.SemaphoreType.DMA
    return [dma((2, 9)), dma((2, 9)), dma((2, 3))]


def ring_peers():
    me = lax.axis_index("dp")
    z, y = me // 4, lax.rem(me, 4)
    along_y = [{"dp": z * 4 + lax.rem(y + by, 4)} for by in (1, 2, 3)]
    return along_y + [{"dp": lax.rem(z + by, 4) * 4 + y} for by in (1, 2, 3)]


def gather_scratch():
    return [
        pltpu.SemaphoreType.DMA((3,)),
        pltpu.SemaphoreType.DMA((3,)),
        pltpu.SemaphoreType.DMA((4,)),
        pltpu.SemaphoreType.DMA((4,)),
    ]


def dp_peers():
    me = lax.axis_index("dp")
    return [{"dp": lax.rem(me + by, N_DP)} for by in range(1, N_DP)]


def place_matrix(shift):
    row = lax.broadcasted_iota(jnp.int32, (WIDTH, 2 * BLOCK), 0)
    lane = lax.broadcasted_iota(jnp.int32, (WIDTH, 2 * BLOCK), 1)
    return jnp.where(lane == row + shift, 1.0, 0.0).astype(jnp.bfloat16)


def wide_gates(gates, wide, shift):
    row = lax.broadcasted_iota(jnp.int32, (WIDTH, BLOCK), 0)
    low = row + shift < BLOCK
    for gate in range(2):
        matrix = gates[gate].astype(jnp.float32)
        wide[gate, :, 0:BLOCK] = jnp.where(low, matrix, 0.0).astype(jnp.bfloat16)
        wide[gate, :, BLOCK : 2 * BLOCK] = jnp.where(low, 0.0, matrix).astype(jnp.bfloat16)


def one_less_exp(z):
    series = 1.0 + z / 7.0
    for term in (6.0, 5.0, 4.0, 3.0, 2.0):
        series = 1.0 + z / term * series
    return jnp.where(z > -0.35, -z * series, 1.0 - jnp.exp(z))


def tiles(count, size, body, unroll=1):
    def step(index, _):
        body(pl.multiple_of(index * size, size))
        return 0

    lax.fori_loop(0, count, step, 0, unroll=unroll)


def norm_rows(source, target, gain, rows):
    def body(first):
        at = pl.ds(first, 16)
        target[at, :] = rms_norm(source[at, :].astype(jnp.float32), gain).astype(jnp.bfloat16)

    tiles(rows // 16, 16, body, min(4, rows // 16))


def shifted(values, by, fill, reverse):
    count = values.shape[0]
    row = lax.broadcasted_iota(jnp.int32, values.shape, 0)
    if reverse:
        return jnp.where(row < count - by, pltpu.roll(values, count - by, 0), fill)
    return jnp.where(row >= by, pltpu.roll(values, by, 0), fill)


def local_scan(factor_at, term_at, values, prods, reverse):
    def step(index, held):
        prod, value = held
        first = pl.multiple_of((ROWS // 8 - 1 - index if reverse else index) * 8, 8)
        factor, term = factor_at(first), term_at(first)
        for by in (1, 2, 4):
            term = term + factor * shifted(term, by, 0.0, reverse)
            factor = factor * shifted(factor, by, 1.0, reverse)
        value = factor * value + term
        prod = factor * prod
        values[pl.ds(first, 8), :] = value
        prods[pl.ds(first, 8), :] = prod
        last = 0 if reverse else 7
        return (
            jnp.broadcast_to(prod[last : last + 1], prod.shape),
            jnp.broadcast_to(value[last : last + 1], value.shape),
        )

    ones = jnp.ones((8, WIDTH), jnp.float32)
    return lax.fori_loop(0, ROWS // 8, step, (ones, jnp.zeros_like(ones)), unroll=8)


def start_share(slots, send, recv):
    me = lax.axis_index("dp")
    copies = []
    for by in range(1, N_DP):
        copy = remote(
            slots.at[me], slots.at[me], send.at[by], recv.at[by], {"dp": lax.rem(me + by, N_DP)}
        )
        copy.start()
        copies.append(copy)
    return copies


def beside_peers():
    index = lax.axis_index("tensor")
    return {"tensor": lax.rem(index + 1, N_T)}, {"tensor": lax.rem(index + N_T - 1, N_T)}


def far_peer():
    index = lax.axis_index("tensor")
    _, core = place()
    return {"tensor": lax.rem(index + N_T - 1 + 2 * core, N_T)}


def gelu_parts(y):
    c = 0.7978845608028654
    inner = jnp.tanh(c * (y + 0.044715 * y * y * y))
    half = 0.5 * (1.0 + inner)
    slope = half + 0.5 * y * (1.0 - inner * inner) * c * (1.0 + 3 * 0.044715 * y * y)
    return y * half, slope


def forward_kernel(
    tokens, branch_hbm, gates, out_hbm, chan, gains, flags, residual, block, *rest
):
    outs = rest[:9]
    (
        normed_one, ext, window, pre_a, pre_x, carry, state, branch_y, mixed,
        branch_w, out_w, halo, halo_norm, wide, placing, update, values, prods, gelu_y, low, high, slots, partial,
        load_sem, store_sem, halo_send, halo_recv, side_send, side_recv, slot_send, slot_recv, *scratch
    ) = rest[9:]
    me, index = lax.axis_index("dp"), lax.axis_index("tensor")
    shift = lax.rem(index * WIDTH, BLOCK)
    loads = [
        pltpu.make_async_copy(branch_hbm.at[0], branch_w.at[0], load_sem.at[0]),
        pltpu.make_async_copy(branch_hbm.at[1], branch_w.at[1], load_sem.at[1]),
        pltpu.make_async_copy(out_hbm, out_w, load_sem.at[2]),
    ]
    for load in loads:
        load.start()
    ready = announce(dp_peers() + tensor_peers() + [far_peer()])
    stores = []

    def store(number, source, target):
        copy = pltpu.make_async_copy(source, target, store_sem.at[number])
        copy.start()
        stores.append(copy)

    send_halo = remote(
        tokens.at[pl.ds(ROWS - 16, 16)],
        halo,
        halo_send,
        halo_recv,
        {"dp": lax.rem(me + 1, N_DP)},
    )
    wide_gates(gates, wide, shift)
    placing[...] = place_matrix(shift)
    gain = gains[0:1, :]
    norm_rows(tokens, normed_one, gain, ROWS)
    ready()
    send_halo.start()
    store(0, normed_one, outs[0])
    loads[0].wait()

    def branch_tile(first):
        at = pl.ds(first, 128)
        value = times_transposed(normed_one[at, :], branch_w[0])
        ext[pl.ds(first + 16, 128), :] = value.astype(jnp.bfloat16).astype(jnp.float32)

    tiles(4, 128, branch_tile)
    send_halo.wait()
    norm_rows(halo, halo_norm, gain, 16)
    ext[0:16, :] = times_transposed(halo_norm[...], branch_w[0]).astype(jnp.bfloat16).astype(jnp.float32)

    def conv_tile(first):
        near = ext[pl.ds(first + 8, 136), :]
        total = chan[0:1, :] * near[8:]
        for tap in range(1, 4):
            counted = flags[pl.ds(first, 128), tap : tap + 1] > 0.0
            total = total + chan[tap : tap + 1, :] * jnp.where(counted, near[8 - tap : 136 - tap], 0.0)
        window[pl.ds(first, 128), :] = matmul(total.astype(jnp.bfloat16), placing[...]).astype(
            jnp.bfloat16
        )

    tiles(4, 128, conv_tile)
    store(1, ext, outs[1])
    up, down = beside_peers()
    to_up = remote(
        window.at[:, pl.ds(BLOCK, BLOCK)], low, side_send.at[0], side_recv.at[0], up
    )
    to_down = remote(window.at[:, pl.ds(0, BLOCK)], high, side_send.at[1], side_recv.at[1], down)
    to_up.start()
    to_down.start()
    loads[1].wait()

    def gelu_tile(first):
        at = pl.ds(first, 128)
        branch_y[at, :] = times_transposed(normed_one[at, :], branch_w[1])

    tiles(4, 128, gelu_tile)
    store(2, branch_y, outs[6])
    to_up.wait()
    to_down.wait()

    def window_tile(first):
        at = pl.ds(first, 128)
        own_conv = lax.dot_general(
            window[at, :], placing[...], (((1,), (1,)), ((), ())), preferred_element_type=jnp.float32
        )
        from_low = jnp.where(shift != 0, low[at, :].astype(jnp.float32), 0.0)
        from_high = jnp.where(shift != 192, high[at, :].astype(jnp.float32), 0.0)
        whole = window[at, :].astype(jnp.float32) + jnp.concatenate([from_low, from_high], 1)
        whole = whole.astype(jnp.bfloat16)
        window[at, :] = whole
        a = times_transposed(whole, wide[0])
        x = times_transposed(whole, wide[1])
        pre_a[at, :] = a
        pre_x[at, :] = x
        reset = flags[at, 4:5] > 0.0
        log_a = -8.0 * jax.nn.sigmoid(a) * chan[5:6, :]
        carry[at, :] = jnp.where(reset, 0.0, jnp.exp(log_a))
        scale = jnp.where(reset, 1.0, jnp.sqrt(one_less_exp(2.0 * log_a)))
        update[at, :] = own_conv * jax.nn.sigmoid(x) * scale

    tiles(4, 128, window_tile)
    store(3, window, outs[2])
    store(4, pre_a, outs[3])
    store(5, pre_x, outs[4])
    carry[ROWS : ROWS + 8, :] = jnp.ones((8, WIDTH), jnp.float32)
    store(6, carry, outs[5])
    prod, value = local_scan(
        lambda first: carry[pl.ds(first, 8), :],
        lambda first: update[pl.ds(first, 8), :],
        values,
        prods,
        False,
    )
    slots[me, 0:1, :] = prod[0:1]
    slots[me, 1:2, :] = value[0:1]
    copies = start_share(slots, slot_send, slot_recv)

    def activate(first):
        at = pl.ds(first, 64)
        y = branch_y[at, :]
        gelu_y[at, :] = gelu_parts(y)[0]

    tiles(8, 64, activate)
    for copy in copies:
        copy.wait()
    before = jnp.zeros((1, WIDTH), jnp.float32)
    for place_at in range(N_DP - 1):
        longer = slots[place_at, 0:1, :] * before + slots[place_at, 1:2, :]
        before = jnp.where(place_at < me, longer, before)

    state[0:8, :] = jnp.broadcast_to(before, (8, WIDTH))

    def finish(first):
        at = pl.ds(first, 64)
        total = values[at, :] + prods[at, :] * before
        state[pl.ds(first + 8, 64), :] = total
        mixed[at, :] = (total * gelu_y[at, :]).astype(jnp.bfloat16)

    tiles(8, 64, finish)
    store(7, state, outs[7])
    store(8, mixed, outs[8])
    loads[2].wait()

    def produce(by):
        at = pl.ds(pl.multiple_of(chip_row(by, 0), 128), 128)
        partial[at, :] = matmul(mixed[at, :], out_w[...]).astype(jnp.bfloat16)

    summed = TensorSum(chip_row, partial, *scratch)
    summed.start(produce)
    _, core = place()
    total = tokens[pl.ds(chip_row(0, core), OWN), :].astype(jnp.float32) + summed.finish()
    residual[...] = total
    block[...] = rms_norm(total, gains[1:2, :]).astype(jnp.bfloat16)
    for copy in stores:
        copy.wait()


def saved_shapes():
    f32, bf16 = jnp.float32, jnp.bfloat16
    return (
        ((ROWS, D), bf16),
        ((ROWS + 16, WIDTH), f32),
        ((ROWS, 2 * BLOCK), bf16),
        ((ROWS, WIDTH), f32),
        ((ROWS, WIDTH), f32),
        ((ROWS + 8, WIDTH), f32),
        ((ROWS, WIDTH), f32),
        ((ROWS + 8, WIDTH), f32),
        ((ROWS, WIDTH), bf16),
    )


def mixer_forward(tokens, branch_in, gate_blocks, out_proj, chan, gains, flags):
    f32, bf16 = jnp.float32, jnp.bfloat16
    dma = pltpu.SemaphoreType.DMA
    here = pl.BlockSpec(memory_space=pltpu.VMEM)
    there = pl.BlockSpec(memory_space=pl.ANY)
    shapes = saved_shapes()
    inside = shapes[:6] + (shapes[7], shapes[6], shapes[8])
    return pl.pallas_call(
        forward_kernel,
        out_shape=(
            jax.ShapeDtypeStruct((OWN, D), f32),
            jax.ShapeDtypeStruct((OWN, D), bf16),
            *(jax.ShapeDtypeStruct(*shape) for shape in shapes),
        ),
        in_specs=[here, there, here, there, here, here, here],
        out_specs=tuple([here] * 2 + [there] * 9),
        scratch_shapes=[pltpu.VMEM(*shape) for shape in inside]
        + [
            pltpu.VMEM((2, WIDTH, D), bf16),
            pltpu.VMEM((WIDTH, D), bf16),
            pltpu.VMEM((16, D), bf16),
            pltpu.VMEM((16, D), bf16),
            pltpu.VMEM((2, WIDTH, 2 * BLOCK), bf16),
            pltpu.VMEM((WIDTH, 2 * BLOCK), bf16),
            pltpu.VMEM((ROWS, WIDTH), f32),
            pltpu.VMEM((ROWS, WIDTH), f32),
            pltpu.VMEM((ROWS, WIDTH), f32),
            pltpu.VMEM((ROWS, WIDTH), f32),
            pltpu.VMEM((ROWS, BLOCK), bf16),
            pltpu.VMEM((ROWS, BLOCK), bf16),
            pltpu.VMEM((N_DP, 8, WIDTH), f32),
            pltpu.VMEM((ROWS, D), bf16),
            dma((3,)),
            dma((9,)),
            dma,
            dma,
            dma((2,)),
            dma((2,)),
            dma((N_DP,)),
            dma((N_DP,)),
        ]
        + reduce_scratch(),
        compiler_params=params(1),
    )(tokens, branch_in, gate_blocks, out_proj, chan, gains, flags)


def norm_back(value, gain, grad):
    scale = lax.rsqrt(jnp.mean(value * value, axis=-1, keepdims=True) + NORM_EPS)
    unit = value * scale
    scaled = grad * gain
    back = scale * (scaled - unit * jnp.mean(scaled * unit, axis=-1, keepdims=True))
    return back, jnp.sum(grad * unit, axis=0, keepdims=True)


def back_kernel(
    block, residual, gains, chan, flags, dy_hbm, ffn_hbm, down_hbm, tokens, out_hbm, branch_hbm, gates_hbm, *rest
):
    saved, rest = rest[:9], rest[9:]
    tokens_grad, out, gain_sum, channel_sum, blocks_share, *rest = rest
    shares, (down_grad, up_grad, gate_grad, mixer_grad), rest = rest[:4], rest[4:8], rest[8:]
    (
        normed, rounded, grad, grad_gain_two, partial, stage, near, near_blocks,
        low_in, high_in, slots, halo, halo_in, gain_t, gain_dp, chan_dp, blocks_grad,
        load_sem, stage_sem, share_sem, slot_send, slot_recv, side_send, side_recv, halo_send, halo_recv,
        t_send, t_recv, g_send, g_recv, c_send, c_recv, reuse_sem, free_sem, *scratch
    ) = rest
    me, index = lax.axis_index("dp"), lax.axis_index("tensor")
    x, core = place()
    shift = lax.rem(index * WIDTH, BLOCK)
    ready = announce(dp_peers() + tensor_peers() + [far_peer()])

    def take(count):
        taken = scratch[:count]
        del scratch[:count]
        return taken

    sum_scratch = take(7)
    summed = TensorSum(arrival_row, partial, *sum_scratch)
    summed_out = TensorSum(arrival_row, partial, *sum_scratch)
    summed_last = TensorSum(chip_row, partial, *sum_scratch)
    before = TensorGather(arrival_row, normed, *take(4))
    after = TensorGather(chip_row, rounded, *take(4))
    first = take(4)
    down_sum = DataSum(down_grad, *first, near, *take(3), HALF)
    up_sum = DataSum(up_grad, *take(4), near, *take(3), HALF)
    gate_sum = DataSum(gate_grad, *take(4), near, *take(3), HALF)
    mixer_sum = DataSum(mixer_grad, *first, near, *take(3), HALF)
    blocks_sum = DataSum(blocks_grad, *take(4), near_blocks, *take(3), GATE_HALF)

    def weight_grad(target, jobs):
        pending = None
        for z in range(4):
            columns = pl.ds(z * 640, 640)
            parts = [transposed_times(left[:, columns], right[...]) for left, right in jobs]
            whole = parts[0] if len(parts) == 1 else jnp.concatenate(parts, 1)
            if pending is not None:
                pending.wait()
            stage[...] = whole.astype(jnp.bfloat16).reshape(4, 2, HALF, HIDE)
            pending = pltpu.make_async_copy(stage, target.at[z], stage_sem)
            pending.start()
        pending.wait()

    def ffn_part(dy, ffn_w, down_w, hidden, to_gate, to_up, gate_pre, up_pre, grad_hidden):
        loads = []

        def load(source, target):
            copy = pltpu.make_async_copy(source, target, load_sem.at[len(loads)])
            copy.start()
            loads.append(copy)

        for by, spot in ARRIVAL.items():
            load(
                dy_hbm.at[pl.ds(pl.multiple_of(lax.rem(x + by, 4) * 128, 128), 128)],
                dy.at[pl.ds(spot * 128, 128)],
            )
        load(down_hbm, down_w)
        load(ffn_hbm.at[pl.ds(0, HIDE)], ffn_w.at[pl.ds(0, HIDE)])
        load(ffn_hbm.at[pl.ds(HIDE, HIDE)], ffn_w.at[pl.ds(HIDE, HIDE)])
        pieces = ((0, 384), (384, 384), (768, 192))
        ready()
        before.start(block[...])
        for copy in loads[:5]:
            copy.wait()
        for start, size in pieces:
            units = pl.ds(start, size)
            grad_hidden[:, units] = times_transposed(dy[...], down_w[units, :])
        for copy in loads[5:]:
            copy.wait()
        before.arrive(1)
        before.settle(0)
        before.settle(1)
        for group in range(2):
            if group:
                before.arrive(3)
                before.arrive(2)
                before.settle(3)
                before.settle(2)
            rows = pl.ds(group * 256, 256)
            for start, size in pieces:
                units = pl.ds(start, size)
                gate_pre[:, 0:size] = times_transposed(normed[rows, :], ffn_w[units, :])
                up_pre[:, 0:size] = times_transposed(normed[rows, :], ffn_w[pl.ds(HIDE + start, size), :])

                def activate(first, units=units, size=size, group=group):
                    here = pl.ds(first, 32)
                    at = pl.ds(pl.multiple_of(group * 256 + first, 32), 32)
                    value, slope = gelu_parts(gate_pre[here, 0:size])
                    up, back = up_pre[here, 0:size], grad_hidden[at, units]
                    hidden[at, units] = (value * up).astype(jnp.bfloat16)
                    to_up[at, units] = (back * value).astype(jnp.bfloat16)
                    to_gate[at, units] = (back * up * slope).astype(jnp.bfloat16)

                tiles(256 // 32, 32, activate)
        before.finish()

        def produce(by):
            at = pl.ds(arrival_row(by, 0), 128)
            total = matmul(to_gate[at, :], ffn_w[0:HIDE, :]) + matmul(
                to_up[at, :], ffn_w[HIDE : 2 * HIDE, :]
            )
            partial[at, :] = total.astype(jnp.bfloat16)

        weight_grad(down_grad, [(dy, hidden)])
        down_sum.start()
        summed.start(produce)
        weight_grad(up_grad, [(normed, to_up)])
        up_sum.start()
        down_sum.middle()
        norm_grad = summed.finish()
        back, gain_part = norm_back(residual[...], gains[1:2, :], norm_grad)
        back = back + dy[pl.ds(arrival_row(0, core), OWN), :].astype(jnp.float32)
        grad[...] = back
        grad_gain_two[...] = gain_part
        after.start(back.astype(jnp.bfloat16))

        def produce_out(first):
            at = pl.ds(first, 128)
            partial[at, :] = matmul(hidden[at, :], down_w[...]).astype(jnp.bfloat16)

        tiles(4, 128, produce_out)
        weight_grad(gate_grad, [(normed, to_gate)])
        gate_sum.start()

    f32, bf16 = jnp.float32, jnp.bfloat16
    pl.run_scoped(
        ffn_part,
        pltpu.VMEM((ROWS, D), bf16),
        pltpu.VMEM((2 * HIDE, D), bf16),
        pltpu.VMEM((HIDE, D), bf16),
        pltpu.VMEM((ROWS, HIDE), bf16),
        pltpu.VMEM((ROWS, HIDE), bf16),
        pltpu.VMEM((ROWS, HIDE), bf16),
        pltpu.VMEM((256, 384), f32),
        pltpu.VMEM((256, 384), f32),
        pltpu.VMEM((ROWS, HIDE), f32),
    )

    def mixer_part(
        normed_one, ext, window, pre_a, pre_x, carry, branch_y, state, mixed,
        out_w, branch_w, gates, own, wide, to_y, local, sums, prods, to_a, to_gx, window_grad, low, high, conv_grad,
        share_stage,
    ):
        targets = (
            normed_one, ext, window, pre_a, pre_x, carry, branch_y, state, mixed, out_w, branch_w, gates, own,
        )
        sources = (
            *saved,
            out_hbm,
            branch_hbm,
            gates_hbm,
            tokens.at[pl.ds(chip_row(0, core), OWN)],
        )
        def keep_share(number):
            copy = pltpu.make_async_copy(share_stage, shares[number], share_sem)
            copy.start()
            copy.wait()

        loads = []
        for source, target in zip(sources, targets):
            loads.append(pltpu.make_async_copy(source, target, load_sem.at[len(loads)]))
            loads[-1].start()
        for by in (1, 3, 2):
            after.arrive(by)
        for by in (0, 1, 3, 2):
            after.settle(by)
        after.finish()
        for step, by in enumerate(summed_out.ORDER):
            summed_out.give(by)
        for by in (2, 1, 3):
            summed_out.pass_on(by)
        up_sum.middle()
        for copy in loads:
            copy.wait()
        wide_gates(gates, wide, shift)

        def mixed_tile(first):
            at = pl.ds(first, 128)
            local[at, :] = times_transposed(rounded[at, :], out_w[...])

        tiles(4, 128, mixed_tile)

        def gelu_tile(first):
            at = pl.ds(first, 64)
            value, slope = gelu_parts(branch_y[at, :])
            mixed_grad = local[at, :]
            to_y[at, :] = (mixed_grad * state[pl.ds(first + 8, 64), :] * slope).astype(jnp.bfloat16)
            local[at, :] = mixed_grad * value

        tiles(8, 64, gelu_tile)
        prod, value = local_scan(
            lambda first: carry[pl.ds(first, 16), :][1:9],
            lambda first: local[pl.ds(first, 8), :],
            sums,
            prods,
            True,
        )
        slots[me, 0:1, :] = carry[0:1, :] * prod[0:1]
        slots[me, 1:2, :] = carry[0:1, :] * value[0:1]
        copies = start_share(slots, slot_send, slot_recv)
        down_sum.turn()

        for copy in copies:
            copy.wait()
        gate_sum.middle()
        later = jnp.zeros((1, WIDTH), jnp.float32)
        for place_at in range(N_DP - 1, 0, -1):
            longer = slots[place_at, 0:1, :] * later + slots[place_at, 1:2, :]
            later = jnp.where(place_at > me, longer, later)
        plus, decay_slope = chan[5:6, :], chan[6:7, :]
        zero_row = jnp.zeros((1, WIDTH), jnp.float32)

        def gate_tile(first, decay_grad):
            at = pl.ds(first, 64)
            total = sums[at, :] + prods[at, :] * later
            near = state[pl.ds(first, 72), :]
            conv = lax.dot_general(
                window[at, :], place_matrix(shift), (((1,), (1,)), ((), ())), preferred_element_type=jnp.float32
            )
            reset = flags[at, 4:5] > 0.0
            gate_a, gate_x = jax.nn.sigmoid(pre_a[at, :]), jax.nn.sigmoid(pre_x[at, :])
            log_a = -8.0 * gate_a * plus
            keep = jnp.exp(log_a)
            scale = jnp.sqrt(one_less_exp(2.0 * log_a))
            scale_here = jnp.where(reset, 1.0, scale)
            conv_grad[at, :] = total * gate_x * scale_here
            to_gx[at, :] = (total * conv * scale_here * gate_x * (1.0 - gate_x)).astype(jnp.bfloat16)
            log_grad = total * near[7:71] * keep - total * conv * gate_x * keep * keep / scale
            log_grad = jnp.where(reset, 0.0, log_grad)
            to_a[at, :] = (log_grad * (-8.0 * plus) * gate_a * (1.0 - gate_a)).astype(jnp.bfloat16)
            return decay_grad + jnp.sum(log_grad * (-8.0 * gate_a), axis=0, keepdims=True)

        decay_grad = lax.fori_loop(
            0, 8, lambda i, held: gate_tile(pl.multiple_of(i * 64, 64), held), zero_row
        )
        decay_grad = decay_grad * decay_slope

        def window_tile(first):
            at = pl.ds(first, 128)
            total = matmul(to_a[at, :], wide[0]) + matmul(to_gx[at, :], wide[1])
            window_grad[at, :] = total
            low[at, :] = total[:, 0:BLOCK].astype(jnp.bfloat16)
            high[at, :] = total[:, BLOCK : 2 * BLOCK].astype(jnp.bfloat16)

        tiles(4, 128, window_tile)
        up, down = beside_peers()
        to_up = remote(high, low_in, side_send.at[0], side_recv.at[0], up)
        to_down = remote(low, high_in, side_send.at[1], side_recv.at[1], down)
        to_up.start()
        to_down.start()
        column = lax.broadcasted_iota(jnp.int32, (BLOCK, WIDTH), 1)
        chosen = []
        for right in (to_a, to_gx):
            both = transposed_times(window[...], right[...])
            chosen.append(
                jnp.where(column + shift < BLOCK, both[0:BLOCK], both[BLOCK : 2 * BLOCK])
            )
        blocks_grad[...] = jnp.concatenate(chosen, 1).reshape(4, 4, 2, GATE_HALF, 2 * WIDTH)
        down_sum.finish(share_stage)
        keep_share(0)
        for peer in ring_peers():
            pl.semaphore_signal(reuse_sem, inc=1, device_id=peer, device_id_type=MESH)
        to_up.wait()
        to_down.wait()

        def conv_tile(first):
            at = pl.ds(first, 64)
            from_low = jnp.where(shift != 0, low_in[at, :].astype(jnp.float32), 0.0)
            from_high = jnp.where(shift != 192, high_in[at, :].astype(jnp.float32), 0.0)
            total = window_grad[at, :] + jnp.concatenate([from_low, from_high], 1)
            total = pltpu.roll(total, lax.rem(2 * BLOCK - shift, 2 * BLOCK), 1)
            conv_grad[at, :] = conv_grad[at, :] + total[:, 0:WIDTH]

        tiles(8, 64, conv_tile)
        conv_grad[ROWS : ROWS + 8, :] = jnp.zeros((8, WIDTH), jnp.float32)
        head = conv_grad[0:8, :]
        rows = []
        for row in range(3):
            total = zero_row
            for tap in range(3 - row, 4):
                from_row = row - 3 + tap
                counted = flags[from_row : from_row + 1, tap : tap + 1] > 0.0
                total = total + chan[tap : tap + 1, :] * jnp.where(
                    counted, head[from_row : from_row + 1], 0.0
                )
            rows.append(total)
        halo[0:5, :] = jnp.zeros((5, WIDTH), jnp.float32)
        for row in range(3):
            halo[5 + row : 6 + row, :] = rows[row]
        send_halo = remote(halo, halo_in, halo_send, halo_recv, {"dp": lax.rem(me + N_DP - 1, N_DP)})
        send_halo.start()
        blocks_sum.start()

        def tap_tile(first, held):
            at = pl.ds(first, 64)
            near = conv_grad[pl.ds(first, 72), :]
            marks = flags[pl.ds(first, 72), :]
            behind = ext[pl.ds(first + 8, 72), :]
            total = chan[0:1, :] * near[0:64]
            taps = [held[0] + jnp.sum(near[0:64] * behind[8:72], axis=0, keepdims=True)]
            for tap in range(1, 4):
                counted = marks[tap : tap + 64, tap : tap + 1] > 0.0
                total = total + chan[tap : tap + 1, :] * jnp.where(counted, near[tap : tap + 64], 0.0)
                here = jnp.where(marks[0:64, tap : tap + 1] > 0.0, near[0:64], 0.0)
                taps.append(
                    held[tap] + jnp.sum(here * behind[8 - tap : 72 - tap], axis=0, keepdims=True)
                )
            local[at, :] = total
            return tuple(taps)

        tap_grads = lax.fori_loop(
            0, 8, lambda i, held: tap_tile(pl.multiple_of(i * 64, 64), held), (zero_row,) * 4
        )
        for tap in range(4):
            chan_dp[me, tap : tap + 1, :] = tap_grads[tap]
        chan_dp[me, 4:5, :] = decay_grad
        chan_dp[me, 5:8, :] = jnp.zeros((3, WIDTH), jnp.float32)
        channel_copies = start_share(chan_dp, c_send, c_recv)
        send_halo.wait()
        local[ROWS - 8 : ROWS, :] = local[ROWS - 8 : ROWS, :] + halo_in[...]
        to_x = to_a
        to_x[...] = local[...].astype(jnp.bfloat16)

        def produce(by):
            at = pl.ds(pl.multiple_of(chip_row(by, 0), 128), 128)
            total = matmul(to_x[at, :], branch_w[0]) + matmul(to_y[at, :], branch_w[1])
            partial[at, :] = total.astype(jnp.bfloat16)

        branches = jnp.concatenate(
            [to_y[...].astype(jnp.float32), to_x[...].astype(jnp.float32)], 1
        ).astype(jnp.bfloat16)
        weight_grad(mixer_grad, [(normed_one, branches), (rounded, mixed)])
        pl.semaphore_wait(reuse_sem, 6)
        mixer_sum.start()
        up_sum.turn()
        out[...] = (residual[...] + summed_out.finish()).astype(jnp.bfloat16)
        for peer in tensor_peers():
            pl.semaphore_signal(free_sem, inc=1, device_id=peer, device_id_type=MESH)
        blocks_sum.middle()
        pl.semaphore_wait(free_sem, 4)
        summed_last.start(produce)
        mixer_sum.middle()
        norm_grad = summed_last.finish()
        before_norm, gain_part = norm_back(own[...].astype(jnp.float32), gains[0:1, :], norm_grad)
        tokens_grad[...] = (grad[...] + before_norm).astype(jnp.bfloat16)
        gain_t[index, 0:1, :] = gain_part
        gain_t[index, 1:2, :] = grad_gain_two[...]
        gain_copies = []
        for by in range(1, N_T):
            copy = remote(
                gain_t.at[index],
                gain_t.at[index],
                t_send.at[by],
                t_recv.at[by],
                {"tensor": lax.rem(index + by, N_T)},
            )
            copy.start()
            gain_copies.append(copy)
        gate_sum.turn()
        for copy in gain_copies:
            copy.wait()
        total = gain_t[0]
        for by in range(1, N_T):
            total = total + gain_t[by]
        gain_dp[me] = total
        gain_copies = start_share(gain_dp, g_send, g_recv)
        up_sum.finish(share_stage)
        keep_share(1)
        blocks_sum.turn()
        gate_sum.finish(share_stage)
        keep_share(2)
        mixer_sum.turn()
        for copy in channel_copies + gain_copies:
            copy.wait()
        total, channels = gain_dp[0], chan_dp[0]
        for by in range(1, N_DP):
            total = total + gain_dp[by]
            channels = channels + chan_dp[by]
        gain_sum[...] = total
        channel_sum[...] = channels
        blocks_sum.finish(blocks_share)
        mixer_sum.finish(share_stage)
        keep_share(3)


    wide_f32 = pltpu.VMEM((ROWS, WIDTH), f32)
    wide_bf16 = pltpu.VMEM((ROWS, WIDTH), bf16)
    pl.run_scoped(
        mixer_part,
        *(pltpu.VMEM(*shape) for shape in saved_shapes()),
        pltpu.VMEM((WIDTH, D), bf16),
        pltpu.VMEM((2, WIDTH, D), bf16),
        pltpu.VMEM((2, WIDTH, BLOCK), bf16),
        pltpu.VMEM((OWN, D), bf16),
        pltpu.VMEM((2, WIDTH, 2 * BLOCK), bf16),
        wide_bf16,
        wide_f32,
        wide_f32,
        wide_f32,
        wide_bf16,
        wide_bf16,
        pltpu.VMEM((ROWS, 2 * BLOCK), f32),
        pltpu.VMEM((ROWS, BLOCK), bf16),
        pltpu.VMEM((ROWS, BLOCK), bf16),
        pltpu.VMEM((ROWS + 8, WIDTH), f32),
        pltpu.VMEM((2 * HALF, HIDE), f32),
    )


def backward(block, residual, gains, chan, flags, dy, ffn_t, down, tokens, out_proj, branch_t, gates_t, saved):
    f32, bf16 = jnp.float32, jnp.bfloat16
    dma = pltpu.SemaphoreType.DMA
    here = pl.BlockSpec(memory_space=pltpu.VMEM)
    there = pl.BlockSpec(memory_space=pl.ANY)
    share = jax.ShapeDtypeStruct((2 * HALF, HIDE), f32)
    shared = jax.ShapeDtypeStruct((4, 4, 2, HALF, HIDE), bf16)
    return pl.pallas_call(
        back_kernel,
        out_shape=(
            jax.ShapeDtypeStruct((OWN, D), bf16),
            jax.ShapeDtypeStruct((OWN, D), bf16),
            jax.ShapeDtypeStruct((2, D), f32),
            jax.ShapeDtypeStruct((8, WIDTH), f32),
            jax.ShapeDtypeStruct((2 * GATE_HALF, 2 * WIDTH), f32),
            *[share] * 4,
            *[shared] * 4,
        ),
        in_specs=[here] * 5 + [there] * 16,
        out_specs=tuple([here] * 5 + [there] * 8),
        scratch_shapes=[
            pltpu.VMEM((ROWS, D), bf16),
            pltpu.VMEM((ROWS, D), bf16),
            pltpu.VMEM((OWN, D), f32),
            pltpu.VMEM((1, D), f32),
            pltpu.VMEM((ROWS, D), bf16),
            pltpu.VMEM((4, 2, HALF, HIDE), bf16),
            pltpu.VMEM((2, 2, HALF, HIDE), bf16),
            pltpu.VMEM((2, 2, GATE_HALF, 2 * WIDTH), f32),
            pltpu.VMEM((ROWS, BLOCK), bf16),
            pltpu.VMEM((ROWS, BLOCK), bf16),
            pltpu.VMEM((N_DP, 8, WIDTH), f32),
            pltpu.VMEM((8, WIDTH), f32),
            pltpu.VMEM((8, WIDTH), f32),
            pltpu.VMEM((N_T, 2, D), f32),
            pltpu.VMEM((N_DP, 2, D), f32),
            pltpu.VMEM((N_DP, 8, WIDTH), f32),
            pltpu.VMEM((4, 4, 2, GATE_HALF, 2 * WIDTH), f32),
            dma((13,)),
            dma,
            dma,
            dma((N_DP,)),
            dma((N_DP,)),
            dma((2,)),
            dma((2,)),
            dma,
            dma,
            dma((N_T,)),
            dma((N_T,)),
            dma((N_DP,)),
            dma((N_DP,)),
            dma((N_DP,)),
            dma((N_DP,)),
            pltpu.SemaphoreType.REGULAR,
            pltpu.SemaphoreType.REGULAR,
        ]
        + reduce_scratch()
        + gather_scratch()
        + gather_scratch()
        + data_buffers(HALF, HIDE, bf16)
        + data_sems()
        + data_buffers(HALF, HIDE, bf16)
        + data_sems()
        + data_buffers(HALF, HIDE, bf16)
        + data_sems()
        + data_sems()
        + data_buffers(GATE_HALF, 2 * WIDTH, f32)
        + data_sems(),
        compiler_params=params(2),
    )(block, residual, gains, chan, flags, dy, ffn_t, down, tokens, out_proj, branch_t, gates_t, *saved)


def rms_norm(values, gain):
    return values * lax.rsqrt(jnp.mean(values * values, axis=-1, keepdims=True) + NORM_EPS) * gain


def matmul(left, right):
    return jnp.dot(left, right, preferred_element_type=jnp.float32)


def times_transposed(left, right):
    return lax.dot_general(
        left, right, (((1,), (1,)), ((), ())), preferred_element_type=jnp.float32
    )


def transposed_times(left, right):
    return lax.dot_general(
        left, right, (((0,), (0,)), ((), ())), preferred_element_type=jnp.float32
    )


def adam_step(weight, grad, first, second, rate, decay):
    first_new = BETA_ONE * first + (1.0 - BETA_ONE) * grad
    second_new = BETA_TWO * second + (1.0 - BETA_TWO) * grad * grad
    first_hat = first_new / (1.0 - BETA_ONE**STEP)
    second_hat = second_new / (1.0 - BETA_TWO**STEP)
    weight_new = weight - rate * (first_hat / (jnp.sqrt(second_hat) + ADAM_EPS) + decay * weight)
    return (first_new, second_new, weight_new)


SHARE = 2 * HALF
SPAN = 384
DECAY = 0.1
BRANCH_RATE, GATE_RATE, OUT_RATE = 3.0 * D**-0.5, 3.0 * BLOCK**-0.5, 3.0 * (L // 8) ** -0.5
FFN_RATE, DOWN_RATE = 3.0 * D**-0.5, 3.0 * (F // 2) ** -0.5


def update_jobs():
    return (
        ("down", None, 0, 0, HIDE, 0, DOWN_RATE),
        ("ffn", 1, 1, 0, HIDE, HIDE, FFN_RATE),
        ("ffn", 0, 2, 0, HIDE, 0, FFN_RATE),
        ("out", None, 3, 2 * WIDTH, WIDTH, 0, OUT_RATE),
        ("branch", 1, 3, 0, WIDTH, WIDTH, BRANCH_RATE),
        ("branch", 0, 3, WIDTH, WIDTH, 0, BRANCH_RATE),
        ("gate", 0, 4, 0, WIDTH, 0, GATE_RATE),
        ("gate", 1, 4, WIDTH, WIDTH, WIDTH, GATE_RATE),
    )


ARRAYS = ("down", "ffn", "out", "branch", "gate")


def update_kernel(*refs):
    shares, weights = refs[:5], dict(zip(ARRAYS, refs[5:10]))
    moments = {name: refs[10 + 2 * i : 12 + 2 * i] for i, name in enumerate(ARRAYS)}
    small, small_outs = refs[20:28], refs[43:49]
    outs = {name: refs[28 + 3 * i : 31 + 3 * i] for i, name in enumerate(ARRAYS)}
    windows = dict(zip(ARRAYS, refs[49:54]))
    held = refs[54:62]
    in_sem, window_sem, out_sem = refs[62:]
    me = lax.axis_index("dp")
    begin = jnp.minimum(me * SHARE // 128 * 128, D - SPAN)
    copies = {}

    def copy(key, source, target, sem):
        copies[key] = pltpu.make_async_copy(source, target, sem)
        copies[key].start()

    jobs = update_jobs()
    waiting = list(ARRAYS)
    for number, (name, part, *_) in enumerate(jobs):
        if name not in copies:
            source = weights[name]
            if name != "gate":
                source = source.at[:, pl.ds(pl.multiple_of(begin, 128), SPAN)]
            copy(name, source, windows[name], window_sem.at[ARRAYS.index(name)])
        for which in range(2):
            source = moments[name][which]
            source = source if part is None else source.at[part]
            copy((number, which), source, held[number].at[which], in_sem.at[number, which])
    value, grad, mean, square = (ref[...] for ref in small[:4])
    for ref, new in zip(small_outs[:3], adam_step(value, grad, mean, square, 1.0, 0.0)):
        ref[...] = new
    value, grad, mean, square = (ref[...] for ref in small[4:])
    row = lax.broadcasted_iota(jnp.int32, value.shape, 0)
    rates = jnp.where(row == 4, 3.0, 1.0)
    for ref, new in zip(small_outs[3:], adam_step(value, grad[:5], mean, square, rates, 0.0)):
        ref[...] = new
    for number, (name, part, share, lane, width, row, rate) in enumerate(jobs):
        if name in waiting:
            waiting.remove(name)
            copies[name].wait()
        count = 16 if name == "gate" else SHARE
        span = BLOCK if name == "gate" else SPAN
        offset = me * count if name == "gate" else me * SHARE - begin
        mine = lax.broadcasted_iota(jnp.int32, (count, span), 0) + offset
        lanes = lax.broadcasted_iota(jnp.int32, (count, span), 1)
        chosen = jnp.where(lanes == mine, 1.0, 0.0).astype(jnp.bfloat16)
        box = held[number]
        box[2] = times_transposed(chosen, windows[name][row : row + width, :])
        for which in range(2):
            copies[number, which].wait()

        def body(first, box=box, share=share, lane=lane, width=width, rate=rate):
            at = pl.ds(first, 16)
            grad = shares[share][at, lane : lane + width]
            new = adam_step(box[2, at, :], grad, box[0, at, :], box[1, at, :], rate, DECAY)
            for which in range(3):
                box[which, at, :] = new[which]

        tiles(count // 16, 16, body, 1 if count == 16 else 5)
        for which in range(3):
            target = outs[name][which]
            target = target if part is None else target.at[part]
            copy((number, which), box.at[which], target, out_sem.at[number, which])
    for number in range(len(jobs)):
        for which in range(3):
            copies[number, which].wait()


def update_weights(shares, weights, moments, small):
    f32, bf16 = jnp.float32, jnp.bfloat16
    dma = pltpu.SemaphoreType.DMA
    here = pl.BlockSpec(memory_space=pltpu.VMEM)
    there = pl.BlockSpec(memory_space=pl.ANY)
    jobs = update_jobs()
    return pl.pallas_call(
        update_kernel,
        out_shape=tuple(
            jax.ShapeDtypeStruct(value.shape, f32)
            for value in (*moments[::2], small[0], small[4])
            for _ in range(3)
        ),
        in_specs=[here] * 5 + [there] * 15 + [here] * 8,
        out_specs=tuple([there] * 15 + [here] * 6),
        scratch_shapes=[
            pltpu.VMEM((weight.shape[0], BLOCK if name == "gate" else SPAN), bf16)
            for name, weight in zip(ARRAYS, weights)
        ]
        + [pltpu.VMEM((3, 16 if job[0] == "gate" else SHARE, job[4]), f32) for job in jobs]
        + [dma((len(jobs), 2)), dma((5,)), dma((len(jobs), 3))],
        compiler_params=pltpu.CompilerParams(vmem_limit_bytes=63 * 2**20),
    )(*shares, *weights, *moments, *small)


def shards(
    tokens,
    cotangent,
    segments,
    gains,
    channel_params,
    branch_in,
    gate_blocks,
    out_proj,
    ffn_in,
    ffn_down,
    gains_first,
    gains_second,
    channel_first,
    channel_second,
    branch_first,
    branch_second,
    gate_first,
    gate_second,
    out_first,
    out_second,
    ffn_in_first,
    ffn_in_second,
    down_first,
    down_second,
):
    rows = ROWS
    data_index = lax.axis_index("dp")

    padded_ids = jnp.concatenate([jnp.full((3,), -1, jnp.int32), segments])
    local_ids = lax.dynamic_slice_in_dim(padded_ids, data_index * rows, rows + 3)
    marks = [local_ids[3 - tap : 3 - tap + rows] == local_ids[3:] for tap in range(4)]
    marks.append(local_ids[3:] != local_ids[2 : 2 + rows])
    flags = jnp.pad(jnp.stack(marks, 1).astype(jnp.float32), ((0, 8), (0, 3)))
    decay_param = channel_params[4:5]
    chan = jnp.concatenate(
        [channel_params, jax.nn.softplus(decay_param), jax.nn.sigmoid(decay_param), decay_param], 0
    )
    branch_t = branch_in.swapaxes(1, 2)
    gates_t = gate_blocks.swapaxes(1, 2)
    ffn_t = ffn_in.swapaxes(1, 2).reshape(2 * HIDE, D)
    residual_own, block, *saved = mixer_forward(
        tokens, branch_t, gates_t, out_proj, chan, gains, flags
    )
    tokens_grad, block_out, gain_grad, channel_grad, blocks_share, down_share, up_share, gate_share, mixer_share, *_ = (
        backward(
            block,
            residual_own,
            gains,
            chan,
            flags,
            cotangent,
            ffn_t,
            ffn_down,
            tokens,
            out_proj,
            branch_t,
            gates_t,
            saved,
        )
    )
    new = update_weights(
        (down_share, up_share, gate_share, mixer_share, blocks_share),
        (
            ffn_down,
            ffn_t,
            out_proj,
            branch_t.reshape(2 * WIDTH, D),
            gates_t.reshape(2 * WIDTH, BLOCK),
        ),
        (
            down_first.T,
            down_second.T,
            ffn_in_first,
            ffn_in_second,
            out_first.T,
            out_second.T,
            branch_first,
            branch_second,
            gate_first,
            gate_second,
        ),
        (
            gains,
            gain_grad,
            gains_first,
            gains_second,
            channel_params,
            channel_grad,
            channel_first,
            channel_second,
        ),
    )
    return (
        block_out,
        tokens_grad,
        *new[15:21],
        *new[9:12],
        *new[12:15],
        *(value.T for value in new[6:9]),
        *new[3:6],
        *(value.T for value in new[0:3]),
    )


def solution(mesh):
    weights = [
        P(None, None, "tensor"),
        P(None, None, "tensor"),
        P("tensor", None),
        P(None, None, "tensor"),
        P("tensor", None),
    ]
    owned = [
        P(None, "dp", "tensor"),
        P(None, "dp", "tensor"),
        P("tensor", "dp"),
        P(None, "dp", "tensor"),
        P("tensor", "dp"),
    ]
    moments = [P(), P(None, "tensor")] + owned
    placed = [P("dp", None), P("dp", None), P(), P(), P(None, "tensor")] + weights
    for spec in moments:
        placed += [spec, spec]
    outs = [P(("dp", "tensor"), None)] * 2
    for spec in moments:
        outs += [spec, spec, spec]
    return jax.shard_map(
        shards, mesh=mesh, in_specs=tuple(placed), out_specs=tuple(outs), check_vma=False
    )
```
